128 devices in a mesh: lat: 8 (over z, y_lo), lon: 16 (over x, y_hi, core).
Axes of the slice: x: 4, y: 4 (y_hi: 2, y_lo: 2; y = y_hi * 2 + y_lo), z: 4, core: 2. Of those that a mesh axis runs over, the one named last changes fastest.
Arguments:
- latent: bfloat16 [4, 96, 384, 512], P(None, 'lat', 'lon'), may hold values from -6 to 6
- gain_first: float32 [512], replicated, may hold values from 0.25 to 1.75
- triple_first: bfloat16 [512, 1536], replicated, may hold values from -3.75 to 3.75
- output_first: bfloat16 [512, 512], replicated, may hold values from -0.25 to 0.25
- gain_merge: float32 [2048], replicated, may hold values from 0.25 to 1.75
- merge_weight: bfloat16 [2048, 1024], replicated, may hold values from -0.125 to 0.125
- gain_second: float32 [1024], replicated, may hold values from 0.25 to 1.75
- triple_second: bfloat16 [1024, 3072], replicated, may hold values from -2.6516504 to 2.6516504
- output_second: bfloat16 [1024, 1024], replicated, may hold values from -0.1875 to 0.1875
- split_weight: bfloat16 [1024, 2048], replicated, may hold values from -0.1875 to 0.1875
Outputs:
- decoded: bfloat16 [4, 96, 384, 512], P(None, 'lat', 'lon')
- level_means: float32 [4, 512], replicated
The draws below stay inside these ranges and needn't reach their ends.
All inputs are finite; a program needn't handle non-finite values.
Results may differ from the reference program's by a relative error of at most 0.028.
Values may be sent and summed in bfloat16 or wider, within the bound.
A program may use at most 192 MiB of HBM per device.

```python
import jax
import jax.numpy as jnp
from jax import lax

D1 = 512
D2 = 1024
HD = 64
LEVELS = 4
WIN_LEV = 2
WIN_LAT = 6
WIN_LON = 12
LAT = 96
LON = 384


def triple_draw(key, width):
    spread = (width // 2) ** (-0.5)
    base_key = jax.random.fold_in(jax.random.fold_in(key, 31), 0)
    drawn = jnp.clip(jax.random.normal(base_key, (width, 3 * width), jnp.float32), -6.0, 6.0)
    return (drawn * spread).astype(jnp.bfloat16)


def draw_triple_first(key, part):
    return triple_draw(jax.random.fold_in(key, 3), D1)


def draw_triple_second(key, part):
    return triple_draw(jax.random.fold_in(key, 7), D2)


def steps_of(key, extent, pieces, least, largest):
    loudness = 1.0
    for dim, shards_of in pieces:
        heights = jax.random.uniform(jax.random.fold_in(jax.random.fold_in(key, 6), dim), (shards_of,), jnp.float32, least / len(pieces), largest / len(pieces))
        loudness = loudness * jnp.repeat(jnp.exp(heights), extent[dim] // shards_of).reshape((-1,) + (1,) * (len(extent) - 1 - dim))
    return loudness


def scatter_about(own_key, extent, scale, limit, pieces=(), kind=jnp.bfloat16):
    loudness = steps_of(own_key, extent, pieces, -0.22, 0.18) if pieces else 1.0
    result = jax.random.normal(own_key, extent, jnp.float32) * scale * loudness
    return jnp.minimum(jnp.maximum(result, -limit), limit).astype(kind)


def setup_inputs(seed: int = 0) -> dict:
    seeds = jax.random.split(jax.random.key(seed), 11)
    return {
        "latent": scatter_about(seeds[0], (LEVELS, LAT, LON, D1), 1.0, 6.0, ((1, 8), (2, 16))),
        "gain_first": jnp.clip(1.0 + 0.15 * jax.random.normal(seeds[1], (D1,), jnp.float32), 0.25, 1.75),
        "triple_first": draw_triple_first(jax.random.fold_in(seeds[10], 71), 0),
        "output_first": scatter_about(seeds[3], (D1, D1), D1 ** -0.5, 0.25),
        "gain_merge": jnp.clip(1.0 + 0.15 * jax.random.normal(seeds[4], (4 * D1,), jnp.float32), 0.25, 1.75),
        "merge_weight": scatter_about(seeds[5], (4 * D1, D2), (4 * D1) ** -0.5, 0.125),
        "gain_second": jnp.clip(1.0 + 0.15 * jax.random.normal(seeds[6], (D2,), jnp.float32), 0.25, 1.75),
        "triple_second": draw_triple_second(jax.random.fold_in(seeds[10], 71), 0),
        "output_second": scatter_about(seeds[8], (D2, D2), D2 ** -0.5, 0.1875),
        "split_weight": scatter_about(seeds[9], (D2, 4 * D1), D2 ** -0.5, 0.1875),
    }


epsilon = 1e-05
masked_score = -1e+30

def layer_norm(values_in, norm_gain):
    row_mean = lax.optimization_barrier(jnp.mean(values_in, -1, keepdims=True))
    centred = values_in - row_mean
    row_var = lax.optimization_barrier(jnp.mean(centred * centred, -1, keepdims=True))
    return centred * lax.rsqrt(row_var + epsilon) * norm_gain.astype(jnp.float32)

def level_windows(levels):
    half_lev = WIN_LEV // 2
    level_index = (jnp.arange(levels, dtype=jnp.int32) + half_lev) % levels
    return (level_index + half_lev) // WIN_LEV

def window_block(field_tile, level_ids, row_ids, row_valid, norm_gain, w_proj, w_out, top_row, left_col, keep_rows, keep_cols):
    levels, height, tile_cols, channels = field_tile.shape
    head_count = channels // HD
    lev_wins = levels // WIN_LEV
    win_rows = height // WIN_LAT
    win_cols = tile_cols // WIN_LON
    window_count = lev_wins * win_rows * win_cols
    normed = layer_norm(field_tile.astype(jnp.float32), norm_gain).astype(jnp.bfloat16)
    projected = jnp.dot(normed.reshape(-1, channels), w_proj, preferred_element_type=jnp.float32).astype(jnp.bfloat16)
    projected = projected.reshape(lev_wins, WIN_LEV, win_rows, WIN_LAT, win_cols, WIN_LON, 3, head_count, HD)
    projected = jnp.transpose(projected, (6, 0, 2, 4, 7, 1, 3, 5, 8))
    projected = projected.reshape(3, window_count, head_count, WIN_LEV * WIN_LAT * WIN_LON, HD)
    queries = projected[0].astype(jnp.float32)
    key_rows = projected[1].astype(jnp.float32)
    values = projected[2].astype(jnp.float32)
    scores = jnp.einsum('wgqd,wgkd->wgqk', queries, key_rows) * HD ** (-0.5)
    shape_ids = (lev_wins, win_rows, win_cols, WIN_LEV, WIN_LAT, WIN_LON)
    token_rows = jnp.broadcast_to(row_ids.reshape(1, win_rows, 1, 1, WIN_LAT, 1), shape_ids).reshape(window_count, -1)
    token_valid = jnp.broadcast_to(row_valid.reshape(1, win_rows, 1, 1, WIN_LAT, 1), shape_ids).reshape(window_count, -1)
    token_levels = jnp.broadcast_to(level_ids.reshape(lev_wins, 1, 1, WIN_LEV, 1, 1), shape_ids).reshape(window_count, -1)
    allowed = (token_rows[:, :, None] == token_rows[:, None, :]) & (token_levels[:, :, None] == token_levels[:, None, :]) & token_valid[:, None, :]
    scores = jnp.where(allowed[:, None], scores, masked_score)
    row_peak = lax.optimization_barrier(jnp.max(scores, -1, keepdims=True))
    exponent = jnp.exp(scores - row_peak)
    row_total = lax.optimization_barrier(jnp.sum(exponent, -1, keepdims=True))
    weights = (exponent / row_total).astype(jnp.bfloat16)
    attended = jnp.einsum('wgqk,wgkd->wgqd', weights.astype(jnp.float32), values).astype(jnp.bfloat16)
    attended = attended.reshape(lev_wins, win_rows, win_cols, head_count, WIN_LEV, WIN_LAT, WIN_LON, HD)
    attended = jnp.transpose(attended, (0, 4, 1, 5, 2, 6, 3, 7)).reshape(levels, height, tile_cols, channels)
    attended = attended[:, top_row:top_row + keep_rows, left_col:left_col + keep_cols]
    update = jnp.dot(attended.reshape(-1, channels), w_out, preferred_element_type=jnp.float32)
    update = update.reshape(levels, keep_rows, keep_cols, channels)
    base_rows = field_tile[:, top_row:top_row + keep_rows, left_col:left_col + keep_cols].astype(jnp.float32)
    return (base_rows + update).astype(jnp.bfloat16)

def shifted_section(field, norm_gain, w_proj, w_out):
    levels, height, tile_cols, channels = field.shape
    half_lev = WIN_LEV // 2
    half_lat = WIN_LAT // 2
    half_lon = WIN_LON // 2
    rolled = jnp.roll(field, (-half_lev, -half_lat, -half_lon), (0, 1, 2))
    band_count = height // WIN_LAT
    stacked = jnp.transpose(rolled.reshape(levels, band_count, WIN_LAT, tile_cols, channels), (1, 0, 2, 3, 4))
    band_starts = jnp.arange(band_count, dtype=jnp.int32) * WIN_LAT
    level_ids = level_windows(levels)

    def one_band(band_args):
        band_field, band_start = band_args
        row_index = (band_start + half_lat + jnp.arange(WIN_LAT, dtype=jnp.int32)) % height
        row_ids = (row_index + half_lat) // WIN_LAT
        row_valid = jnp.ones((WIN_LAT,), bool)
        return window_block(band_field, level_ids, row_ids, row_valid, norm_gain, w_proj, w_out, 0, 0, WIN_LAT, tile_cols)
    banded = lax.map(one_band, (stacked, band_starts))
    banded = jnp.transpose(banded, (1, 0, 2, 3, 4)).reshape(levels, height, tile_cols, channels)
    return jnp.roll(banded, (half_lev, half_lat, half_lon), (0, 1, 2))

def merge_patches(field, norm_gain, w_merge):
    levels, height, tile_cols, channels = field.shape
    grouped = field.reshape(levels, height // 2, 2, tile_cols // 2, 2, channels)
    grouped = jnp.transpose(grouped, (0, 1, 3, 2, 4, 5)).reshape(levels, height // 2, tile_cols // 2, 4 * channels)
    normed = layer_norm(grouped.astype(jnp.float32), norm_gain).astype(jnp.bfloat16)
    merged = jnp.dot(normed.reshape(-1, 4 * channels), w_merge, preferred_element_type=jnp.float32).astype(jnp.bfloat16)
    return merged.reshape(levels, height // 2, tile_cols // 2, -1)

def split_patches(coarse, skip_field, w_split):
    levels, half_rows, half_cols, wide = coarse.shape
    channels = skip_field.shape[-1]
    spread = jnp.dot(coarse.reshape(-1, wide), w_split, preferred_element_type=jnp.float32)
    spread = spread.reshape(levels, half_rows, half_cols, 2, 2, channels)
    spread = jnp.transpose(spread, (0, 1, 3, 2, 4, 5)).reshape(levels, 2 * half_rows, 2 * half_cols, channels)
    return (skip_field.astype(jnp.float32) + spread).astype(jnp.bfloat16)

def row_weights(row_index, total_rows):
    position = (row_index.astype(jnp.float32) + 0.5) / total_rows - 0.5
    return jnp.cos(jnp.pi * position)

def reference(latent, gain_first, triple_first, output_first, gain_merge, merge_weight, gain_second, triple_second, output_second, split_weight):
    fine_field = shifted_section(latent, gain_first, triple_first, output_first)
    coarse = merge_patches(fine_field, gain_merge, merge_weight)
    upper = shifted_section(coarse, gain_second, triple_second, output_second)
    decoded = split_patches(upper, fine_field, split_weight)
    total_rows = decoded.shape[1]
    all_weights = row_weights(jnp.arange(total_rows, dtype=jnp.int32), total_rows)
    scale_total = jnp.sqrt(decoded.shape[2] * jnp.sum(all_weights * all_weights))
    summed = lax.optimization_barrier(jnp.sum(decoded.astype(jnp.float32) * all_weights[None, :, None, None], (1, 2)))
    return (decoded, summed / scale_total)
```

```python
import functools

import jax
import jax.numpy as jnp
import ml_dtypes
import numpy as np
from jax import lax
from jax.experimental import pallas as pl
from jax.experimental.pallas import tpu as pltpu
from jax.sharding import PartitionSpec as P

HD = 64
D1 = 512
D2 = 1024
EPS = 1e-05
MASKED = -1e30
QUAD = 72
WIN = 288
GROUP = 144
MESH = pl.DeviceIdType.MESH
F32 = jnp.float32
BF16 = jnp.bfloat16


def permutation(rows, source):
    matrix = np.zeros((rows, rows), np.float32)
    matrix[np.arange(rows), source] = 1.0
    return matrix.astype(ml_dtypes.bfloat16)


@functools.lru_cache(None)
def tables(lats, lons):
    q, l, r, c = np.meshgrid(*map(np.arange, (4, 4, 3, 6)), indexing="ij")
    to_quads = permutation(WIN, (l * 72 + r * 24 + q * 6 + c).ravel())
    p, q, r, c = np.meshgrid(*map(np.arange, (4, 4, 3, 6)), indexing="ij")
    to_window = permutation(WIN, (((q * 4 + (p + 1) % 4) * 3 + r) * 6 + c).ravel())
    ro, co, l, cr, cc = np.meshgrid(*map(np.arange, (2, 2, 4, 3, 6)), indexing="ij")
    row, col = 2 * cr + ro, 2 * cc + co
    quad = (row // 3) * 2 + col // 6
    to_patches = permutation(WIN, (((quad * 4 + l) * 3 + row % 3) * 6 + col % 6).ravel())
    l, row, col = np.meshgrid(*map(np.arange, (4, 6, 24)), indexing="ij")
    j, col = col // 12, col % 12
    off = (row % 2) * 2 + col % 2
    to_rows = permutation(
        2 * WIN, ((((j * 4 + off) * 4 + l) * 3 + row // 2) * 6 + col // 2).ravel()
    )
    total_rows = 12 * lats
    position = (np.arange(total_rows, dtype=np.float32) + np.float32(0.5)) / np.float32(
        total_rows
    ) - np.float32(0.5)
    weights = np.cos(np.float32(np.pi) * position).astype(np.float32)
    scale = float(np.sqrt(24.0 * lons * np.sum(weights.astype(np.float64) ** 2)))
    high = weights.astype(ml_dtypes.bfloat16)
    low = (weights - high.astype(np.float32)).astype(ml_dtypes.bfloat16)
    parts = np.stack([high, low]).astype(np.float32)
    sums = np.zeros((lats, 3, 16, WIN), np.float32)
    quad, l, r, c = [v.ravel() for v in np.meshgrid(*map(np.arange, (4, 4, 3, 6)), indexing="ij")]
    token = np.arange(WIN)
    for lat in range(lats):
        for part in range(2):
            for a in range(2):
                row = (lat * 12 + 3 + 6 * a + 3 * (quad // 2) + r) % total_rows
                sums[lat, a, part * 4 + l, token] = parts[part, row]
            for ro in range(2):
                row = (2 * (lat * 6 + 3 + 3 * (quad // 2) + r) + ro) % total_rows
                sums[lat, 2, part * 8 + ro * 4 + l, token] = parts[part, row]
    return (
        to_quads,
        to_window,
        np.ascontiguousarray(to_window.T),
        to_patches,
        to_rows,
        sums.astype(ml_dtypes.bfloat16),
        scale,
    )


def dot(a, b):
    return jnp.dot(a, b, preferred_element_type=F32)


def dot_nt(a, b):
    return lax.dot_general(a, b, (((1,), (1,)), ((), ())), preferred_element_type=F32)


def layer_norm(x, gain):
    mean = jnp.mean(x, -1, keepdims=True)
    centred = x - mean
    var = jnp.mean(centred * centred, -1, keepdims=True)
    return centred * lax.rsqrt(var + EPS) * gain


def kernel(
    lats,
    lons,
    scale,
    latent_h,
    triple1_h,
    out1_h,
    merge_h,
    triple2_h,
    out2_h,
    split_h,
    quads_h,
    window_h,
    unwindow_h,
    patches_h,
    rows_h,
    sums_h,
    gain1,
    gainm,
    gain2,
    decoded,
    means,
    latent,
    triple1,
    out1,
    mergew,
    triple2,
    out2,
    splitw,
    quads_p,
    window_p,
    unwindow_p,
    patches_p,
    rows_p,
    sums,
    xq,
    fq,
    normed,
    qs,
    ks,
    vs,
    att,
    bias,
    grouped,
    groupn,
    coarse,
    up,
    ur,
    ub,
    fg,
    fsum,
    part1,
    part2,
    load_sem,
    send_sem,
    recv_sem,
    ar_send,
    ar_recv,
):
    lat = lax.axis_index("lat")
    lon = lax.axis_index("lon")

    def at(dlat, dlon):
        return {
            "lat": lax.rem(lat + dlat + lats, lats),
            "lon": lax.rem(lon + dlon + lons, lons),
        }

    loads = [
        pltpu.make_async_copy(s, d, load_sem.at[i])
        for i, (s, d) in enumerate(
            [
                (latent_h, latent),
                (quads_h, quads_p),
                (window_h, window_p),
                (triple1_h, triple1),
                (unwindow_h, unwindow_p),
                (out1_h, out1),
                (sums_h.at[lat], sums),
                (patches_h, patches_p),
                (merge_h, mergew),
                (triple2_h, triple2),
                (out2_h, out2),
                (split_h, splitw),
                (rows_h, rows_p),
            ]
        )
    ]
    (l_latent, l_quads, l_window, l_triple1, l_unwindow, l_out1, l_sums) = loads[:7]
    (l_patches, l_merge, l_triple2, l_out2, l_split, l_rows) = loads[7:]
    for load in loads:
        load.start()

    barrier = pltpu.get_barrier_semaphore()
    peers = [at(k, 0) for k in range(1, lats)] + [at(0, k) for k in range(1, lons)]
    peers += [at(1, 1), at(-1, -1)]
    for peer in peers:
        pl.semaphore_signal(barrier, inc=1, device_id=peer, device_id_type=MESH)

    tq = lax.broadcasted_iota(jnp.int32, (GROUP, GROUP), 0)
    tk = lax.broadcasted_iota(jnp.int32, (GROUP, GROUP), 1)
    lev_q, lev_k = tq >= 72, tk >= 72
    half_q = jnp.where(lev_q, tq - 72, tq) >= 36
    half_k = jnp.where(lev_k, tk - 72, tk) >= 36
    other_lev = jnp.where(lev_q == lev_k, 0.0, MASKED).astype(F32)
    other_row = jnp.where(half_q == half_k, 0.0, MASKED).astype(F32)
    bias[0] = jnp.zeros((GROUP, GROUP), F32)
    bias[1] = other_lev
    bias[2] = other_row
    bias[3] = jnp.minimum(other_lev, other_row)
    fsum[...] = jnp.zeros_like(fsum)

    def copy(number, src, dst, target):
        return pltpu.make_async_remote_copy(
            src_ref=src,
            dst_ref=dst,
            send_sem=send_sem.at[number],
            recv_sem=recv_sem.at[number],
            device_id=target,
            device_id_type=MESH,
        )

    x_lat = copy(0, xq.at[0, pl.ds(1, 3)], xq.at[4, pl.ds(1, 3)], at(-1, 0))
    x_lon = copy(1, xq.at[pl.ds(1, 3), 0], xq.at[pl.ds(1, 3), 4], at(0, -1))
    x_dia = copy(2, xq.at[0, 0], xq.at[4, 4], at(-1, -1))
    f_lat = copy(3, fq.at[1, pl.ds(2, 3)], fq.at[5, pl.ds(2, 3)], at(-1, 0))
    f_lon = copy(4, fq.at[pl.ds(2, 3), 1], fq.at[pl.ds(2, 3), 5], at(0, -1))
    f_dia = copy(5, fq.at[1, 1], fq.at[5, 5], at(-1, -1))
    b_lat = copy(6, fq.at[4, pl.ds(1, 3)], fq.at[0, pl.ds(1, 3)], at(1, 0))
    b_lon = copy(7, fq.at[pl.ds(1, 3), 4], fq.at[pl.ds(1, 3), 0], at(0, 1))
    b_dia = copy(8, fq.at[4, 4], fq.at[0, 0], at(1, 1))
    u_lat = copy(9, up.at[1, 0], ur.at[0, 1], at(1, 0))
    u_lon = copy(10, up.at[0, 1], ur.at[1, 0], at(0, 1))
    u_dia = copy(11, up.at[1, 1], ur.at[0, 0], at(1, 1))

    l_latent.wait()
    l_quads.wait()

    def form_quads(qr, carry):
        rows = latent[:, qr].astype(F32).reshape(WIN, D1).astype(BF16)
        xq[qr, pl.ds(0, 4)] = dot(quads_p[...], rows).reshape(4, QUAD, D1).astype(BF16)
        return carry

    lax.fori_loop(0, 4, form_quads, 0)

    pl.semaphore_wait(barrier, len(peers))
    x_lon.start()
    x_lat.start()
    x_dia.start()

    l_window.wait()
    l_triple1.wait()
    l_unwindow.wait()
    l_out1.wait()
    l_sums.wait()

    lane = lax.broadcasted_iota(jnp.int32, (1, 256), 1)
    head_masks = [((lane >= HD * h) & (lane < HD * (h + 1))).astype(BF16) for h in range(4)]
    head_ones = [jnp.broadcast_to(m, (GROUP, 256)) for m in head_masks]

    def section(x, gain, triple, out_w, width, rows_apart):
        n = layer_norm(x, gain).astype(BF16)
        normed[:, :width] = dot(window_p[...], n).astype(BF16)
        groups = width // 256

        for which, dest in enumerate((qs, ks, vs)):

            def project(i, carry, which=which, dest=dest):
                src = pl.ds(pl.multiple_of(which * width + i * 256, 256), 256)
                dst = pl.ds(pl.multiple_of(i * 256, 256), 256)
                value = dot(normed[:, :width], triple[:, src]).astype(BF16)
                if which == 0:
                    value = value * jnp.asarray(HD**-0.5, BF16)
                dest[:, dst] = value
                return carry

            lax.fori_loop(0, groups, project, 0)

        def attend(i, carry):
            g, hg = i // groups, i % groups
            rows = pl.ds(pl.multiple_of(g * GROUP, 16), GROUP)
            lanes = pl.ds(pl.multiple_of(hg * 256, 256), 256)
            q, k, v = qs[rows, lanes], ks[rows, lanes], vs[rows, lanes]
            away = bias[g + 2 * rows_apart]
            total = None
            for h in range(4):
                s = dot_nt(q, k * head_masks[h]) + away
                peak = jnp.max(s, -1, keepdims=True)
                e = jnp.exp(s - peak).astype(BF16)
                top = dot(e, v * head_masks[h])
                low = dot(e, head_ones[h])
                total = (top, low) if total is None else (total[0] + top, total[1] + low)
            att[rows, lanes] = (total[0] / total[1]).astype(BF16)
            return carry

        lax.fori_loop(0, 2 * groups, attend, 0)
        back = dot(unwindow_p[...], att[:, :width]).astype(BF16)
        return x + dot(back, out_w[...])

    def fine_window(w, carry):
        a, b = w // 2, w % 2

        @pl.when(w == 1)
        def _():
            x_lon.wait_recv()

        @pl.when(w == 2)
        def _():
            x_lat.wait_recv()

        @pl.when(w == 3)
        def _():
            x_dia.wait_recv()

        quads_r, quads_c = pl.ds(1 + 2 * a, 2), pl.ds(1 + 2 * b, 2)
        x = xq[quads_r, quads_c].astype(F32).reshape(WIN, D1)
        apart = jnp.where((a == 1) & (lat == lats - 1), 1, 0)
        fine = section(x, gain1[...], triple1, out1, D1, apart)
        fq[quads_r, quads_c] = fine.reshape(2, 2, QUAD, D1).astype(BF16)
        fsum[...] += dot(sums[a], fine.astype(BF16))

        @pl.when(w == 0)
        def _():
            f_dia.start()

        @pl.when(w == 1)
        def _():
            f_lat.start()

        @pl.when(w == 2)
        def _():
            f_lon.start()

        return carry

    lax.fori_loop(0, 4, fine_window, 0)
    b_lon.start()
    b_lat.start()
    b_dia.start()

    l_patches.wait()

    def patches(first_r, first_c):
        x = fq[pl.ds(first_r, 2), pl.ds(first_c, 2)].astype(F32).reshape(WIN, D1).astype(BF16)
        return dot(patches_p[...], x)

    f_dia.wait_recv()
    f_lat.wait_recv()
    f_lon.wait_recv()

    def gather(cq, carry):
        x = patches(2 + 2 * (cq // 2), 2 + 2 * (cq % 2))
        rows = pl.ds(pl.multiple_of(cq * QUAD, 8), QUAD)
        for off in range(4):
            grouped[rows, off * D1 : (off + 1) * D1] = x[off * QUAD : (off + 1) * QUAD]
        return carry

    lax.fori_loop(0, 4, gather, 0)

    def norm_grouped(i, carry):
        rows = pl.ds(pl.multiple_of(i * 96, 16), 96)
        groupn[rows, :] = layer_norm(grouped[rows, :], gainm[...]).astype(BF16)
        return carry

    lax.fori_loop(0, 3, norm_grouped, 0)
    l_merge.wait()

    def merge(i, carry):
        lanes = pl.ds(pl.multiple_of(i * 256, 256), 256)
        coarse[:, lanes] = dot(groupn[...], mergew[:, lanes]).astype(BF16)
        return carry

    lax.fori_loop(0, 4, merge, 0)
    l_triple2.wait()
    l_out2.wait()
    apart = jnp.where(lat == lats - 1, 1, 0)
    upper = section(coarse[...].astype(F32), gain2[...], triple2, out2, D2, apart)
    up[...] = upper.reshape(2, 2, QUAD, D2).astype(BF16)
    u_lon.start()
    u_lat.start()
    u_dia.start()
    ur[1, 1] = up[0, 0]

    usum = dot(sums[2], upper.astype(BF16))
    usum = usum[:8] + usum[8:]
    high = usum.astype(BF16).astype(F32)
    usum = jnp.concatenate([high, usum - high], 0).astype(BF16)
    l_split.wait()
    partial = fsum[0:4] + fsum[4:8]
    for ro in range(2):
        for co in range(2):
            off = 2 * ro + co
            t = dot(usum, splitw[:, off * D1 : (off + 1) * D1])
            t = t[:8] + t[8:]
            partial += t[4 * ro : 4 * ro + 4]
    part1[lat] = partial

    def ar_copy(buf, me, number, target):
        return pltpu.make_async_remote_copy(
            src_ref=buf.at[me],
            dst_ref=buf.at[me],
            send_sem=ar_send.at[number],
            recv_sem=ar_recv.at[number],
            device_id=target,
            device_id_type=MESH,
        )

    ar1 = [ar_copy(part1, lat, k, at(k, 0)) for k in range(1, lats)]
    ar2 = [ar_copy(part2, lon, lats + k, at(0, k)) for k in range(1, lons)]
    for c in ar1:
        c.start()

    b_lat.wait_recv()
    b_lon.wait_recv()
    b_dia.wait_recv()

    def skip(cq, carry):
        x = patches(2 * (cq // 2), 2 * (cq % 2))
        rows = pl.ds(pl.multiple_of(cq * QUAD, 8), QUAD)
        for off in range(4):
            fg[off, rows, :] = x[off * QUAD : (off + 1) * QUAD]
        return carry

    lax.fori_loop(0, 4, skip, 0)

    for c in ar1:
        c.wait_recv()
    total = part1[0]
    for k in range(1, lats):
        total += part1[k]
    part2[lon] = total
    for c in ar2:
        c.start()

    u_lat.wait_recv()
    u_lon.wait_recv()
    u_dia.wait_recv()
    ub[...] = ur[...].astype(F32).reshape(WIN, D2).astype(BF16)

    def spread(i, carry):
        off, half = i // 2, i % 2
        src = pl.ds(pl.multiple_of(i * 256, 256), 256)
        dst = pl.ds(pl.multiple_of(half * 256, 256), 256)
        fg[off, :, dst] += dot(ub[...], splitw[:, src])
        return carry

    lax.fori_loop(0, 8, spread, 0)
    l_rows.wait()

    def place(i, carry):
        pieces = []
        for j in range(2):
            rows = pl.ds(pl.multiple_of((2 * i + j) * QUAD, 8), QUAD)
            for off in range(4):
                pieces.append(fg[off, rows, :])
        x = jnp.concatenate(pieces, 0).astype(BF16)
        decoded[:, i] = dot(rows_p[...], x).reshape(4, 144, D1).astype(BF16)
        return carry

    lax.fori_loop(0, 2, place, 0)

    for c in ar2:
        c.wait_recv()
    total = part2[0]
    for k in range(1, lons):
        total += part2[k]
    means[...] = total * (1.0 / scale)
    for c in (x_lat, x_lon, x_dia, f_lat, f_lon, f_dia, b_lat, b_lon, b_dia, u_lat, u_lon, u_dia):
        c.wait_send()
    for c in ar1 + ar2:
        c.wait_send()


def solution(mesh):
    lats, lons = mesh.shape["lat"], mesh.shape["lon"]
    *consts, scale = tables(lats, lons)

    def shards(
        latent,
        gain_first,
        triple_first,
        output_first,
        gain_merge,
        merge_weight,
        gain_second,
        triple_second,
        output_second,
        split_weight,
    ):
        hbm = pl.BlockSpec(memory_space=pl.ANY)
        vmem = pl.BlockSpec(memory_space=pltpu.VMEM)
        bf = lambda *shape: pltpu.VMEM(shape, BF16)
        f4 = lambda *shape: pltpu.VMEM(shape, F32)
        decoded, means = pl.pallas_call(
            functools.partial(kernel, lats, lons, scale),
            name="windows",
            out_shape=(
                jax.ShapeDtypeStruct((4, 2, 144, D1), BF16),
                jax.ShapeDtypeStruct((4, D1), F32),
            ),
            in_specs=[hbm] * 13 + [vmem] * 3,
            out_specs=(vmem, vmem),
            scratch_shapes=[
                bf(4, 4, QUAD, D1),
                bf(D1, 3 * D1),
                bf(D1, D1),
                bf(4 * D1, D2),
                bf(D2, 3 * D2),
                bf(D2, D2),
                bf(D2, 4 * D1),
                bf(WIN, WIN),
                bf(WIN, WIN),
                bf(WIN, WIN),
                bf(WIN, WIN),
                bf(2 * WIN, 2 * WIN),
                bf(3, 16, WIN),
                bf(5, 5, QUAD, D1),
                bf(6, 6, QUAD, D1),
                bf(WIN, D2),
                bf(WIN, D2),
                bf(WIN, D2),
                bf(WIN, D2),
                bf(WIN, D2),
                f4(4, GROUP, GROUP),
                f4(WIN, 4 * D1),
                bf(WIN, 4 * D1),
                bf(WIN, D2),
                bf(2, 2, QUAD, D2),
                bf(2, 2, QUAD, D2),
                bf(WIN, D2),
                f4(4, WIN, D1),
                f4(16, D1),
                f4(lats, 4, D1),
                f4(lons, 4, D1),
                pltpu.SemaphoreType.DMA((13,)),
                pltpu.SemaphoreType.DMA((12,)),
                pltpu.SemaphoreType.DMA((12,)),
                pltpu.SemaphoreType.DMA((lats + lons,)),
                pltpu.SemaphoreType.DMA((lats + lons,)),
            ],
            compiler_params=pltpu.CompilerParams(
                collective_id=0, has_side_effects=True, vmem_limit_bytes=60 * 1024 * 1024
            ),
        )(
            latent.reshape(4, 4, QUAD, D1),
            triple_first,
            output_first,
            merge_weight,
            triple_second,
            output_second,
            split_weight,
            *[jnp.asarray(c) for c in consts],
            gain_first.reshape(1, -1),
            gain_merge.reshape(1, -1),
            gain_second.reshape(1, -1),
        )
        return decoded.reshape(4, 12, 24, D1), means

    in_specs = (P(None, "lat", "lon", None),) + (P(),) * 9
    out_specs = (P(None, "lat", "lon", None), P())
    return jax.shard_map(
        shards, mesh=mesh, in_specs=in_specs, out_specs=out_specs, check_vma=False
    )
```

```python
import functools

import jax
import jax.numpy as jnp
import ml_dtypes
import numpy as np
from jax import lax
from jax.experimental import pallas as pl
from jax.experimental.pallas import tpu as pltpu
from jax.sharding import PartitionSpec as P

HD = 64
D1 = 512
D2 = 1024
EPS = 1e-05
MASKED = -1e30
QUAD = 72
WIN = 288
GROUP = 144
MESH = pl.DeviceIdType.MESH
F32 = jnp.float32
BF16 = jnp.bfloat16


def permutation(rows, source):
    matrix = np.zeros((rows, rows), np.float32)
    matrix[np.arange(rows), source] = 1.0
    return matrix.astype(ml_dtypes.bfloat16)


@functools.lru_cache(None)
def tables(lats, lons):
    q, l, r, c = np.meshgrid(*map(np.arange, (4, 4, 3, 6)), indexing="ij")
    to_quads = permutation(WIN, (l * 72 + r * 24 + q * 6 + c).ravel())
    p, q, r, c = np.meshgrid(*map(np.arange, (4, 4, 3, 6)), indexing="ij")
    to_window = permutation(WIN, (((q * 4 + (p + 1) % 4) * 3 + r) * 6 + c).ravel())
    ro, co, l, cr, cc = np.meshgrid(*map(np.arange, (2, 2, 4, 3, 6)), indexing="ij")
    row, col = 2 * cr + ro, 2 * cc + co
    quad = (row // 3) * 2 + col // 6
    to_patches = permutation(WIN, (((quad * 4 + l) * 3 + row % 3) * 6 + col % 6).ravel())
    l, row, col = np.meshgrid(*map(np.arange, (4, 6, 24)), indexing="ij")
    j, col = col // 12, col % 12
    off = (row % 2) * 2 + col % 2
    to_rows = permutation(
        2 * WIN, ((((j * 4 + off) * 4 + l) * 3 + row // 2) * 6 + col // 2).ravel()
    )
    total_rows = 12 * lats
    position = (np.arange(total_rows, dtype=np.float32) + np.float32(0.5)) / np.float32(
        total_rows
    ) - np.float32(0.5)
    weights = np.cos(np.float32(np.pi) * position).astype(np.float32)
    scale = float(np.sqrt(24.0 * lons * np.sum(weights.astype(np.float64) ** 2)))
    high = weights.astype(ml_dtypes.bfloat16)
    low = (weights - high.astype(np.float32)).astype(ml_dtypes.bfloat16)
    parts = np.stack([high, low]).astype(np.float32)
    sums = np.zeros((lats, 3, 16, WIN), np.float32)
    quad, l, r, c = [v.ravel() for v in np.meshgrid(*map(np.arange, (4, 4, 3, 6)), indexing="ij")]
    token = np.arange(WIN)
    for lat in range(lats):
        for part in range(2):
            for a in range(2):
                row = (lat * 12 + 3 + 6 * a + 3 * (quad // 2) + r) % total_rows
                sums[lat, a, part * 4 + l, token] = parts[part, row]
            for ro in range(2):
                row = (2 * (lat * 6 + 3 + 3 * (quad // 2) + r) + ro) % total_rows
                sums[lat, 2, part * 8 + ro * 4 + l, token] = parts[part, row]
    return (
        to_quads,
        to_window,
        np.ascontiguousarray(to_window.T),
        to_patches,
        to_rows,
        sums.astype(ml_dtypes.bfloat16),
        scale,
    )


def dot(a, b):
    return jnp.dot(a, b, preferred_element_type=F32)


def dot_nt(a, b):
    return lax.dot_general(a, b, (((1,), (1,)), ((), ())), preferred_element_type=F32)


def layer_norm(x, gain):
    mean = jnp.mean(x, -1, keepdims=True)
    centred = x - mean
    var = jnp.mean(centred * centred, -1, keepdims=True)
    return centred * lax.rsqrt(var + EPS) * gain


def kernel(
    lats,
    lons,
    scale,
    latent_h,
    triple1_h,
    out1_h,
    merge_h,
    triple2_h,
    out2_h,
    split_h,
    quads_h,
    window_h,
    unwindow_h,
    patches_h,
    rows_h,
    sums_h,
    gain1,
    gainm,
    gain2,
    decoded,
    means,
    latent,
    triple1,
    out1,
    mergew,
    triple2,
    out2,
    splitw,
    quads_p,
    window_p,
    unwindow_p,
    patches_p,
    rows_p,
    sums,
    xq,
    fq,
    normed,
    qs,
    ks,
    vs,
    att,
    bias,
    grouped,
    groupn,
    coarse,
    up,
    ur,
    ub,
    fg,
    fsum,
    part1,
    part2,
    load_sem,
    send_sem,
    recv_sem,
    ar_send,
    ar_recv,
):
    lat = lax.axis_index("lat")
    lon = lax.axis_index("lon")

    def at(dlat, dlon):
        return {
            "lat": lax.rem(lat + dlat + lats, lats),
            "lon": lax.rem(lon + dlon + lons, lons),
        }

    loads = [
        pltpu.make_async_copy(s, d, load_sem.at[i])
        for i, (s, d) in enumerate(
            [
                (latent_h, latent),
                (quads_h, quads_p),
                (window_h, window_p),
                (triple1_h, triple1),
                (unwindow_h, unwindow_p),
                (out1_h, out1),
                (sums_h.at[lat], sums),
                (patches_h, patches_p),
                (merge_h, mergew),
                (triple2_h, triple2),
                (out2_h, out2),
                (split_h, splitw),
                (rows_h, rows_p),
            ]
        )
    ]
    (l_latent, l_quads, l_window, l_triple1, l_unwindow, l_out1, l_sums) = loads[:7]
    (l_patches, l_merge, l_triple2, l_out2, l_split, l_rows) = loads[7:]
    for load in loads:
        load.start()

    barrier = pltpu.get_barrier_semaphore()
    peers = [at(k, 0) for k in range(1, lats)] + [at(0, k) for k in range(1, lons)]
    peers += [at(1, 1), at(-1, -1)]
    for peer in peers:
        pl.semaphore_signal(barrier, inc=1, device_id=peer, device_id_type=MESH)

    tq = lax.broadcasted_iota(jnp.int32, (GROUP, GROUP), 0)
    tk = lax.broadcasted_iota(jnp.int32, (GROUP, GROUP), 1)
    lev_q, lev_k = tq >= 72, tk >= 72
    half_q = jnp.where(lev_q, tq - 72, tq) >= 36
    half_k = jnp.where(lev_k, tk - 72, tk) >= 36
    other_lev = jnp.where(lev_q == lev_k, 0.0, MASKED).astype(F32)
    other_row = jnp.where(half_q == half_k, 0.0, MASKED).astype(F32)
    bias[0] = jnp.zeros((GROUP, GROUP), F32)
    bias[1] = other_lev
    bias[2] = other_row
    bias[3] = jnp.minimum(other_lev, other_row)
    fsum[...] = jnp.zeros_like(fsum)

    def copy(number, src, dst, target):
        return pltpu.make_async_remote_copy(
            src_ref=src,
            dst_ref=dst,
            send_sem=send_sem.at[number],
            recv_sem=recv_sem.at[number],
            device_id=target,
            device_id_type=MESH,
        )

    x_lat = copy(0, xq.at[0, pl.ds(1, 3)], xq.at[4, pl.ds(1, 3)], at(-1, 0))
    x_lon = copy(1, xq.at[pl.ds(1, 3), 0], xq.at[pl.ds(1, 3), 4], at(0, -1))
    x_dia = copy(2, xq.at[0, 0], xq.at[4, 4], at(-1, -1))
    f_lat = copy(3, fq.at[1, pl.ds(2, 3)], fq.at[5, pl.ds(2, 3)], at(-1, 0))
    f_lon = copy(4, fq.at[pl.ds(2, 3), 1], fq.at[pl.ds(2, 3), 5], at(0, -1))
    f_dia = copy(5, fq.at[1, 1], fq.at[5, 5], at(-1, -1))
    b_lat = copy(6, fq.at[4, pl.ds(1, 3)], fq.at[0, pl.ds(1, 3)], at(1, 0))
    b_lon = copy(7, fq.at[pl.ds(1, 3), 4], fq.at[pl.ds(1, 3), 0], at(0, 1))
    b_dia = copy(8, fq.at[4, 4], fq.at[0, 0], at(1, 1))
    u_lat = copy(9, up.at[1, 0], ur.at[0, 1], at(1, 0))
    u_lon = copy(10, up.at[0, 1], ur.at[1, 0], at(0, 1))
    u_dia = copy(11, up.at[1, 1], ur.at[0, 0], at(1, 1))

    l_latent.wait()
    l_quads.wait()

    def form_quads(qr, carry):
        rows = latent[:, qr].astype(F32).reshape(WIN, D1).astype(BF16)
        xq[qr, pl.ds(0, 4)] = dot(quads_p[...], rows).reshape(4, QUAD, D1).astype(BF16)
        return carry

    lax.fori_loop(0, 4, form_quads, 0, unroll=True)

    pl.semaphore_wait(barrier, len(peers))
    x_lon.start()
    x_lat.start()
    x_dia.start()

    l_window.wait()
    l_triple1.wait()
    l_unwindow.wait()
    l_out1.wait()
    l_sums.wait()

    lane = lax.broadcasted_iota(jnp.int32, (1, 256), 1)
    head_masks = [((lane >= HD * h) & (lane < HD * (h + 1))).astype(BF16) for h in range(4)]

    def section(x, gain, triple, out_w, width, rows_apart):
        n = layer_norm(x, gain).astype(BF16)
        normed[:, :width] = dot(window_p[...], n).astype(BF16)
        groups = width // 256

        for which, dest in enumerate((qs, ks, vs)):

            def project(i, carry, which=which, dest=dest):
                src = pl.ds(pl.multiple_of(which * width + i * 256, 256), 256)
                dst = pl.ds(pl.multiple_of(i * 256, 256), 256)
                value = dot(normed[:, :width], triple[:, src]).astype(BF16)
                if which == 0:
                    value = value * jnp.asarray(HD**-0.5, BF16)
                dest[:, dst] = value
                return carry

            lax.fori_loop(0, groups, project, 0, unroll=True)

        def attend(i, carry):
            g, hg = i // groups, i % groups
            rows = pl.ds(pl.multiple_of(g * GROUP, 16), GROUP)
            lanes = pl.ds(pl.multiple_of(hg * 256, 256), 256)
            q, k, v = qs[rows, lanes], ks[rows, lanes], vs[rows, lanes]
            away = bias[g + 2 * rows_apart]
            scores = dot_nt(jnp.concatenate([q * mask for mask in head_masks], 0), k)
            weights = []
            for h in range(4):
                s = scores[h * GROUP : (h + 1) * GROUP] + away
                peak = jnp.max(s, -1, keepdims=True)
                weights.append(jnp.exp(s - peak).astype(BF16))
            weights = jnp.concatenate(weights, 0)
            values = dot(weights, v) / jnp.sum(weights.astype(F32), -1, keepdims=True)
            result = values[:GROUP]
            for h in range(1, 4):
                own = values[h * GROUP : (h + 1) * GROUP]
                result = jnp.where(lane >= HD * h, own, result)
            att[rows, lanes] = result.astype(BF16)
            return carry

        lax.fori_loop(0, 2 * groups, attend, 0, unroll=4)
        back = dot(unwindow_p[...], att[:, :width]).astype(BF16)
        return x + dot(back, out_w[...])

    def fine_window(w, carry):
        a, b = w // 2, w % 2

        @pl.when(w == 1)
        def _():
            x_lon.wait_recv()

        @pl.when(w == 2)
        def _():
            x_lat.wait_recv()

        @pl.when(w == 3)
        def _():
            x_dia.wait_recv()

        quads_r, quads_c = pl.ds(1 + 2 * a, 2), pl.ds(1 + 2 * b, 2)
        x = xq[quads_r, quads_c].astype(F32).reshape(WIN, D1)
        apart = jnp.where((a == 1) & (lat == lats - 1), 1, 0)
        fine = section(x, gain1[...], triple1, out1, D1, apart)
        fq[quads_r, quads_c] = fine.reshape(2, 2, QUAD, D1).astype(BF16)
        fsum[...] += dot(sums[a], fine.astype(BF16))

        @pl.when(w == 0)
        def _():
            f_dia.start()

        @pl.when(w == 1)
        def _():
            f_lat.start()

        @pl.when(w == 2)
        def _():
            f_lon.start()

        return carry

    lax.fori_loop(0, 4, fine_window, 0)
    b_lon.start()
    b_lat.start()
    b_dia.start()

    l_patches.wait()

    def patches(first_r, first_c):
        x = fq[pl.ds(first_r, 2), pl.ds(first_c, 2)].astype(F32).reshape(WIN, D1).astype(BF16)
        return dot(patches_p[...], x)

    f_dia.wait_recv()
    f_lat.wait_recv()
    f_lon.wait_recv()

    def gather(cq, carry):
        x = patches(2 + 2 * (cq // 2), 2 + 2 * (cq % 2))
        rows = pl.ds(pl.multiple_of(cq * QUAD, 8), QUAD)
        for off in range(4):
            grouped[rows, off * D1 : (off + 1) * D1] = x[off * QUAD : (off + 1) * QUAD]
        return carry

    lax.fori_loop(0, 4, gather, 0, unroll=True)

    def norm_grouped(i, carry):
        rows = pl.ds(pl.multiple_of(i * 96, 16), 96)
        groupn[rows, :] = layer_norm(grouped[rows, :], gainm[...]).astype(BF16)
        return carry

    lax.fori_loop(0, 3, norm_grouped, 0, unroll=True)
    l_merge.wait()

    def merge(i, carry):
        lanes = pl.ds(pl.multiple_of(i * 256, 256), 256)
        coarse[:, lanes] = dot(groupn[...], mergew[:, lanes]).astype(BF16)
        return carry

    lax.fori_loop(0, 4, merge, 0, unroll=True)
    l_triple2.wait()
    l_out2.wait()
    apart = jnp.where(lat == lats - 1, 1, 0)
    upper = section(coarse[...].astype(F32), gain2[...], triple2, out2, D2, apart)
    up[...] = upper.reshape(2, 2, QUAD, D2).astype(BF16)
    u_lon.start()
    u_lat.start()
    u_dia.start()
    ur[1, 1] = up[0, 0]

    usum = dot(sums[2], upper.astype(BF16))
    usum = usum[:8] + usum[8:]
    high = usum.astype(BF16).astype(F32)
    usum = jnp.concatenate([high, usum - high], 0).astype(BF16)
    l_split.wait()
    partial = fsum[0:4] + fsum[4:8]
    for ro in range(2):
        for co in range(2):
            off = 2 * ro + co
            t = dot(usum, splitw[:, off * D1 : (off + 1) * D1])
            t = t[:8] + t[8:]
            partial += t[4 * ro : 4 * ro + 4]
    part1[lat] = partial

    def ar_copy(buf, me, number, target):
        return pltpu.make_async_remote_copy(
            src_ref=buf.at[me],
            dst_ref=buf.at[me],
            send_sem=ar_send.at[number],
            recv_sem=ar_recv.at[number],
            device_id=target,
            device_id_type=MESH,
        )

    ar1 = [ar_copy(part1, lat, k, at(k, 0)) for k in range(1, lats)]
    ar2 = [ar_copy(part2, lon, lats + k, at(0, k)) for k in range(1, lons)]
    for c in ar1:
        c.start()

    b_lat.wait_recv()
    b_lon.wait_recv()
    b_dia.wait_recv()

    def skip(cq, carry):
        x = patches(2 * (cq // 2), 2 * (cq % 2))
        rows = pl.ds(pl.multiple_of(cq * QUAD, 8), QUAD)
        for off in range(4):
            fg[off, rows, :] = x[off * QUAD : (off + 1) * QUAD]
        return carry

    lax.fori_loop(0, 4, skip, 0, unroll=True)

    for c in ar1:
        c.wait_recv()
    total = part1[0]
    for k in range(1, lats):
        total += part1[k]
    part2[lon] = total
    for c in ar2:
        c.start()

    u_lat.wait_recv()
    u_lon.wait_recv()
    u_dia.wait_recv()
    ub[...] = ur[...].astype(F32).reshape(WIN, D2).astype(BF16)

    def spread(i, carry):
        off, half = i // 2, i % 2
        src = pl.ds(pl.multiple_of(i * 256, 256), 256)
        dst = pl.ds(pl.multiple_of(half * 256, 256), 256)
        fg[off, :, dst] += dot(ub[...], splitw[:, src])
        return carry

    lax.fori_loop(0, 8, spread, 0, unroll=True)
    l_rows.wait()

    def place(i, carry):
        pieces = []
        for j in range(2):
            rows = pl.ds(pl.multiple_of((2 * i + j) * QUAD, 8), QUAD)
            for off in range(4):
                pieces.append(fg[off, rows, :])
        x = jnp.concatenate(pieces, 0).astype(BF16)
        decoded[:, i] = dot(rows_p[...], x).reshape(4, 144, D1).astype(BF16)
        return carry

    lax.fori_loop(0, 2, place, 0, unroll=True)

    for c in ar2:
        c.wait_recv()
    total = part2[0]
    for k in range(1, lons):
        total += part2[k]
    means[...] = total * (1.0 / scale)
    for c in (x_lat, x_lon, x_dia, f_lat, f_lon, f_dia, b_lat, b_lon, b_dia, u_lat, u_lon, u_dia):
        c.wait_send()
    for c in ar1 + ar2:
        c.wait_send()


def solution(mesh):
    lats, lons = mesh.shape["lat"], mesh.shape["lon"]
    *consts, scale = tables(lats, lons)

    def shards(
        latent,
        gain_first,
        triple_first,
        output_first,
        gain_merge,
        merge_weight,
        gain_second,
        triple_second,
        output_second,
        split_weight,
    ):
        hbm = pl.BlockSpec(memory_space=pl.ANY)
        vmem = pl.BlockSpec(memory_space=pltpu.VMEM)
        bf = lambda *shape: pltpu.VMEM(shape, BF16)
        f4 = lambda *shape: pltpu.VMEM(shape, F32)
        decoded, means = pl.pallas_call(
            functools.partial(kernel, lats, lons, scale),
            name="windows",
            out_shape=(
                jax.ShapeDtypeStruct((4, 2, 144, D1), BF16),
                jax.ShapeDtypeStruct((4, D1), F32),
            ),
            in_specs=[hbm] * 13 + [vmem] * 3,
            out_specs=(vmem, vmem),
            scratch_shapes=[
                bf(4, 4, QUAD, D1),
                bf(D1, 3 * D1),
                bf(D1, D1),
                bf(4 * D1, D2),
                bf(D2, 3 * D2),
                bf(D2, D2),
                bf(D2, 4 * D1),
                bf(WIN, WIN),
                bf(WIN, WIN),
                bf(WIN, WIN),
                bf(WIN, WIN),
                bf(2 * WIN, 2 * WIN),
                bf(3, 16, WIN),
                bf(5, 5, QUAD, D1),
                bf(6, 6, QUAD, D1),
                bf(WIN, D2),
                bf(WIN, D2),
                bf(WIN, D2),
                bf(WIN, D2),
                bf(WIN, D2),
                f4(4, GROUP, GROUP),
                f4(WIN, 4 * D1),
                bf(WIN, 4 * D1),
                bf(WIN, D2),
                bf(2, 2, QUAD, D2),
                bf(2, 2, QUAD, D2),
                bf(WIN, D2),
                f4(4, WIN, D1),
                f4(16, D1),
                f4(lats, 4, D1),
                f4(lons, 4, D1),
                pltpu.SemaphoreType.DMA((13,)),
                pltpu.SemaphoreType.DMA((12,)),
                pltpu.SemaphoreType.DMA((12,)),
                pltpu.SemaphoreType.DMA((lats + lons,)),
                pltpu.SemaphoreType.DMA((lats + lons,)),
            ],
            compiler_params=pltpu.CompilerParams(
                collective_id=0, has_side_effects=True, vmem_limit_bytes=60 * 1024 * 1024
            ),
        )(
            latent.reshape(4, 4, QUAD, D1),
            triple_first,
            output_first,
            merge_weight,
            triple_second,
            output_second,
            split_weight,
            *[jnp.asarray(c) for c in consts],
            gain_first.reshape(1, -1),
            gain_merge.reshape(1, -1),
            gain_second.reshape(1, -1),
        )
        return decoded.reshape(4, 12, 24, D1), means

    in_specs = (P(None, "lat", "lon", None),) + (P(),) * 9
    out_specs = (P(None, "lat", "lon", None), P())
    return jax.shard_map(
        shards, mesh=mesh, in_specs=in_specs, out_specs=out_specs, check_vma=False
    )
```

```python
import functools

import jax
import jax.numpy as jnp
import ml_dtypes
import numpy as np
from jax import lax
from jax.experimental import pallas as pl
from jax.experimental.pallas import tpu as pltpu
from jax.sharding import PartitionSpec as P

HD = 64
D1 = 512
D2 = 1024
EPS = 1e-05
MASKED = -1e30
QUAD = 40
QUADS = 160
GROUP = 144
LEVELS = np.array([[1, 2], [3, 0]])
MESH = pl.DeviceIdType.MESH
F32 = jnp.float32
BF16 = jnp.bfloat16


def permutation(rows, columns, place, source):
    matrix = np.zeros((rows, columns), np.float32)
    matrix[place.ravel(), source.ravel()] = 1.0
    return matrix.astype(ml_dtypes.bfloat16)


def grid(*extents):
    return np.meshgrid(*map(np.arange, extents), indexing="ij")


@functools.lru_cache(None)
def tables(lats, lons):
    q, l, r, c = grid(4, 2, 3, 6)
    quads = q * QUAD + l * 18 + r * 6 + c
    to_quads = permutation(QUADS, GROUP, quads, l * 72 + r * 24 + q * 6 + c)
    to_window = permutation(GROUP, QUADS, l * 72 + q * 18 + r * 6 + c, quads)
    ro, co, l, cr, cc = grid(2, 2, 2, 3, 6)
    row, col = 2 * cr + ro, 2 * cc + co
    quad = (row // 3) * 2 + col // 6
    to_patches = permutation(
        QUADS,
        QUADS,
        (2 * ro + co) * QUAD + l * 18 + cr * 6 + cc,
        quad * QUAD + l * 18 + (row % 3) * 6 + col % 6,
    )
    l, row, col = grid(2, 6, 24)
    j, c12 = col // 12, col % 12
    off = (row % 2) * 2 + c12 % 2
    to_rows = permutation(
        2 * GROUP,
        2 * QUADS,
        l * 144 + row * 24 + col,
        (j * 4 + off) * QUAD + l * 18 + (row // 2) * 6 + c12 // 2,
    )
    total_rows = 12 * lats
    position = (np.arange(total_rows, dtype=np.float32) + np.float32(0.5)) / np.float32(
        total_rows
    ) - np.float32(0.5)
    weights = np.cos(np.float32(np.pi) * position).astype(np.float32)
    scale = float(np.sqrt(24.0 * lons * np.sum(weights.astype(np.float64) ** 2)))
    high = weights.astype(ml_dtypes.bfloat16)
    low = (weights - high.astype(np.float32)).astype(ml_dtypes.bfloat16)
    parts = np.stack([high, low]).astype(np.float32)
    sums = np.zeros((lats, 2, 3, 16, GROUP), np.float32)
    l, quad, r, c = [v.ravel() for v in grid(2, 4, 3, 6)]
    token = np.arange(GROUP)
    for lat in range(lats):
        for half in range(2):
            level = LEVELS[half][l]
            for part in range(2):
                for a in range(2):
                    row = (lat * 12 + 3 + 6 * a + 3 * (quad // 2) + r) % total_rows
                    sums[lat, half, a, part * 4 + level, token] = parts[part, row]
                for ro in range(2):
                    row = (2 * (lat * 6 + 3 + 3 * (quad // 2) + r) + ro) % total_rows
                    sums[lat, half, 2, part * 8 + ro * 4 + level, token] = parts[part, row]
    return (
        to_quads,
        to_window,
        np.ascontiguousarray(to_window.T),
        to_patches,
        to_rows,
        sums.astype(ml_dtypes.bfloat16),
        scale,
    )


def dot(a, b):
    return jnp.dot(a, b, preferred_element_type=F32)


def dot_nt(a, b):
    return lax.dot_general(a, b, (((1,), (1,)), ((), ())), preferred_element_type=F32)


def layer_norm(x, gain):
    mean = jnp.mean(x, -1, keepdims=True)
    centred = x - mean
    var = jnp.mean(centred * centred, -1, keepdims=True)
    return centred * lax.rsqrt(var + EPS) * gain


def kernel(
    lats,
    lons,
    scale,
    latent_h,
    triple1_h,
    out1_h,
    merge_h,
    triple2_h,
    out2_h,
    split_h,
    quads_h,
    window_h,
    unwindow_h,
    patches_h,
    rows_h,
    sums_h,
    gain1,
    gainm,
    gain2,
    decoded,
    means,
    latent,
    triple1,
    out1,
    mergew,
    triple2,
    out2,
    splitw,
    quads_p,
    window_p,
    unwindow_p,
    patches_p,
    rows_p,
    sums,
    xq,
    fq,
    normed,
    qs,
    ks,
    vs,
    att,
    bias,
    grouped,
    groupn,
    coarse,
    up,
    ur,
    ub,
    fg,
    fsum,
    usums,
    part1,
    part2,
    load_sem,
    send_sem,
    recv_sem,
    ar_send,
    ar_recv,
):
    lat = lax.axis_index("lat")
    lon = lax.axis_index("lon")

    def at(dlat, dlon):
        return {
            "lat": lax.rem(lat + dlat + lats, lats),
            "lon": lax.rem(lon + dlon + lons, lons),
        }

    loads = [
        pltpu.make_async_copy(s, d, load_sem.at[i])
        for i, (s, d) in enumerate(
            [
                (latent_h, latent),
                (quads_h, quads_p),
                (window_h, window_p),
                (triple1_h, triple1),
                (unwindow_h, unwindow_p),
                (out1_h, out1),
                (sums_h.at[lat], sums),
                (patches_h, patches_p),
                (merge_h, mergew),
                (triple2_h, triple2),
                (out2_h, out2),
                (split_h, splitw),
                (rows_h, rows_p),
            ]
        )
    ]
    (l_latent, l_quads, l_window, l_triple1, l_unwindow, l_out1, l_sums) = loads[:7]
    (l_patches, l_merge, l_triple2, l_out2, l_split, l_rows) = loads[7:]
    for load in loads:
        load.start()

    barrier = pltpu.get_barrier_semaphore()
    peers = [at(k, 0) for k in range(1, lats)] + [at(0, k) for k in range(1, lons)]
    peers += [at(1, 1), at(-1, -1)]
    for peer in peers:
        pl.semaphore_signal(barrier, inc=1, device_id=peer, device_id_type=MESH)

    tq = lax.broadcasted_iota(jnp.int32, (GROUP, GROUP), 0)
    tk = lax.broadcasted_iota(jnp.int32, (GROUP, GROUP), 1)
    lev_q, lev_k = tq >= 72, tk >= 72
    half_q = jnp.where(lev_q, tq - 72, tq) >= 36
    half_k = jnp.where(lev_k, tk - 72, tk) >= 36
    other_lev = jnp.where(lev_q == lev_k, 0.0, MASKED).astype(F32)
    other_row = jnp.where(half_q == half_k, 0.0, MASKED).astype(F32)
    bias[0] = jnp.zeros((GROUP, GROUP), F32)
    bias[1] = other_lev
    bias[2] = other_row
    bias[3] = jnp.minimum(other_lev, other_row)
    fsum[...] = jnp.zeros_like(fsum)
    usums[...] = jnp.zeros_like(usums)

    def copy(number, half, src, dst, target):
        number = number + 12 * half
        return pltpu.make_async_remote_copy(
            src_ref=src,
            dst_ref=dst,
            send_sem=send_sem.at[number],
            recv_sem=recv_sem.at[number],
            device_id=target,
            device_id_type=MESH,
        )

    three, edge = pl.ds(1, 3), pl.ds(2, 3)

    def x_lat(h):
        return copy(0, h, xq.at[h, 0, three], xq.at[h, 4, three], at(-1, 0))

    def x_lon(h):
        return copy(1, h, xq.at[h, three, 0], xq.at[h, three, 4], at(0, -1))

    def x_dia(h):
        return copy(2, h, xq.at[h, 0, 0], xq.at[h, 4, 4], at(-1, -1))

    def f_lat(h):
        return copy(3, h, fq.at[h, 1, edge], fq.at[h, 5, edge], at(-1, 0))

    def f_lon(h):
        return copy(4, h, fq.at[h, edge, 1], fq.at[h, edge, 5], at(0, -1))

    def f_dia(h):
        return copy(5, h, fq.at[h, 1, 1], fq.at[h, 5, 5], at(-1, -1))

    def b_lat(h):
        return copy(6, h, fq.at[h, 4, three], fq.at[h, 0, three], at(1, 0))

    def b_lon(h):
        return copy(7, h, fq.at[h, three, 4], fq.at[h, three, 0], at(0, 1))

    def b_dia(h):
        return copy(8, h, fq.at[h, 4, 4], fq.at[h, 0, 0], at(1, 1))

    def u_lat(h):
        return copy(9, h, up.at[h, 1, 0], ur.at[h, 0, 1], at(1, 0))

    def u_lon(h):
        return copy(10, h, up.at[h, 0, 1], ur.at[h, 1, 0], at(0, 1))

    def u_dia(h):
        return copy(11, h, up.at[h, 1, 1], ur.at[h, 0, 0], at(1, 1))

    l_latent.wait()
    l_quads.wait()

    def form_quads(h):
        def form(qr, carry):
            rows = jnp.concatenate([latent[int(l), qr].astype(F32) for l in LEVELS[h]], 0)
            quads = dot(quads_p[...], rows.astype(BF16))
            xq[h, qr, pl.ds(0, 4)] = quads.reshape(4, QUAD, D1).astype(BF16)
            return carry

        lax.fori_loop(0, 4, form, 0, unroll=True)

    form_quads(0)
    pl.semaphore_wait(barrier, len(peers))
    x_lon(0).start()
    x_lat(0).start()
    x_dia(0).start()
    form_quads(1)
    x_lon(1).start()
    x_lat(1).start()
    x_dia(1).start()

    l_window.wait()
    l_triple1.wait()
    l_unwindow.wait()
    l_out1.wait()
    l_sums.wait()

    lane = lax.broadcasted_iota(jnp.int32, (1, 256), 1)
    head_masks = [((lane >= HD * h) & (lane < HD * (h + 1))).astype(BF16) for h in range(4)]

    def section(x, gain, triple, out_w, width, kinds):
        count = len(kinds)
        size = count * GROUP
        normed[:size, :width] = layer_norm(x, gain).astype(BF16)
        groups = width // 256

        for which, dest in enumerate((qs, ks, vs)):

            def project(i, carry, which=which, dest=dest):
                src = pl.ds(pl.multiple_of(which * width + i * 256, 256), 256)
                dst = pl.ds(pl.multiple_of(i * 256, 256), 256)
                value = dot(normed[:size, :width], triple[:, src]).astype(BF16)
                if which == 0:
                    value = value * jnp.asarray(HD**-0.5, BF16)
                dest[:size, dst] = value
                return carry

            lax.fori_loop(0, groups, project, 0, unroll=True)

        for slot in range(count):
            for hg in range(groups):
                rows = slice(slot * GROUP, (slot + 1) * GROUP)
                lanes = slice(hg * 256, (hg + 1) * 256)
                q, k, v = qs[rows, lanes], ks[rows, lanes], vs[rows, lanes]
                away = bias[kinds[slot]]
                scores = dot_nt(jnp.concatenate([q * mask for mask in head_masks], 0), k)
                weights = []
                for h in range(4):
                    s = scores[h * GROUP : (h + 1) * GROUP] + away
                    peak = jnp.max(s, -1, keepdims=True)
                    weights.append(jnp.exp(s - peak).astype(BF16))
                weights = jnp.concatenate(weights, 0)
                values = dot(weights, v) / jnp.sum(weights.astype(F32), -1, keepdims=True)
                result = values[:GROUP]
                for h in range(1, 4):
                    own = values[h * GROUP : (h + 1) * GROUP]
                    result = jnp.where(lane >= HD * h, own, result)
                att[rows, lanes] = result.astype(BF16)
        return x + dot(att[:size, :width], out_w[...])

    def fine_step(w, carry):
        pick = lambda yes: jnp.where(yes, 1, 0)
        slots = [
            (pick(w == 2), pick(w == 3), pick(w >= 1)),
            (pick(w != 1), pick(w >= 1), pick(w == 3)),
        ]

        @pl.when(w == 1)
        def _():
            x_lon(0).wait_recv()
            x_lat(0).wait_recv()

        @pl.when(w == 2)
        def _():
            x_lon(1).wait_recv()
            x_lat(1).wait_recv()

        @pl.when(w == 3)
        def _():
            x_dia(0).wait_recv()
            x_dia(1).wait_recv()

        x, kinds = [], []
        for h, a, b in slots:
            quads = xq[h, pl.ds(1 + 2 * a, 2), pl.ds(1 + 2 * b, 2)]
            x.append(dot(window_p[...], quads.astype(F32).reshape(QUADS, D1).astype(BF16)))
            kinds.append(h + jnp.where((a == 1) & (lat == lats - 1), 2, 0))
        fine = section(jnp.concatenate(x, 0), gain1[...], triple1, out1, D1, kinds).astype(BF16)
        for slot, (h, a, b) in enumerate(slots):
            own = fine[slot * GROUP : (slot + 1) * GROUP]
            quads = dot(unwindow_p[...], own).reshape(2, 2, QUAD, D1)
            fq[h, pl.ds(1 + 2 * a, 2), pl.ds(1 + 2 * b, 2)] = quads.astype(BF16)
            fsum[...] += dot(sums[h, a], own)

        @pl.when(w == 0)
        def _():
            f_dia(0).start()
            f_dia(1).start()

        @pl.when(w == 1)
        def _():
            f_lon(0).start()
            f_lat(0).start()

        @pl.when(w == 2)
        def _():
            f_lon(1).start()
            f_lat(1).start()

        return carry

    lax.fori_loop(0, 4, fine_step, 0)
    for h in range(2):
        b_lon(h).start()
        b_lat(h).start()
        b_dia(h).start()

    l_patches.wait()
    l_merge.wait()
    l_triple2.wait()
    l_out2.wait()

    def patches(h, first_r, first_c):
        x = fq[h, pl.ds(first_r, 2), pl.ds(first_c, 2)]
        return dot(patches_p[...], x.astype(F32).reshape(QUADS, D1).astype(BF16))

    def coarse_half(h, carry):
        f_dia(h).wait_recv()
        f_lat(h).wait_recv()
        f_lon(h).wait_recv()
        for cq in range(4):
            x = patches(h, 2 + 2 * (cq // 2), 2 + 2 * (cq % 2))
            for off in range(4):
                rows = slice(cq * QUAD, (cq + 1) * QUAD)
                grouped[rows, off * D1 : (off + 1) * D1] = x[off * QUAD : (off + 1) * QUAD]
        for i in range(2):
            rows = slice(i * 80, (i + 1) * 80)
            groupn[rows, :] = layer_norm(grouped[rows, :], gainm[...]).astype(BF16)
        for i in range(4):
            lanes = slice(i * 256, (i + 1) * 256)
            coarse[:, lanes] = dot(groupn[...], mergew[:, lanes]).astype(BF16)
        x = dot(window_p[...], coarse[...])
        kind = h + jnp.where(lat == lats - 1, 2, 0)
        upper = section(x, gain2[...], triple2, out2, D2, [kind]).astype(BF16)
        up[h] = dot(unwindow_p[...], upper).reshape(2, 2, QUAD, D2).astype(BF16)
        u_lon(h).start()
        u_lat(h).start()
        u_dia(h).start()
        ur[h, 1, 1] = up[h, 0, 0]
        usums[...] += dot(sums[h, 2], upper)
        return carry

    lax.fori_loop(0, 2, coarse_half, 0)

    usum = usums[:8] + usums[8:]
    high = usum.astype(BF16).astype(F32)
    usum = jnp.concatenate([high, usum - high], 0).astype(BF16)
    l_split.wait()
    partial = fsum[0:4] + fsum[4:8]
    for ro in range(2):
        for co in range(2):
            off = 2 * ro + co
            t = dot(usum, splitw[:, off * D1 : (off + 1) * D1])
            t = t[:8] + t[8:]
            partial += t[4 * ro : 4 * ro + 4]
    part1[lat] = partial

    def ar_copy(buf, me, number, target):
        return pltpu.make_async_remote_copy(
            src_ref=buf.at[me],
            dst_ref=buf.at[me],
            send_sem=ar_send.at[number],
            recv_sem=ar_recv.at[number],
            device_id=target,
            device_id_type=MESH,
        )

    ar1 = [ar_copy(part1, lat, k, at(k, 0)) for k in range(1, lats)]
    ar2 = [ar_copy(part2, lon, lats + k, at(0, k)) for k in range(1, lons)]
    for c in ar1:
        c.start()

    def skip(h):
        b_lat(h).wait_recv()
        b_lon(h).wait_recv()
        b_dia(h).wait_recv()
        for cq in range(4):
            x = patches(h, 2 * (cq // 2), 2 * (cq % 2))
            for off in range(4):
                rows = slice(cq * QUAD, (cq + 1) * QUAD)
                fg[h, off, rows, :] = x[off * QUAD : (off + 1) * QUAD]

    def split(h):
        u_lat(h).wait_recv()
        u_lon(h).wait_recv()
        u_dia(h).wait_recv()
        ub[...] = ur[h].astype(F32).reshape(QUADS, D2).astype(BF16)
        for i in range(8):
            dst = slice((i % 2) * 256, (i % 2) * 256 + 256)
            fg[h, i // 2, :, dst] += dot(ub[...], splitw[:, i * 256 : (i + 1) * 256])
        for i in range(2):
            pieces = []
            for j in range(2):
                rows = slice((2 * i + j) * QUAD, (2 * i + j + 1) * QUAD)
                pieces += [fg[h, off, rows, :] for off in range(4)]
            x = jnp.concatenate(pieces, 0).astype(BF16)
            x = dot(rows_p[...], x).astype(BF16)
            for l in range(2):
                decoded[int(LEVELS[h][l]), i] = x[l * 144 : (l + 1) * 144]

    skip(0)
    l_rows.wait()
    split(0)
    for c in ar1:
        c.wait_recv()
    total = part1[0]
    for k in range(1, lats):
        total += part1[k]
    part2[lon] = total
    for c in ar2:
        c.start()
    skip(1)
    split(1)

    for c in ar2:
        c.wait_recv()
    total = part2[0]
    for k in range(1, lons):
        total += part2[k]
    means[...] = total * (1.0 / scale)
    for c in (x_lat, x_lon, x_dia, f_lat, f_lon, f_dia, b_lat, b_lon, b_dia, u_lat, u_lon, u_dia):
        c(0).wait_send()
        c(1).wait_send()
    for c in ar1 + ar2:
        c.wait_send()


def solution(mesh):
    lats, lons = mesh.shape["lat"], mesh.shape["lon"]
    *consts, scale = tables(lats, lons)

    def shards(
        latent,
        gain_first,
        triple_first,
        output_first,
        gain_merge,
        merge_weight,
        gain_second,
        triple_second,
        output_second,
        split_weight,
    ):
        hbm = pl.BlockSpec(memory_space=pl.ANY)
        vmem = pl.BlockSpec(memory_space=pltpu.VMEM)
        bf = lambda *shape: pltpu.VMEM(shape, BF16)
        f4 = lambda *shape: pltpu.VMEM(shape, F32)
        decoded, means = pl.pallas_call(
            functools.partial(kernel, lats, lons, scale),
            name="windows",
            out_shape=(
                jax.ShapeDtypeStruct((4, 2, 144, D1), BF16),
                jax.ShapeDtypeStruct((4, D1), F32),
            ),
            in_specs=[hbm] * 13 + [vmem] * 3,
            out_specs=(vmem, vmem),
            scratch_shapes=[
                bf(4, 4, 72, D1),
                bf(D1, 3 * D1),
                bf(D1, D1),
                bf(4 * D1, D2),
                bf(D2, 3 * D2),
                bf(D2, D2),
                bf(D2, 4 * D1),
                bf(QUADS, GROUP),
                bf(GROUP, QUADS),
                bf(QUADS, GROUP),
                bf(QUADS, QUADS),
                bf(2 * GROUP, 2 * QUADS),
                bf(2, 3, 16, GROUP),
                bf(2, 5, 5, QUAD, D1),
                bf(2, 6, 6, QUAD, D1),
                bf(2 * GROUP, D2),
                bf(2 * GROUP, D2),
                bf(2 * GROUP, D2),
                bf(2 * GROUP, D2),
                bf(2 * GROUP, D2),
                f4(4, GROUP, GROUP),
                f4(QUADS, 4 * D1),
                bf(QUADS, 4 * D1),
                bf(QUADS, D2),
                bf(2, 2, 2, QUAD, D2),
                bf(2, 2, 2, QUAD, D2),
                bf(QUADS, D2),
                f4(2, 4, QUADS, D1),
                f4(16, D1),
                f4(16, D2),
                f4(lats, 4, D1),
                f4(lons, 4, D1),
                pltpu.SemaphoreType.DMA((13,)),
                pltpu.SemaphoreType.DMA((24,)),
                pltpu.SemaphoreType.DMA((24,)),
                pltpu.SemaphoreType.DMA((lats + lons,)),
                pltpu.SemaphoreType.DMA((lats + lons,)),
            ],
            compiler_params=pltpu.CompilerParams(
                collective_id=0, has_side_effects=True, vmem_limit_bytes=60 * 1024 * 1024
            ),
        )(
            latent.reshape(4, 4, 72, D1),
            triple_first,
            output_first,
            merge_weight,
            triple_second,
            output_second,
            split_weight,
            *[jnp.asarray(c) for c in consts],
            gain_first.reshape(1, -1),
            gain_merge.reshape(1, -1),
            gain_second.reshape(1, -1),
        )
        return decoded.reshape(4, 12, 24, D1), means

    in_specs = (P(None, "lat", "lon", None),) + (P(),) * 9
    out_specs = (P(None, "lat", "lon", None), P())
    return jax.shard_map(
        shards, mesh=mesh, in_specs=in_specs, out_specs=out_specs, check_vma=False
    )
```

```python
import functools

import jax
import jax.numpy as jnp
import ml_dtypes
import numpy as np
from jax import lax
from jax.experimental import pallas as pl
from jax.experimental.pallas import tpu as pltpu
from jax.sharding import PartitionSpec as P

HD = 64
D1 = 512
D2 = 1024
EPS = 1e-05
MASKED = -1e30
QUAD = 40
QUADS = 160
GROUP = 144
LEVELS = np.array([[1, 2], [3, 0]])
MESH = pl.DeviceIdType.MESH
F32 = jnp.float32
BF16 = jnp.bfloat16


def permutation(rows, columns, place, source):
    matrix = np.zeros((rows, columns), np.float32)
    matrix[place.ravel(), source.ravel()] = 1.0
    return matrix.astype(ml_dtypes.bfloat16)


def grid(*extents):
    return np.meshgrid(*map(np.arange, extents), indexing="ij")


@functools.lru_cache(None)
def tables(lats, lons):
    q, l, r, c = grid(4, 2, 3, 6)
    quads = q * QUAD + l * 18 + r * 6 + c
    to_quads = permutation(QUADS, GROUP, quads, l * 72 + r * 24 + q * 6 + c)
    to_window = permutation(GROUP, QUADS, l * 72 + q * 18 + r * 6 + c, quads)
    ro, co, l, cr, cc = grid(2, 2, 2, 3, 6)
    row, col = 2 * cr + ro, 2 * cc + co
    quad = (row // 3) * 2 + col // 6
    to_patches = permutation(
        QUADS,
        QUADS,
        (2 * ro + co) * QUAD + l * 18 + cr * 6 + cc,
        quad * QUAD + l * 18 + (row % 3) * 6 + col % 6,
    )
    l, row, col = grid(2, 6, 24)
    j, c12 = col // 12, col % 12
    off = (row % 2) * 2 + c12 % 2
    to_rows = permutation(
        2 * GROUP,
        2 * QUADS,
        l * 144 + row * 24 + col,
        (j * 4 + off) * QUAD + l * 18 + (row // 2) * 6 + c12 // 2,
    )
    total_rows = 12 * lats
    position = (np.arange(total_rows, dtype=np.float32) + np.float32(0.5)) / np.float32(
        total_rows
    ) - np.float32(0.5)
    weights = np.cos(np.float32(np.pi) * position).astype(np.float32)
    scale = float(np.sqrt(24.0 * lons * np.sum(weights.astype(np.float64) ** 2)))
    high = weights.astype(ml_dtypes.bfloat16)
    low = (weights - high.astype(np.float32)).astype(ml_dtypes.bfloat16)
    parts = np.stack([high, low]).astype(np.float32)
    sums = np.zeros((lats, 2, 3, 16, GROUP), np.float32)
    l, quad, r, c = [v.ravel() for v in grid(2, 4, 3, 6)]
    token = np.arange(GROUP)
    for lat in range(lats):
        for half in range(2):
            level = LEVELS[half][l]
            for part in range(2):
                for a in range(2):
                    row = (lat * 12 + 3 + 6 * a + 3 * (quad // 2) + r) % total_rows
                    sums[lat, half, a, part * 4 + level, token] = parts[part, row]
                for ro in range(2):
                    row = (2 * (lat * 6 + 3 + 3 * (quad // 2) + r) + ro) % total_rows
                    sums[lat, half, 2, part * 8 + ro * 4 + level, token] = parts[part, row]
    return (
        to_quads,
        to_window,
        np.ascontiguousarray(to_window.T),
        to_patches,
        sums.astype(ml_dtypes.bfloat16),
        to_rows,
        scale,
    )


def dot(a, b):
    return jnp.dot(a, b, preferred_element_type=F32)


def dot_nt(a, b):
    return lax.dot_general(a, b, (((1,), (1,)), ((), ())), preferred_element_type=F32)


def layer_norm(x, gain):
    mean = jnp.mean(x, -1, keepdims=True)
    centred = x - mean
    var = jnp.mean(centred * centred, -1, keepdims=True)
    return centred * lax.rsqrt(var + EPS) * gain


def kernel(
    lats,
    lons,
    scale,
    latent_h,
    triple1_h,
    out1_h,
    merge_h,
    triple2_h,
    out2_h,
    split_h,
    quads_h,
    window_h,
    unwindow_h,
    patches_h,
    sums_h,
    gain1,
    gainm,
    gain2,
    pieces_h,
    means,
    latent,
    triple1,
    out1,
    mergew,
    triple2,
    out2,
    splitw,
    quads_p,
    window_p,
    unwindow_p,
    patches_p,
    sums,
    xq,
    fq,
    normed,
    qs,
    ks,
    vs,
    att,
    bias,
    grouped,
    groupn,
    coarse,
    up,
    ur,
    ub,
    fg,
    fsum,
    usums,
    pieces_v,
    part1,
    part2,
    load_sem,
    send_sem,
    recv_sem,
    ar_send,
    ar_recv,
):
    lat = lax.axis_index("lat")
    lon = lax.axis_index("lon")

    def at(dlat, dlon):
        return {
            "lat": lax.rem(lat + dlat + lats, lats),
            "lon": lax.rem(lon + dlon + lons, lons),
        }

    loads = [
        pltpu.make_async_copy(s, d, load_sem.at[i])
        for i, (s, d) in enumerate(
            [
                (latent_h, latent),
                (quads_h, quads_p),
                (window_h, window_p),
                (triple1_h, triple1),
                (unwindow_h, unwindow_p),
                (out1_h, out1),
                (sums_h.at[lat], sums),
                (patches_h, patches_p),
                (merge_h, mergew),
                (triple2_h, triple2),
                (out2_h, out2),
                (split_h, splitw),
            ]
        )
    ]
    (l_latent, l_quads, l_window, l_triple1, l_unwindow, l_out1, l_sums) = loads[:7]
    (l_patches, l_merge, l_triple2, l_out2, l_split) = loads[7:]
    for load in loads:
        load.start()

    barrier = pltpu.get_barrier_semaphore()
    peers = [at(k, 0) for k in range(1, lats)] + [at(0, k) for k in range(1, lons)]
    peers += [at(1, 1), at(-1, -1)]
    for peer in peers:
        pl.semaphore_signal(barrier, inc=1, device_id=peer, device_id_type=MESH)

    tq = lax.broadcasted_iota(jnp.int32, (GROUP, GROUP), 0)
    tk = lax.broadcasted_iota(jnp.int32, (GROUP, GROUP), 1)
    lev_q, lev_k = tq >= 72, tk >= 72
    half_q = jnp.where(lev_q, tq - 72, tq) >= 36
    half_k = jnp.where(lev_k, tk - 72, tk) >= 36
    other_lev = jnp.where(lev_q == lev_k, 0.0, MASKED).astype(F32)
    other_row = jnp.where(half_q == half_k, 0.0, MASKED).astype(F32)
    bias[0] = jnp.zeros((GROUP, GROUP), F32)
    bias[1] = other_lev
    bias[2] = other_row
    bias[3] = jnp.minimum(other_lev, other_row)
    fsum[...] = jnp.zeros_like(fsum)
    usums[...] = jnp.zeros_like(usums)

    def copy(number, half, src, dst, target):
        number = number + 12 * half
        return pltpu.make_async_remote_copy(
            src_ref=src,
            dst_ref=dst,
            send_sem=send_sem.at[number],
            recv_sem=recv_sem.at[number],
            device_id=target,
            device_id_type=MESH,
        )

    three, edge = pl.ds(1, 3), pl.ds(2, 3)

    def x_lat(h):
        return copy(0, h, xq.at[h, 0, three], xq.at[h, 4, three], at(-1, 0))

    def x_lon(h):
        return copy(1, h, xq.at[h, three, 0], xq.at[h, three, 4], at(0, -1))

    def x_dia(h):
        return copy(2, h, xq.at[h, 0, 0], xq.at[h, 4, 4], at(-1, -1))

    def f_lat(h):
        return copy(3, h, fq.at[h, 1, edge], fq.at[h, 5, edge], at(-1, 0))

    def f_lon(h):
        return copy(4, h, fq.at[h, edge, 1], fq.at[h, edge, 5], at(0, -1))

    def f_dia(h):
        return copy(5, h, fq.at[h, 1, 1], fq.at[h, 5, 5], at(-1, -1))

    def b_lat(h):
        return copy(6, h, fq.at[h, 4, three], fq.at[h, 0, three], at(1, 0))

    def b_lon(h):
        return copy(7, h, fq.at[h, three, 4], fq.at[h, three, 0], at(0, 1))

    def b_dia(h):
        return copy(8, h, fq.at[h, 4, 4], fq.at[h, 0, 0], at(1, 1))

    def u_lat(h):
        return copy(9, h, up.at[h, 1, 0], ur.at[h, 0, 1], at(1, 0))

    def u_lon(h):
        return copy(10, h, up.at[h, 0, 1], ur.at[h, 1, 0], at(0, 1))

    def u_dia(h):
        return copy(11, h, up.at[h, 1, 1], ur.at[h, 0, 0], at(1, 1))

    l_latent.wait()
    l_quads.wait()

    def form_quads(h):
        def form(qr, carry):
            rows = jnp.concatenate([latent[int(l), qr].astype(F32) for l in LEVELS[h]], 0)
            quads = dot(quads_p[...], rows.astype(BF16))
            xq[h, qr, pl.ds(0, 4)] = quads.reshape(4, QUAD, D1).astype(BF16)
            return carry

        lax.fori_loop(0, 4, form, 0, unroll=True)

    form_quads(0)
    pl.semaphore_wait(barrier, len(peers))
    x_lon(0).start()
    x_lat(0).start()
    x_dia(0).start()
    form_quads(1)
    x_lon(1).start()
    x_lat(1).start()
    x_dia(1).start()

    l_window.wait()
    l_triple1.wait()
    l_unwindow.wait()
    l_out1.wait()
    l_sums.wait()

    lane = lax.broadcasted_iota(jnp.int32, (1, 256), 1)
    head_masks = [((lane >= HD * h) & (lane < HD * (h + 1))).astype(BF16) for h in range(4)]

    def section(x, gain, triple, out_w, width, kinds):
        count = len(kinds)
        size = count * GROUP
        normed[:size, :width] = layer_norm(x, gain).astype(BF16)
        groups = width // 256

        for which, dest in enumerate((qs, ks, vs)):

            def project(i, carry, which=which, dest=dest):
                src = pl.ds(pl.multiple_of(which * width + i * 256, 256), 256)
                dst = pl.ds(pl.multiple_of(i * 256, 256), 256)
                value = dot(normed[:size, :width], triple[:, src]).astype(BF16)
                if which == 0:
                    value = value * jnp.asarray(HD**-0.5, BF16)
                dest[:size, dst] = value
                return carry

            lax.fori_loop(0, groups, project, 0, unroll=True)

        for slot in range(count):
            for hg in range(groups):
                rows = slice(slot * GROUP, (slot + 1) * GROUP)
                lanes = slice(hg * 256, (hg + 1) * 256)
                q, k, v = qs[rows, lanes], ks[rows, lanes], vs[rows, lanes]
                away = bias[kinds[slot]]
                scores = dot_nt(jnp.concatenate([q * mask for mask in head_masks], 0), k)
                weights = []
                for h in range(4):
                    s = scores[h * GROUP : (h + 1) * GROUP] + away
                    peak = jnp.max(s, -1, keepdims=True)
                    weights.append(jnp.exp(s - peak).astype(BF16))
                weights = jnp.concatenate(weights, 0)
                values = dot(weights, v) / jnp.sum(weights.astype(F32), -1, keepdims=True)
                result = values[:GROUP]
                for h in range(1, 4):
                    own = values[h * GROUP : (h + 1) * GROUP]
                    result = jnp.where(lane >= HD * h, own, result)
                att[rows, lanes] = result.astype(BF16)
        return x + dot(att[:size, :width], out_w[...])

    def fine_step(w, carry):
        pick = lambda yes: jnp.where(yes, 1, 0)
        slots = [
            (pick(w == 2), pick(w == 3), pick(w >= 1)),
            (pick(w != 1), pick(w >= 1), pick(w == 3)),
        ]

        @pl.when(w == 1)
        def _():
            x_lon(0).wait_recv()
            x_lat(0).wait_recv()

        @pl.when(w == 2)
        def _():
            x_lon(1).wait_recv()
            x_lat(1).wait_recv()

        @pl.when(w == 3)
        def _():
            x_dia(0).wait_recv()
            x_dia(1).wait_recv()

        x, kinds = [], []
        for h, a, b in slots:
            quads = xq[h, pl.ds(1 + 2 * a, 2), pl.ds(1 + 2 * b, 2)]
            x.append(dot(window_p[...], quads.astype(F32).reshape(QUADS, D1).astype(BF16)))
            kinds.append(h + jnp.where((a == 1) & (lat == lats - 1), 2, 0))
        fine = section(jnp.concatenate(x, 0), gain1[...], triple1, out1, D1, kinds).astype(BF16)
        for slot, (h, a, b) in enumerate(slots):
            own = fine[slot * GROUP : (slot + 1) * GROUP]
            quads = dot(unwindow_p[...], own).reshape(2, 2, QUAD, D1)
            fq[h, pl.ds(1 + 2 * a, 2), pl.ds(1 + 2 * b, 2)] = quads.astype(BF16)
            fsum[...] += dot(sums[h, a], own)

        @pl.when(w == 0)
        def _():
            f_dia(0).start()
            f_dia(1).start()

        @pl.when(w == 1)
        def _():
            f_lon(0).start()
            f_lat(0).start()

        @pl.when(w == 2)
        def _():
            f_lon(1).start()
            f_lat(1).start()

        return carry

    lax.fori_loop(0, 4, fine_step, 0)
    for h in range(2):
        b_lon(h).start()
        b_lat(h).start()
        b_dia(h).start()

    l_patches.wait()
    l_merge.wait()
    l_triple2.wait()
    l_out2.wait()

    def patches(h, first_r, first_c):
        x = fq[h, pl.ds(first_r, 2), pl.ds(first_c, 2)]
        return dot(patches_p[...], x.astype(F32).reshape(QUADS, D1).astype(BF16))

    def coarse_half(h, carry):
        f_dia(h).wait_recv()
        f_lat(h).wait_recv()
        f_lon(h).wait_recv()
        for cq in range(4):
            x = patches(h, 2 + 2 * (cq // 2), 2 + 2 * (cq % 2))
            for off in range(4):
                rows = slice(cq * QUAD, (cq + 1) * QUAD)
                grouped[rows, off * D1 : (off + 1) * D1] = x[off * QUAD : (off + 1) * QUAD]
        for i in range(2):
            rows = slice(i * 80, (i + 1) * 80)
            groupn[rows, :] = layer_norm(grouped[rows, :], gainm[...]).astype(BF16)
        for i in range(4):
            lanes = slice(i * 256, (i + 1) * 256)
            coarse[:, lanes] = dot(groupn[...], mergew[:, lanes]).astype(BF16)
        x = dot(window_p[...], coarse[...])
        kind = h + jnp.where(lat == lats - 1, 2, 0)
        upper = section(x, gain2[...], triple2, out2, D2, [kind]).astype(BF16)
        up[h] = dot(unwindow_p[...], upper).reshape(2, 2, QUAD, D2).astype(BF16)

        @pl.when(h == 0)
        def _():
            u_lon(0).start()
            u_lat(0).start()
            u_dia(0).start()

        ur[h, 1, 1] = up[h, 0, 0]
        usums[...] += dot(sums[h, 2], upper)
        return carry

    lax.fori_loop(0, 2, coarse_half, 0)

    usum = usums[:8] + usums[8:]
    high = usum.astype(BF16).astype(F32)
    usum = jnp.concatenate([high, usum - high], 0).astype(BF16)
    l_split.wait()
    partial = fsum[0:4] + fsum[4:8]
    for ro in range(2):
        for co in range(2):
            off = 2 * ro + co
            t = dot(usum, splitw[:, off * D1 : (off + 1) * D1])
            t = t[:8] + t[8:]
            partial += t[4 * ro : 4 * ro + 4]
    part1[lat] = partial

    def ar_copy(buf, me, number, target):
        return pltpu.make_async_remote_copy(
            src_ref=buf.at[me],
            dst_ref=buf.at[me],
            send_sem=ar_send.at[number],
            recv_sem=ar_recv.at[number],
            device_id=target,
            device_id_type=MESH,
        )

    ar1 = [ar_copy(part1, lat, k, at(k, 0)) for k in range(1, lats)]
    ar2 = [ar_copy(part2, lon, lats + k, at(0, k)) for k in range(1, lons)]
    for c in ar1:
        c.start()
    u_lon(1).start()
    u_lat(1).start()
    u_dia(1).start()

    def skip(h):
        b_lat(h).wait_recv()
        b_lon(h).wait_recv()
        b_dia(h).wait_recv()
        for cq in range(4):
            x = patches(h, 2 * (cq // 2), 2 * (cq % 2))
            for off in range(4):
                rows = slice(cq * QUAD, (cq + 1) * QUAD)
                fg[h, off, rows, :] = x[off * QUAD : (off + 1) * QUAD]

    def out_copy(h, i):
        return pltpu.make_async_copy(pieces_v.at[h, i], pieces_h.at[h, i], load_sem.at[12 + 2 * h + i])

    def split(h):
        u_lat(h).wait_recv()
        u_lon(h).wait_recv()
        u_dia(h).wait_recv()
        ub[...] = ur[h].astype(F32).reshape(QUADS, D2).astype(BF16)
        for i in range(8):
            dst = slice((i % 2) * 256, (i % 2) * 256 + 256)
            fg[h, i // 2, :, dst] += dot(ub[...], splitw[:, i * 256 : (i + 1) * 256])
        for i in range(2):
            pieces = []
            for j in range(2):
                rows = slice((2 * i + j) * QUAD, (2 * i + j + 1) * QUAD)
                pieces += [fg[h, off, rows, :] for off in range(4)]
            pieces_v[h, i] = jnp.concatenate(pieces, 0).astype(BF16)
            out_copy(h, i).start()

    skip(0)
    split(0)
    for c in ar1:
        c.wait_recv()
    total = part1[0]
    for k in range(1, lats):
        total += part1[k]
    part2[lon] = total
    for c in ar2:
        c.start()
    skip(1)
    split(1)

    for c in ar2:
        c.wait_recv()
    total = part2[0]
    for k in range(1, lons):
        total += part2[k]
    means[...] = total * (1.0 / scale)
    for c in (x_lat, x_lon, x_dia, f_lat, f_lon, f_dia, b_lat, b_lon, b_dia, u_lat, u_lon, u_dia):
        c(0).wait_send()
        c(1).wait_send()
    for h in range(2):
        for i in range(2):
            out_copy(h, i).wait()
    for c in ar1 + ar2:
        c.wait_send()


def place(pieces_h, rows_p, means_in, decoded_h, means, pieces, decoded, in_sem, out_sem):
    steps = [(h, i) for h in range(2) for i in range(2)]
    loads = [
        pltpu.make_async_copy(pieces_h.at[h, i], pieces.at[h, i], in_sem.at[n])
        for n, (h, i) in enumerate(steps)
    ]
    for load in loads:
        load.start()
    means[...] = means_in[...]
    stores = []
    for n, (h, i) in enumerate(steps):
        loads[n].wait()
        x = dot(rows_p[...], pieces[h, i]).astype(BF16)
        for l in range(2):
            level = int(LEVELS[h][l])
            decoded[level, i] = x[l * 144 : (l + 1) * 144]
            stores.append(
                pltpu.make_async_copy(
                    decoded.at[level, i], decoded_h.at[level, i], out_sem.at[2 * n + l]
                )
            )
            stores[-1].start()
    for store in stores:
        store.wait()


def solution(mesh):
    lats, lons = mesh.shape["lat"], mesh.shape["lon"]
    *consts, to_rows, scale = tables(lats, lons)

    def shards(
        latent,
        gain_first,
        triple_first,
        output_first,
        gain_merge,
        merge_weight,
        gain_second,
        triple_second,
        output_second,
        split_weight,
    ):
        hbm = pl.BlockSpec(memory_space=pl.ANY)
        vmem = pl.BlockSpec(memory_space=pltpu.VMEM)
        bf = lambda *shape: pltpu.VMEM(shape, BF16)
        f4 = lambda *shape: pltpu.VMEM(shape, F32)
        pieces, means = pl.pallas_call(
            functools.partial(kernel, lats, lons, scale),
            name="windows",
            out_shape=(
                jax.ShapeDtypeStruct((2, 2, 2 * QUADS, D1), BF16),
                jax.ShapeDtypeStruct((4, D1), F32),
            ),
            in_specs=[hbm] * 12 + [vmem] * 3,
            out_specs=(hbm, vmem),
            scratch_shapes=[
                bf(4, 4, 72, D1),
                bf(D1, 3 * D1),
                bf(D1, D1),
                bf(4 * D1, D2),
                bf(D2, 3 * D2),
                bf(D2, D2),
                bf(D2, 4 * D1),
                bf(QUADS, GROUP),
                bf(GROUP, QUADS),
                bf(QUADS, GROUP),
                bf(QUADS, QUADS),
                bf(2, 3, 16, GROUP),
                bf(2, 5, 5, QUAD, D1),
                bf(2, 6, 6, QUAD, D1),
                bf(2 * GROUP, D2),
                bf(2 * GROUP, D2),
                bf(2 * GROUP, D2),
                bf(2 * GROUP, D2),
                bf(2 * GROUP, D2),
                f4(4, GROUP, GROUP),
                f4(QUADS, 4 * D1),
                bf(QUADS, 4 * D1),
                bf(QUADS, D2),
                bf(2, 2, 2, QUAD, D2),
                bf(2, 2, 2, QUAD, D2),
                bf(QUADS, D2),
                f4(2, 4, QUADS, D1),
                f4(16, D1),
                f4(16, D2),
                bf(2, 2, 2 * QUADS, D1),
                f4(lats, 4, D1),
                f4(lons, 4, D1),
                pltpu.SemaphoreType.DMA((16,)),
                pltpu.SemaphoreType.DMA((24,)),
                pltpu.SemaphoreType.DMA((24,)),
                pltpu.SemaphoreType.DMA((lats + lons,)),
                pltpu.SemaphoreType.DMA((lats + lons,)),
            ],
            compiler_params=pltpu.CompilerParams(
                collective_id=0, has_side_effects=True, vmem_limit_bytes=60 * 1024 * 1024
            ),
        )(
            latent.reshape(4, 4, 72, D1),
            triple_first,
            output_first,
            merge_weight,
            triple_second,
            output_second,
            split_weight,
            *[jnp.asarray(c) for c in consts],
            gain_first.reshape(1, -1),
            gain_merge.reshape(1, -1),
            gain_second.reshape(1, -1),
        )
        decoded, means = pl.pallas_call(
            place,
            name="place",
            out_shape=(
                jax.ShapeDtypeStruct((4, 2, 144, D1), BF16),
                jax.ShapeDtypeStruct((4, D1), F32),
            ),
            in_specs=[hbm, vmem, vmem],
            out_specs=(hbm, vmem),
            scratch_shapes=[
                bf(2, 2, 2 * QUADS, D1),
                bf(4, 2, 144, D1),
                pltpu.SemaphoreType.DMA((4,)),
                pltpu.SemaphoreType.DMA((8,)),
            ],
            cost_estimate=pl.CostEstimate(
                flops=2 * 8 * 144 * 320 * D1, bytes_accessed=4000000, transcendentals=0
            ),
            compiler_params=pltpu.CompilerParams(vmem_limit_bytes=16 * 1024 * 1024),
        )(pieces, jnp.asarray(to_rows), means)
        return decoded.reshape(4, 12, 24, D1), means

    in_specs = (P(None, "lat", "lon", None),) + (P(),) * 9
    out_specs = (P(None, "lat", "lon", None), P())
    return jax.shard_map(
        shards, mesh=mesh, in_specs=in_specs, out_specs=out_specs, check_vma=False
    )
```

```python
import functools

import jax
import jax.numpy as jnp
import ml_dtypes
import numpy as np
from jax import lax
from jax.experimental import pallas as pl
from jax.experimental.pallas import tpu as pltpu
from jax.sharding import PartitionSpec as P

HD = 64
D1 = 512
D2 = 1024
EPS = 1e-05
MASKED = -1e30
CELLS = 36
SENT = 72
QUAD = 40
QUADS = 160
GROUP = 144
LEVELS = np.array([[1, 2], [3, 0]])
MESH = pl.DeviceIdType.MESH
F32 = jnp.float32
BF16 = jnp.bfloat16


def permutation(rows, columns, place, source):
    matrix = np.zeros((rows, columns), np.float32)
    matrix[place.ravel(), source.ravel()] = 1.0
    return matrix.astype(ml_dtypes.bfloat16)


def grid(*extents):
    return np.meshgrid(*map(np.arange, extents), indexing="ij")


@functools.lru_cache(None)
def tables(lats, lons):
    q, f, l, r, c = grid(4, 2, 2, 3, 6)
    token = l * 18 + r * 6 + c
    quads = q * SENT + f * CELLS + token
    to_quads = permutation(
        4 * SENT, 2 * GROUP, quads, f * GROUP + l * 72 + r * 24 + q * 6 + c
    )
    window = l * 72 + q * 18 + r * 6 + c
    to_window = permutation(2 * GROUP, 4 * SENT, f * GROUP + window, quads)
    to_coarse = permutation(2 * QUADS, 4 * SENT, f * QUADS + q * QUAD + token, quads)
    coarse_window = permutation(GROUP, QUADS, window[:, 0], (q * QUAD + token)[:, 0])
    f, ro, co, l, cr, cc = grid(2, 2, 2, 2, 3, 6)
    row, col = 2 * cr + ro, 2 * cc + co
    quad = (row // 3) * 2 + col // 6
    to_patches = permutation(
        2 * QUADS,
        4 * SENT,
        f * QUADS + (2 * ro + co) * QUAD + l * 18 + cr * 6 + cc,
        quad * SENT + f * CELLS + l * 18 + (row % 3) * 6 + col % 6,
    )
    l, row, col = grid(2, 6, 24)
    j, c12 = col // 12, col % 12
    off = (row % 2) * 2 + c12 % 2
    to_rows = permutation(
        2 * GROUP,
        2 * QUADS,
        l * 144 + row * 24 + col,
        (j * 4 + off) * QUAD + l * 18 + (row // 2) * 6 + c12 // 2,
    )
    total_rows = 12 * lats
    position = (np.arange(total_rows, dtype=np.float32) + np.float32(0.5)) / np.float32(
        total_rows
    ) - np.float32(0.5)
    weights = np.cos(np.float32(np.pi) * position).astype(np.float32)
    scale = float(np.sqrt(24.0 * lons * np.sum(weights.astype(np.float64) ** 2)))
    high = weights.astype(ml_dtypes.bfloat16)
    low = (weights - high.astype(np.float32)).astype(ml_dtypes.bfloat16)
    parts = np.stack([high, low]).astype(np.float32)
    sums = np.zeros((lats, 2, 3, 16, GROUP), np.float32)
    l, quad, r, c = [v.ravel() for v in grid(2, 4, 3, 6)]
    token = np.arange(GROUP)
    for lat in range(lats):
        for half in range(2):
            level = LEVELS[half][l]
            for part in range(2):
                for a in range(2):
                    row = (lat * 12 + 3 + 6 * a + 3 * (quad // 2) + r) % total_rows
                    sums[lat, half, a, part * 4 + level, token] = parts[part, row]
                for ro in range(2):
                    row = (2 * (lat * 6 + 3 + 3 * (quad // 2) + r) + ro) % total_rows
                    sums[lat, half, 2, part * 8 + ro * 4 + level, token] = parts[part, row]
    return (
        to_quads,
        to_window,
        np.ascontiguousarray(to_window.T),
        to_patches,
        to_coarse,
        coarse_window,
        sums.astype(ml_dtypes.bfloat16),
        to_rows,
        scale,
    )


def dot(a, b):
    return jnp.dot(a, b, preferred_element_type=F32)


def dot_nt(a, b):
    return lax.dot_general(a, b, (((1,), (1,)), ((), ())), preferred_element_type=F32)


def stacked(x):
    half = x.shape[1] // 2
    return jnp.concatenate([x[:, :half], x[:, half:]], 0)


def unstacked(x):
    half = x.shape[0] // 2
    return jnp.concatenate([x[:half], x[half:]], 1)


def quad_rows(quads):
    rows = quads.shape[0] * quads.shape[1] * quads.shape[2]
    return quads.astype(F32).reshape(rows, quads.shape[3]).astype(BF16)


def layer_norm(x, gain):
    mean = jnp.mean(x, -1, keepdims=True)
    centred = x - mean
    var = jnp.mean(centred * centred, -1, keepdims=True)
    return centred * lax.rsqrt(var + EPS) * gain


def kernel(
    lats,
    lons,
    scale,
    latent_h,
    triple1_h,
    out1_h,
    merge_h,
    triple2_h,
    out2_h,
    split_h,
    quads_h,
    window_h,
    unwindow_h,
    patches_h,
    to_coarse_h,
    coarse_window_h,
    sums_h,
    rows_h,
    gain1,
    gainm,
    gain2,
    decoded_h,
    means,
    latent,
    triple1,
    out1,
    mergew,
    triple2,
    out2,
    splitw,
    quads_p,
    window_p,
    unwindow_p,
    patches_p,
    to_coarse_p,
    coarse_window_p,
    sums,
    rows_p,
    xq,
    fq,
    normed,
    qs,
    ks,
    vs,
    att,
    bias,
    grouped,
    groupn,
    coarse,
    up,
    ur,
    ub,
    fg,
    fsum,
    usums,
    decoded_v,
    part1,
    part2,
    load_sem,
    out_sem,
    send_sem,
    recv_sem,
    ar_send,
    ar_recv,
):
    lat = lax.axis_index("lat")
    lon = lax.axis_index("lon")

    def at(dlat, dlon):
        return {
            "lat": lax.rem(lat + dlat + lats, lats),
            "lon": lax.rem(lon + dlon + lons, lons),
        }

    loads = [
        pltpu.make_async_copy(s, d, load_sem.at[i])
        for i, (s, d) in enumerate(
            [
                (latent_h, latent),
                (quads_h, quads_p),
                (window_h, window_p),
                (triple1_h, triple1),
                (unwindow_h, unwindow_p),
                (out1_h, out1),
                (sums_h.at[lat], sums),
                (patches_h, patches_p),
                (merge_h, mergew),
                (triple2_h, triple2),
                (out2_h, out2),
                (split_h, splitw),
                (to_coarse_h, to_coarse_p),
                (coarse_window_h, coarse_window_p),
                (rows_h, rows_p),
            ]
        )
    ]
    (l_latent, l_quads, l_window, l_triple1, l_unwindow, l_out1, l_sums) = loads[:7]
    (l_patches, l_merge, l_triple2, l_out2, l_split) = loads[7:12]
    (l_coarse, l_window2, l_rows) = loads[12:]
    for load in loads:
        load.start()

    barrier = pltpu.get_barrier_semaphore()
    peers = [at(k, 0) for k in range(1, lats)] + [at(0, k) for k in range(1, lons)]
    peers += [at(1, 1), at(-1, -1)]
    for peer in peers:
        pl.semaphore_signal(barrier, inc=1, device_id=peer, device_id_type=MESH)

    tq = lax.broadcasted_iota(jnp.int32, (GROUP, GROUP), 0)
    tk = lax.broadcasted_iota(jnp.int32, (GROUP, GROUP), 1)
    lev_q, lev_k = tq >= 72, tk >= 72
    half_q = jnp.where(lev_q, tq - 72, tq) >= 36
    half_k = jnp.where(lev_k, tk - 72, tk) >= 36
    other_lev = jnp.where(lev_q == lev_k, 0.0, MASKED).astype(F32)
    other_row = jnp.where(half_q == half_k, 0.0, MASKED).astype(F32)
    bias[0] = jnp.zeros((GROUP, GROUP), F32)
    bias[1] = other_lev
    bias[2] = other_row
    bias[3] = jnp.minimum(other_lev, other_row)
    fsum[...] = jnp.zeros_like(fsum)
    usums[...] = jnp.zeros_like(usums)

    def copy(number, half, src, dst, target):
        number = number + 12 * half
        return pltpu.make_async_remote_copy(
            src_ref=src,
            dst_ref=dst,
            send_sem=send_sem.at[number],
            recv_sem=recv_sem.at[number],
            device_id=target,
            device_id_type=MESH,
        )

    three, edge = pl.ds(1, 3), pl.ds(2, 3)

    def x_lat(h):
        return copy(0, h, xq.at[h, 0, three], xq.at[h, 4, three], at(-1, 0))

    def x_lon(h):
        return copy(1, h, xq.at[h, three, 0], xq.at[h, three, 4], at(0, -1))

    def x_dia(h):
        return copy(2, h, xq.at[h, 0, 0], xq.at[h, 4, 4], at(-1, -1))

    def f_lat(h):
        return copy(3, h, fq.at[h, 1, edge], fq.at[h, 5, edge], at(-1, 0))

    def f_lon(h):
        return copy(4, h, fq.at[h, edge, 1], fq.at[h, edge, 5], at(0, -1))

    def f_dia(h):
        return copy(5, h, fq.at[h, 1, 1], fq.at[h, 5, 5], at(-1, -1))

    def b_lat(h):
        return copy(6, h, fq.at[h, 4, three], fq.at[h, 0, three], at(1, 0))

    def b_lon(h):
        return copy(7, h, fq.at[h, three, 4], fq.at[h, three, 0], at(0, 1))

    def b_dia(h):
        return copy(8, h, fq.at[h, 4, 4], fq.at[h, 0, 0], at(1, 1))

    def u_lat(h):
        return copy(9, h, up.at[h, 1, 0], ur.at[h, 0, 1], at(1, 0))

    def u_lon(h):
        return copy(10, h, up.at[h, 0, 1], ur.at[h, 1, 0], at(0, 1))

    def u_dia(h):
        return copy(11, h, up.at[h, 1, 1], ur.at[h, 0, 0], at(1, 1))

    l_latent.wait()
    l_quads.wait()

    def form_quads(h):
        def form(qr, carry):
            rows = jnp.concatenate([latent[int(l), qr].astype(F32) for l in LEVELS[h]], 0)
            quads = dot(quads_p[...], stacked(rows.astype(BF16)))
            xq[h, qr, pl.ds(0, 4)] = quads.reshape(4, SENT, D1 // 2).astype(BF16)
            return carry

        lax.fori_loop(0, 4, form, 0, unroll=True)

    form_quads(0)
    pl.semaphore_wait(barrier, len(peers))
    x_lon(0).start()
    x_lat(0).start()
    x_dia(0).start()
    form_quads(1)
    x_lon(1).start()
    x_lat(1).start()
    x_dia(1).start()

    l_window.wait()
    l_triple1.wait()
    l_unwindow.wait()
    l_out1.wait()
    l_sums.wait()

    lane = lax.broadcasted_iota(jnp.int32, (1, 256), 1)
    head_masks = [((lane >= HD * h) & (lane < HD * (h + 1))).astype(BF16) for h in range(4)]

    def section(x, gain, triple, out_w, width, kinds):
        count = len(kinds)
        size = count * GROUP
        normed[:size, :width] = layer_norm(x, gain).astype(BF16)
        groups = width // 256

        for which, dest in enumerate((qs, ks, vs)):

            def project(i, carry, which=which, dest=dest):
                src = pl.ds(pl.multiple_of(which * width + i * 256, 256), 256)
                dst = pl.ds(pl.multiple_of(i * 256, 256), 256)
                value = dot(normed[:size, :width], triple[:, src]).astype(BF16)
                if which == 0:
                    value = value * jnp.asarray(HD**-0.5, BF16)
                dest[:size, dst] = value
                return carry

            lax.fori_loop(0, groups, project, 0, unroll=True)

        for slot in range(count):
            for hg in range(groups):
                rows = slice(slot * GROUP, (slot + 1) * GROUP)
                lanes = slice(hg * 256, (hg + 1) * 256)
                q, k, v = qs[rows, lanes], ks[rows, lanes], vs[rows, lanes]
                away = bias[kinds[slot]]
                scores = dot_nt(jnp.concatenate([q * mask for mask in head_masks], 0), k)
                weights = []
                for h in range(4):
                    s = scores[h * GROUP : (h + 1) * GROUP] + away
                    peak = jnp.max(s, -1, keepdims=True)
                    weights.append(jnp.exp(s - peak).astype(BF16))
                weights = jnp.concatenate(weights, 0)
                values = dot(weights, v) / jnp.sum(weights.astype(F32), -1, keepdims=True)
                result = values[:GROUP]
                for h in range(1, 4):
                    own = values[h * GROUP : (h + 1) * GROUP]
                    result = jnp.where(lane >= HD * h, own, result)
                att[rows, lanes] = result.astype(BF16)
        return x + dot(att[:size, :width], out_w[...])

    def fine_step(w, carry):
        pick = lambda yes: jnp.where(yes, 1, 0)
        slots = [
            (pick(w == 2), pick(w == 3), pick(w >= 1)),
            (pick(w != 1), pick(w >= 1), pick(w == 3)),
        ]

        @pl.when(w == 1)
        def _():
            x_lon(0).wait_recv()
            x_lat(0).wait_recv()

        @pl.when(w == 2)
        def _():
            x_lon(1).wait_recv()
            x_lat(1).wait_recv()

        @pl.when(w == 3)
        def _():
            x_dia(0).wait_recv()
            x_dia(1).wait_recv()

        x, kinds = [], []
        for h, a, b in slots:
            quads = xq[h, pl.ds(1 + 2 * a, 2), pl.ds(1 + 2 * b, 2)]
            x.append(unstacked(dot(window_p[...], quad_rows(quads))))
            kinds.append(h + jnp.where((a == 1) & (lat == lats - 1), 2, 0))
        fine = section(jnp.concatenate(x, 0), gain1[...], triple1, out1, D1, kinds).astype(BF16)
        for slot, (h, a, b) in enumerate(slots):
            own = fine[slot * GROUP : (slot + 1) * GROUP]
            quads = dot(unwindow_p[...], stacked(own)).reshape(2, 2, SENT, D1 // 2)
            fq[h, pl.ds(1 + 2 * a, 2), pl.ds(1 + 2 * b, 2)] = quads.astype(BF16)
            fsum[...] += dot(sums[h, a], own)

        @pl.when(w == 0)
        def _():
            f_dia(0).start()
            f_dia(1).start()

        @pl.when(w == 1)
        def _():
            f_lon(0).start()
            f_lat(0).start()

        @pl.when(w == 2)
        def _():
            f_lon(1).start()
            f_lat(1).start()

        return carry

    lax.fori_loop(0, 4, fine_step, 0)
    for h in range(2):
        b_lon(h).start()
        b_lat(h).start()
        b_dia(h).start()

    l_patches.wait()
    l_window2.wait()
    l_merge.wait()
    l_triple2.wait()
    l_out2.wait()

    def patches(h, first_r, first_c):
        x = fq[h, pl.ds(first_r, 2), pl.ds(first_c, 2)]
        return unstacked(dot(patches_p[...], quad_rows(x)))

    def coarse_half(h, carry):
        f_dia(h).wait_recv()
        f_lat(h).wait_recv()
        f_lon(h).wait_recv()
        for cq in range(4):
            x = patches(h, 2 + 2 * (cq // 2), 2 + 2 * (cq % 2))
            for off in range(4):
                rows = slice(cq * QUAD, (cq + 1) * QUAD)
                grouped[rows, off * D1 : (off + 1) * D1] = x[off * QUAD : (off + 1) * QUAD]
        for i in range(2):
            rows = slice(i * 80, (i + 1) * 80)
            groupn[rows, :] = layer_norm(grouped[rows, :], gainm[...]).astype(BF16)
        for i in range(4):
            lanes = slice(i * 256, (i + 1) * 256)
            coarse[:, lanes] = dot(groupn[...], mergew[:, lanes]).astype(BF16)
        x = dot(coarse_window_p[...], coarse[...])
        kind = h + jnp.where(lat == lats - 1, 2, 0)
        upper = section(x, gain2[...], triple2, out2, D2, [kind]).astype(BF16)
        quads = dot(unwindow_p[...], stacked(upper))
        up[h] = quads.reshape(2, 2, SENT, D2 // 2).astype(BF16)

        @pl.when(h == 0)
        def _():
            u_lon(0).start()
            u_lat(0).start()
            u_dia(0).start()

        ur[h, 1, 1] = up[h, 0, 0]
        usums[...] += dot(sums[h, 2], upper)
        return carry

    lax.fori_loop(0, 2, coarse_half, 0)

    usum = usums[:8] + usums[8:]
    high = usum.astype(BF16).astype(F32)
    usum = jnp.concatenate([high, usum - high], 0).astype(BF16)
    l_split.wait()
    partial = fsum[0:4] + fsum[4:8]
    for ro in range(2):
        for co in range(2):
            off = 2 * ro + co
            t = dot(usum, splitw[:, off * D1 : (off + 1) * D1])
            t = t[:8] + t[8:]
            partial += t[4 * ro : 4 * ro + 4]
    part1[lat] = partial

    def ar_copy(buf, me, number, target):
        return pltpu.make_async_remote_copy(
            src_ref=buf.at[me],
            dst_ref=buf.at[me],
            send_sem=ar_send.at[number],
            recv_sem=ar_recv.at[number],
            device_id=target,
            device_id_type=MESH,
        )

    ar1 = [ar_copy(part1, lat, k, at(k, 0)) for k in range(1, lats)]
    ar2 = [ar_copy(part2, lon, lats + k, at(0, k)) for k in range(1, lons)]
    for c in ar1:
        c.start()
    u_lon(1).start()
    u_lat(1).start()
    u_dia(1).start()

    def skip(h):
        b_lat(h).wait_recv()
        b_lon(h).wait_recv()
        b_dia(h).wait_recv()
        for cq in range(4):
            x = patches(h, 2 * (cq // 2), 2 * (cq % 2))
            for off in range(4):
                rows = slice(cq * QUAD, (cq + 1) * QUAD)
                fg[h, off, rows, :] = x[off * QUAD : (off + 1) * QUAD]

    def out_copy(level, i):
        return pltpu.make_async_copy(
            decoded_v.at[level, i], decoded_h.at[level, i], out_sem.at[2 * level + i]
        )

    def split(h):
        u_lat(h).wait_recv()
        u_lon(h).wait_recv()
        u_dia(h).wait_recv()
        ub[...] = unstacked(dot(to_coarse_p[...], quad_rows(ur[h]))).astype(BF16)
        for i in range(8):
            dst = slice((i % 2) * 256, (i % 2) * 256 + 256)
            fg[h, i // 2, :, dst] += dot(ub[...], splitw[:, i * 256 : (i + 1) * 256])
        for i in range(2):
            pieces = []
            for j in range(2):
                rows = slice((2 * i + j) * QUAD, (2 * i + j + 1) * QUAD)
                pieces += [fg[h, off, rows, :] for off in range(4)]
            x = dot(rows_p[...], jnp.concatenate(pieces, 0).astype(BF16)).astype(BF16)
            for l in range(2):
                level = int(LEVELS[h][l])
                decoded_v[level, i] = x[l * 144 : (l + 1) * 144]
                out_copy(level, i).start()

    skip(0)
    l_coarse.wait()
    l_rows.wait()
    split(0)
    for c in ar1:
        c.wait_recv()
    total = part1[0]
    for k in range(1, lats):
        total += part1[k]
    part2[lon] = total
    for c in ar2:
        c.start()
    skip(1)
    split(1)

    for c in ar2:
        c.wait_recv()
    total = part2[0]
    for k in range(1, lons):
        total += part2[k]
    means[...] = total * (1.0 / scale)
    for c in (x_lat, x_lon, x_dia, f_lat, f_lon, f_dia, b_lat, b_lon, b_dia, u_lat, u_lon, u_dia):
        c(0).wait_send()
        c(1).wait_send()
    for level in range(4):
        for i in range(2):
            out_copy(level, i).wait()
    for c in ar1 + ar2:
        c.wait_send()


def hand_on(decoded_in, means_in, decoded, means, sems):
    copies = [
        pltpu.make_async_copy(decoded_in.at[level], decoded.at[level], sems.at[level])
        for level in range(4)
    ]
    for copy in copies:
        copy.start()
    means[...] = means_in[...]
    for copy in copies:
        copy.wait()


def solution(mesh):
    lats, lons = mesh.shape["lat"], mesh.shape["lon"]
    *consts, scale = tables(lats, lons)

    def shards(
        latent,
        gain_first,
        triple_first,
        output_first,
        gain_merge,
        merge_weight,
        gain_second,
        triple_second,
        output_second,
        split_weight,
    ):
        hbm = pl.BlockSpec(memory_space=pl.ANY)
        vmem = pl.BlockSpec(memory_space=pltpu.VMEM)
        bf = lambda *shape: pltpu.VMEM(shape, BF16)
        f4 = lambda *shape: pltpu.VMEM(shape, F32)
        decoded, means = pl.pallas_call(
            functools.partial(kernel, lats, lons, scale),
            name="windows",
            out_shape=(
                jax.ShapeDtypeStruct((4, 2, 144, D1), BF16),
                jax.ShapeDtypeStruct((4, D1), F32),
            ),
            in_specs=[hbm] * 15 + [vmem] * 3,
            out_specs=(hbm, vmem),
            scratch_shapes=[
                bf(4, 4, 72, D1),
                bf(D1, 3 * D1),
                bf(D1, D1),
                bf(4 * D1, D2),
                bf(D2, 3 * D2),
                bf(D2, D2),
                bf(D2, 4 * D1),
                bf(4 * SENT, 2 * GROUP),
                bf(2 * GROUP, 4 * SENT),
                bf(4 * SENT, 2 * GROUP),
                bf(2 * QUADS, 4 * SENT),
                bf(2 * QUADS, 4 * SENT),
                bf(GROUP, QUADS),
                bf(2, 3, 16, GROUP),
                bf(2 * GROUP, 2 * QUADS),
                bf(2, 5, 5, SENT, D1 // 2),
                bf(2, 6, 6, SENT, D1 // 2),
                bf(2 * GROUP, D2),
                bf(2 * GROUP, D2),
                bf(2 * GROUP, D2),
                bf(2 * GROUP, D2),
                bf(2 * GROUP, D2),
                f4(4, GROUP, GROUP),
                f4(QUADS, 4 * D1),
                bf(QUADS, 4 * D1),
                bf(QUADS, D2),
                bf(2, 2, 2, SENT, D2 // 2),
                bf(2, 2, 2, SENT, D2 // 2),
                bf(QUADS, D2),
                f4(2, 4, QUADS, D1),
                f4(16, D1),
                f4(16, D2),
                bf(4, 2, 144, D1),
                f4(lats, 4, D1),
                f4(lons, 4, D1),
                pltpu.SemaphoreType.DMA((15,)),
                pltpu.SemaphoreType.DMA((8,)),
                pltpu.SemaphoreType.DMA((24,)),
                pltpu.SemaphoreType.DMA((24,)),
                pltpu.SemaphoreType.DMA((lats + lons,)),
                pltpu.SemaphoreType.DMA((lats + lons,)),
            ],
            compiler_params=pltpu.CompilerParams(
                collective_id=0, has_side_effects=True, vmem_limit_bytes=60 * 1024 * 1024
            ),
        )(
            latent.reshape(4, 4, 72, D1),
            triple_first,
            output_first,
            merge_weight,
            triple_second,
            output_second,
            split_weight,
            *[jnp.asarray(c) for c in consts],
            gain_first.reshape(1, -1),
            gain_merge.reshape(1, -1),
            gain_second.reshape(1, -1),
        )
        decoded, means = pl.pallas_call(
            hand_on,
            name="hand_on",
            out_shape=(
                jax.ShapeDtypeStruct((4, 2, 144, D1), BF16),
                jax.ShapeDtypeStruct((4, D1), F32),
            ),
            in_specs=[pl.BlockSpec(memory_space=pltpu.HBM), vmem],
            out_specs=(pl.BlockSpec(memory_space=pltpu.HBM), vmem),
            scratch_shapes=[pltpu.SemaphoreType.DMA((4,))],
        )(decoded, means)
        return decoded.reshape(4, 12, 24, D1), means

    in_specs = (P(None, "lat", "lon", None),) + (P(),) * 9
    out_specs = (P(None, "lat", "lon", None), P())
    return jax.shard_map(
        shards, mesh=mesh, in_specs=in_specs, out_specs=out_specs, check_vma=False
    )
```

```python
import functools

import jax
import jax.numpy as jnp
import ml_dtypes
import numpy as np
from jax import lax
from jax.experimental import pallas as pl
from jax.experimental.pallas import tpu as pltpu
from jax.sharding import PartitionSpec as P

HD = 64
D1 = 512
D2 = 1024
EPS = 1e-05
MASKED = -1e30
CELLS = 36
SENT = 72
QUAD = 40
QUADS = 160
GROUP = 144
LEVELS = np.array([[1, 2], [3, 0]])
MESH = pl.DeviceIdType.MESH
F32 = jnp.float32
BF16 = jnp.bfloat16


def permutation(rows, columns, place, source):
    matrix = np.zeros((rows, columns), np.float32)
    matrix[place.ravel(), source.ravel()] = 1.0
    return matrix.astype(ml_dtypes.bfloat16)


def grid(*extents):
    return np.meshgrid(*map(np.arange, extents), indexing="ij")


@functools.lru_cache(None)
def tables(lats, lons):
    q, f, l, r, c = grid(4, 2, 2, 3, 6)
    token = l * 18 + r * 6 + c
    quads = q * SENT + f * CELLS + token
    to_quads = permutation(
        4 * SENT, 2 * GROUP, quads, f * GROUP + l * 72 + r * 24 + q * 6 + c
    )
    window = l * 72 + q * 18 + r * 6 + c
    to_window = permutation(2 * GROUP, 4 * SENT, f * GROUP + window, quads)
    to_coarse = permutation(2 * QUADS, 4 * SENT, f * QUADS + q * QUAD + token, quads)
    coarse_window = permutation(GROUP, QUADS, window[:, 0], (q * QUAD + token)[:, 0])
    f, ro, co, l, cr, cc = grid(2, 2, 2, 2, 3, 6)
    row, col = 2 * cr + ro, 2 * cc + co
    quad = (row // 3) * 2 + col // 6
    to_patches = permutation(
        2 * QUADS,
        4 * SENT,
        f * QUADS + (2 * ro + co) * QUAD + l * 18 + cr * 6 + cc,
        quad * SENT + f * CELLS + l * 18 + (row % 3) * 6 + col % 6,
    )
    l, row, col = grid(2, 6, 24)
    j, c12 = col // 12, col % 12
    off = (row % 2) * 2 + c12 % 2
    to_rows = permutation(
        2 * GROUP,
        2 * QUADS,
        l * 144 + row * 24 + col,
        (j * 4 + off) * QUAD + l * 18 + (row // 2) * 6 + c12 // 2,
    )
    total_rows = 12 * lats
    position = (np.arange(total_rows, dtype=np.float32) + np.float32(0.5)) / np.float32(
        total_rows
    ) - np.float32(0.5)
    weights = np.cos(np.float32(np.pi) * position).astype(np.float32)
    scale = float(np.sqrt(24.0 * lons * np.sum(weights.astype(np.float64) ** 2)))
    high = weights.astype(ml_dtypes.bfloat16)
    low = (weights - high.astype(np.float32)).astype(ml_dtypes.bfloat16)
    parts = np.stack([high, low]).astype(np.float32)
    sums = np.zeros((lats, 2, 3, 16, GROUP), np.float32)
    l, quad, r, c = [v.ravel() for v in grid(2, 4, 3, 6)]
    token = np.arange(GROUP)
    for lat in range(lats):
        for half in range(2):
            level = LEVELS[half][l]
            for part in range(2):
                for a in range(2):
                    row = (lat * 12 + 3 + 6 * a + 3 * (quad // 2) + r) % total_rows
                    sums[lat, half, a, part * 4 + level, token] = parts[part, row]
                for ro in range(2):
                    row = (2 * (lat * 6 + 3 + 3 * (quad // 2) + r) + ro) % total_rows
                    sums[lat, half, 2, part * 8 + ro * 4 + level, token] = parts[part, row]
    return (
        to_quads,
        to_window,
        np.ascontiguousarray(to_window.T),
        to_patches,
        to_coarse,
        coarse_window,
        sums.astype(ml_dtypes.bfloat16),
        to_rows,
        scale,
    )


def dot(a, b):
    return jnp.dot(a, b, preferred_element_type=F32)


def dot_nt(a, b):
    return lax.dot_general(a, b, (((1,), (1,)), ((), ())), preferred_element_type=F32)


def stacked(x):
    half = x.shape[1] // 2
    return jnp.concatenate([x[:, :half], x[:, half:]], 0)


def unstacked(x):
    half = x.shape[0] // 2
    return jnp.concatenate([x[:half], x[half:]], 1)


def quad_rows(quads):
    rows = quads.shape[0] * quads.shape[1] * quads.shape[2]
    return quads.astype(F32).reshape(rows, quads.shape[3]).astype(BF16)


def layer_norm(x, gain):
    mean = jnp.mean(x, -1, keepdims=True)
    centred = x - mean
    var = jnp.mean(centred * centred, -1, keepdims=True)
    return centred * lax.rsqrt(var + EPS) * gain


def kernel(
    lats,
    lons,
    scale,
    latent_h,
    triple1_h,
    out1_h,
    merge_h,
    triple2_h,
    out2_h,
    split_h,
    quads_h,
    window_h,
    unwindow_h,
    patches_h,
    to_coarse_h,
    coarse_window_h,
    sums_h,
    rows_h,
    gain1,
    gainm,
    gain2,
    decoded_h,
    means,
    latent,
    triple1,
    out1,
    mergew,
    triple2,
    out2,
    splitw,
    quads_p,
    window_p,
    unwindow_p,
    patches_p,
    to_coarse_p,
    coarse_window_p,
    sums,
    rows_p,
    xq,
    fq,
    normed,
    qs,
    ks,
    vs,
    att,
    bias,
    grouped,
    groupn,
    coarse,
    up,
    ur,
    ub,
    fg,
    fsum,
    usums,
    decoded_v,
    part1,
    part2,
    load_sem,
    out_sem,
    send_sem,
    recv_sem,
    ar_send,
    ar_recv,
):
    lat = lax.axis_index("lat")
    lon = lax.axis_index("lon")

    def at(dlat, dlon):
        return {
            "lat": lax.rem(lat + dlat + lats, lats),
            "lon": lax.rem(lon + dlon + lons, lons),
        }

    loads = [
        pltpu.make_async_copy(s, d, load_sem.at[i])
        for i, (s, d) in enumerate(
            [
                (latent_h, latent),
                (quads_h, quads_p),
                (window_h, window_p),
                (triple1_h, triple1),
                (unwindow_h, unwindow_p),
                (out1_h, out1),
                (sums_h.at[lat], sums),
                (patches_h, patches_p),
                (merge_h, mergew),
                (triple2_h, triple2),
                (out2_h, out2),
                (split_h, splitw),
                (to_coarse_h, to_coarse_p),
                (coarse_window_h, coarse_window_p),
                (rows_h, rows_p),
            ]
        )
    ]
    (l_latent, l_quads, l_window, l_triple1, l_unwindow, l_out1, l_sums) = loads[:7]
    (l_patches, l_merge, l_triple2, l_out2, l_split) = loads[7:12]
    (l_coarse, l_window2, l_rows) = loads[12:]
    for load in loads:
        load.start()

    barrier = pltpu.get_barrier_semaphore()
    peers = [at(k, 0) for k in range(1, lats)] + [at(0, k) for k in range(1, lons)]
    peers += [at(1, 1), at(-1, -1)]
    for peer in peers:
        pl.semaphore_signal(barrier, inc=1, device_id=peer, device_id_type=MESH)

    tq = lax.broadcasted_iota(jnp.int32, (GROUP, GROUP), 0)
    tk = lax.broadcasted_iota(jnp.int32, (GROUP, GROUP), 1)
    lev_q, lev_k = tq >= 72, tk >= 72
    half_q = jnp.where(lev_q, tq - 72, tq) >= 36
    half_k = jnp.where(lev_k, tk - 72, tk) >= 36
    other_lev = jnp.where(lev_q == lev_k, 0.0, MASKED).astype(F32)
    other_row = jnp.where(half_q == half_k, 0.0, MASKED).astype(F32)
    bias[0] = jnp.zeros((GROUP, GROUP), F32)
    bias[1] = other_lev
    bias[2] = other_row
    bias[3] = jnp.minimum(other_lev, other_row)
    fsum[...] = jnp.zeros_like(fsum)
    usums[...] = jnp.zeros_like(usums)

    def copy(number, half, src, dst, target):
        number = number + 12 * half
        return pltpu.make_async_remote_copy(
            src_ref=src,
            dst_ref=dst,
            send_sem=send_sem.at[number],
            recv_sem=recv_sem.at[number],
            device_id=target,
            device_id_type=MESH,
        )

    three, edge = pl.ds(1, 3), pl.ds(2, 3)

    def x_lat(h):
        return copy(0, h, xq.at[h, 0, three], xq.at[h, 4, three], at(-1, 0))

    def x_lon(h):
        return copy(1, h, xq.at[h, three, 0], xq.at[h, three, 4], at(0, -1))

    def x_dia(h):
        return copy(2, h, xq.at[h, 0, 0], xq.at[h, 4, 4], at(-1, -1))

    def f_lat(h):
        return copy(3, h, fq.at[h, 1, edge], fq.at[h, 5, edge], at(-1, 0))

    def f_lon(h):
        return copy(4, h, fq.at[h, edge, 1], fq.at[h, edge, 5], at(0, -1))

    def f_dia(h):
        return copy(5, h, fq.at[h, 1, 1], fq.at[h, 5, 5], at(-1, -1))

    def b_lat(h):
        return copy(6, h, fq.at[h, 4, three], fq.at[h, 0, three], at(1, 0))

    def b_lon(h):
        return copy(7, h, fq.at[h, three, 4], fq.at[h, three, 0], at(0, 1))

    def b_dia(h):
        return copy(8, h, fq.at[h, 4, 4], fq.at[h, 0, 0], at(1, 1))

    def u_lat(h):
        return copy(9, h, up.at[h, 1, 0], ur.at[h, 0, 1], at(1, 0))

    def u_lon(h):
        return copy(10, h, up.at[h, 0, 1], ur.at[h, 1, 0], at(0, 1))

    def u_dia(h):
        return copy(11, h, up.at[h, 1, 1], ur.at[h, 0, 0], at(1, 1))

    l_latent.wait()
    l_quads.wait()

    def form_quads(h):
        def form(qr, carry):
            rows = jnp.concatenate([latent[int(l), qr].astype(F32) for l in LEVELS[h]], 0)
            quads = dot(quads_p[...], stacked(rows.astype(BF16)))
            xq[h, qr, pl.ds(0, 4)] = quads.reshape(4, SENT, D1 // 2).astype(BF16)
            return carry

        lax.fori_loop(0, 4, form, 0, unroll=True)

    form_quads(0)
    pl.semaphore_wait(barrier, len(peers))
    x_lon(0).start()
    x_lat(0).start()
    x_dia(0).start()
    form_quads(1)

    l_window.wait()
    l_triple1.wait()
    l_unwindow.wait()
    l_out1.wait()
    l_sums.wait()

    lane = lax.broadcasted_iota(jnp.int32, (1, 256), 1)
    head_masks = [((lane >= HD * h) & (lane < HD * (h + 1))).astype(BF16) for h in range(4)]

    def section(x, gain, triple, out_w, width, kinds):
        count = len(kinds)
        size = count * GROUP
        normed[:size, :width] = layer_norm(x, gain).astype(BF16)
        groups = width // 256

        for which, dest in enumerate((qs, ks, vs)):

            def project(i, carry, which=which, dest=dest):
                src = pl.ds(pl.multiple_of(which * width + i * 256, 256), 256)
                dst = pl.ds(pl.multiple_of(i * 256, 256), 256)
                value = dot(normed[:size, :width], triple[:, src]).astype(BF16)
                if which == 0:
                    value = value * jnp.asarray(HD**-0.5, BF16)
                dest[:size, dst] = value
                return carry

            lax.fori_loop(0, groups, project, 0, unroll=True)

        for slot in range(count):
            for hg in range(groups):
                rows = slice(slot * GROUP, (slot + 1) * GROUP)
                lanes = slice(hg * 256, (hg + 1) * 256)
                q, k, v = qs[rows, lanes], ks[rows, lanes], vs[rows, lanes]
                away = bias[kinds[slot]]
                scores = dot_nt(jnp.concatenate([q * mask for mask in head_masks], 0), k)
                weights = []
                for h in range(4):
                    s = scores[h * GROUP : (h + 1) * GROUP] + away
                    peak = jnp.max(s, -1, keepdims=True)
                    weights.append(jnp.exp(s - peak).astype(BF16))
                weights = jnp.concatenate(weights, 0)
                values = dot(weights, v) / jnp.sum(weights.astype(F32), -1, keepdims=True)
                result = values[:GROUP]
                for h in range(1, 4):
                    own = values[h * GROUP : (h + 1) * GROUP]
                    result = jnp.where(lane >= HD * h, own, result)
                att[rows, lanes] = result.astype(BF16)
        return x + dot(att[:size, :width], out_w[...])

    def fine_step(w, carry):
        pick = lambda yes: jnp.where(yes, 1, 0)
        slots = [
            (pick(w == 2), pick(w == 3), pick(w >= 1)),
            (pick(w != 1), pick(w >= 1), pick(w == 3)),
        ]

        @pl.when(w == 1)
        def _():
            x_lon(0).wait_send()
            x_lat(0).wait_send()
            x_dia(0).wait_send()
            x_lon(1).start()
            x_lat(1).start()
            x_dia(1).start()
            x_lon(0).wait_recv()
            x_lat(0).wait_recv()

        @pl.when(w == 2)
        def _():
            x_lon(1).wait_recv()
            x_lat(1).wait_recv()

        @pl.when(w == 3)
        def _():
            x_dia(0).wait_recv()
            x_dia(1).wait_recv()

        x, kinds = [], []
        for h, a, b in slots:
            quads = xq[h, pl.ds(1 + 2 * a, 2), pl.ds(1 + 2 * b, 2)]
            x.append(unstacked(dot(window_p[...], quad_rows(quads))))
            kinds.append(h + jnp.where((a == 1) & (lat == lats - 1), 2, 0))
        fine = section(jnp.concatenate(x, 0), gain1[...], triple1, out1, D1, kinds).astype(BF16)
        for slot, (h, a, b) in enumerate(slots):
            own = fine[slot * GROUP : (slot + 1) * GROUP]
            quads = dot(unwindow_p[...], stacked(own)).reshape(2, 2, SENT, D1 // 2)
            fq[h, pl.ds(1 + 2 * a, 2), pl.ds(1 + 2 * b, 2)] = quads.astype(BF16)
            fsum[...] += dot(sums[h, a], own)

        @pl.when(w == 0)
        def _():
            f_dia(0).start()
            f_dia(1).start()

        @pl.when(w == 1)
        def _():
            f_lon(0).start()
            f_lat(0).start()

        @pl.when(w == 2)
        def _():
            f_lon(1).start()
            f_lat(1).start()

        return carry

    lax.fori_loop(0, 4, fine_step, 0)
    for h in range(2):
        b_lon(h).start()
        b_lat(h).start()
        b_dia(h).start()

    l_patches.wait()
    l_window2.wait()
    l_merge.wait()
    l_triple2.wait()
    l_out2.wait()

    def patches(h, first_r, first_c):
        x = fq[h, pl.ds(first_r, 2), pl.ds(first_c, 2)]
        return unstacked(dot(patches_p[...], quad_rows(x)))

    def coarse_half(h, carry):
        f_dia(h).wait_recv()
        f_lat(h).wait_recv()
        f_lon(h).wait_recv()
        for cq in range(4):
            x = patches(h, 2 + 2 * (cq // 2), 2 + 2 * (cq % 2))
            for off in range(4):
                rows = slice(cq * QUAD, (cq + 1) * QUAD)
                grouped[rows, off * D1 : (off + 1) * D1] = x[off * QUAD : (off + 1) * QUAD]
        for i in range(2):
            rows = slice(i * 80, (i + 1) * 80)
            groupn[rows, :] = layer_norm(grouped[rows, :], gainm[...]).astype(BF16)
        for i in range(4):
            lanes = slice(i * 256, (i + 1) * 256)
            coarse[:, lanes] = dot(groupn[...], mergew[:, lanes]).astype(BF16)
        x = dot(coarse_window_p[...], coarse[...])
        kind = h + jnp.where(lat == lats - 1, 2, 0)
        upper = section(x, gain2[...], triple2, out2, D2, [kind]).astype(BF16)
        quads = dot(unwindow_p[...], stacked(upper))
        up[h] = quads.reshape(2, 2, SENT, D2 // 2).astype(BF16)

        @pl.when(h == 0)
        def _():
            u_lon(0).start()
            u_lat(0).start()
            u_dia(0).start()

        ur[h, 1, 1] = up[h, 0, 0]
        usums[...] += dot(sums[h, 2], upper)
        return carry

    lax.fori_loop(0, 2, coarse_half, 0)

    usum = usums[:8] + usums[8:]
    high = usum.astype(BF16).astype(F32)
    usum = jnp.concatenate([high, usum - high], 0).astype(BF16)
    l_split.wait()
    partial = fsum[0:4] + fsum[4:8]
    for ro in range(2):
        for co in range(2):
            off = 2 * ro + co
            t = dot(usum, splitw[:, off * D1 : (off + 1) * D1])
            t = t[:8] + t[8:]
            partial += t[4 * ro : 4 * ro + 4]
    part1[lat] = partial

    def ar_copy(buf, me, number, target):
        return pltpu.make_async_remote_copy(
            src_ref=buf.at[me],
            dst_ref=buf.at[me],
            send_sem=ar_send.at[number],
            recv_sem=ar_recv.at[number],
            device_id=target,
            device_id_type=MESH,
        )

    ar1 = [ar_copy(part1, lat, k, at(k, 0)) for k in range(1, lats)]
    ar2 = [ar_copy(part2, lon, lats + k, at(0, k)) for k in range(1, lons)]
    for c in ar1:
        c.start()
    u_lon(1).start()
    u_lat(1).start()
    u_dia(1).start()

    def skip(h):
        b_lat(h).wait_recv()
        b_lon(h).wait_recv()
        b_dia(h).wait_recv()
        for cq in range(4):
            x = patches(h, 2 * (cq // 2), 2 * (cq % 2))
            for off in range(4):
                rows = slice(cq * QUAD, (cq + 1) * QUAD)
                fg[h, off, rows, :] = x[off * QUAD : (off + 1) * QUAD]

    def out_copy(level, i):
        return pltpu.make_async_copy(
            decoded_v.at[level, i], decoded_h.at[level, i], out_sem.at[2 * level + i]
        )

    def split(h):
        u_lat(h).wait_recv()
        u_lon(h).wait_recv()
        u_dia(h).wait_recv()
        ub[...] = unstacked(dot(to_coarse_p[...], quad_rows(ur[h]))).astype(BF16)
        for i in range(8):
            dst = slice((i % 2) * 256, (i % 2) * 256 + 256)
            fg[h, i // 2, :, dst] += dot(ub[...], splitw[:, i * 256 : (i + 1) * 256])
        for i in range(2):
            pieces = []
            for j in range(2):
                rows = slice((2 * i + j) * QUAD, (2 * i + j + 1) * QUAD)
                pieces += [fg[h, off, rows, :] for off in range(4)]
            x = dot(rows_p[...], jnp.concatenate(pieces, 0).astype(BF16)).astype(BF16)
            for l in range(2):
                level = int(LEVELS[h][l])
                decoded_v[level, i] = x[l * 144 : (l + 1) * 144]
                out_copy(level, i).start()

    skip(0)
    l_coarse.wait()
    l_rows.wait()
    split(0)
    for c in ar1:
        c.wait_recv()
    total = part1[0]
    for k in range(1, lats):
        total += part1[k]
    part2[lon] = total
    for c in ar2:
        c.start()
    skip(1)
    split(1)

    for c in ar2:
        c.wait_recv()
    total = part2[0]
    for k in range(1, lons):
        total += part2[k]
    means[...] = total * (1.0 / scale)
    for c in (x_lat, x_lon, x_dia):
        c(1).wait_send()
    for c in (f_lat, f_lon, f_dia, b_lat, b_lon, b_dia, u_lat, u_lon, u_dia):
        c(0).wait_send()
        c(1).wait_send()
    for level in range(4):
        for i in range(2):
            out_copy(level, i).wait()
    for c in ar1 + ar2:
        c.wait_send()


def solution(mesh):
    lats, lons = mesh.shape["lat"], mesh.shape["lon"]
    *consts, scale = tables(lats, lons)

    def shards(
        latent,
        gain_first,
        triple_first,
        output_first,
        gain_merge,
        merge_weight,
        gain_second,
        triple_second,
        output_second,
        split_weight,
    ):
        hbm = pl.BlockSpec(memory_space=pl.ANY)
        vmem = pl.BlockSpec(memory_space=pltpu.VMEM)
        bf = lambda *shape: pltpu.VMEM(shape, BF16)
        f4 = lambda *shape: pltpu.VMEM(shape, F32)
        decoded, means = pl.pallas_call(
            functools.partial(kernel, lats, lons, scale),
            name="windows",
            out_shape=(
                jax.ShapeDtypeStruct((4, 2, 144, D1), BF16),
                jax.ShapeDtypeStruct((4, D1), F32),
            ),
            in_specs=[hbm] * 15 + [vmem] * 3,
            out_specs=(hbm, vmem),
            scratch_shapes=[
                bf(4, 4, 72, D1),
                bf(D1, 3 * D1),
                bf(D1, D1),
                bf(4 * D1, D2),
                bf(D2, 3 * D2),
                bf(D2, D2),
                bf(D2, 4 * D1),
                bf(4 * SENT, 2 * GROUP),
                bf(2 * GROUP, 4 * SENT),
                bf(4 * SENT, 2 * GROUP),
                bf(2 * QUADS, 4 * SENT),
                bf(2 * QUADS, 4 * SENT),
                bf(GROUP, QUADS),
                bf(2, 3, 16, GROUP),
                bf(2 * GROUP, 2 * QUADS),
                bf(2, 5, 5, SENT, D1 // 2),
                bf(2, 6, 6, SENT, D1 // 2),
                bf(2 * GROUP, D2),
                bf(2 * GROUP, D2),
                bf(2 * GROUP, D2),
                bf(2 * GROUP, D2),
                bf(2 * GROUP, D2),
                f4(4, GROUP, GROUP),
                f4(QUADS, 4 * D1),
                bf(QUADS, 4 * D1),
                bf(QUADS, D2),
                bf(2, 2, 2, SENT, D2 // 2),
                bf(2, 2, 2, SENT, D2 // 2),
                bf(QUADS, D2),
                f4(2, 4, QUADS, D1),
                f4(16, D1),
                f4(16, D2),
                bf(4, 2, 144, D1),
                f4(lats, 4, D1),
                f4(lons, 4, D1),
                pltpu.SemaphoreType.DMA((15,)),
                pltpu.SemaphoreType.DMA((8,)),
                pltpu.SemaphoreType.DMA((24,)),
                pltpu.SemaphoreType.DMA((24,)),
                pltpu.SemaphoreType.DMA((lats + lons,)),
                pltpu.SemaphoreType.DMA((lats + lons,)),
            ],
            compiler_params=pltpu.CompilerParams(
                collective_id=0, has_side_effects=True, vmem_limit_bytes=60 * 1024 * 1024
            ),
        )(
            latent.reshape(4, 4, 72, D1),
            triple_first,
            output_first,
            merge_weight,
            triple_second,
            output_second,
            split_weight,
            *[jnp.asarray(c) for c in consts],
            gain_first.reshape(1, -1),
            gain_merge.reshape(1, -1),
            gain_second.reshape(1, -1),
        )
        return decoded.reshape(4, 12, 24, D1), means

    in_specs = (P(None, "lat", "lon", None),) + (P(),) * 9
    out_specs = (P(None, "lat", "lon", None), P())
    return jax.shard_map(
        shards, mesh=mesh, in_specs=in_specs, out_specs=out_specs, check_vma=False
    )
```

```python
import functools

import jax
import jax.numpy as jnp
import ml_dtypes
import numpy as np
from jax import lax
from jax.experimental import pallas as pl
from jax.experimental.pallas import tpu as pltpu
from jax.sharding import PartitionSpec as P

HD = 64
D1 = 512
D2 = 1024
EPS = 1e-05
MASKED = -1e30
CELLS = 36
SENT = 72
QUAD = 40
QUADS = 160
GROUP = 144
LEVELS = np.array([[1, 2], [3, 0]])
MESH = pl.DeviceIdType.MESH
F32 = jnp.float32
BF16 = jnp.bfloat16


def permutation(rows, columns, place, source):
    matrix = np.zeros((rows, columns), np.float32)
    matrix[place.ravel(), source.ravel()] = 1.0
    return matrix.astype(ml_dtypes.bfloat16)


def grid(*extents):
    return np.meshgrid(*map(np.arange, extents), indexing="ij")


@functools.lru_cache(None)
def tables(lats, lons):
    q, f, l, r, c = grid(4, 2, 2, 3, 6)
    token = l * 18 + r * 6 + c
    quads = q * SENT + f * CELLS + token
    to_quads = permutation(
        4 * SENT, 2 * GROUP, quads, f * GROUP + l * 72 + r * 24 + q * 6 + c
    )
    window = l * 72 + q * 18 + r * 6 + c
    to_window = permutation(2 * GROUP, 4 * SENT, f * GROUP + window, quads)
    to_coarse = permutation(2 * QUADS, 4 * SENT, f * QUADS + q * QUAD + token, quads)
    coarse_window = permutation(GROUP, QUADS, window[:, 0], (q * QUAD + token)[:, 0])
    f, ro, co, l, cr, cc = grid(2, 2, 2, 2, 3, 6)
    row, col = 2 * cr + ro, 2 * cc + co
    quad = (row // 3) * 2 + col // 6
    to_patches = permutation(
        2 * QUADS,
        4 * SENT,
        f * QUADS + (2 * ro + co) * QUAD + l * 18 + cr * 6 + cc,
        quad * SENT + f * CELLS + l * 18 + (row % 3) * 6 + col % 6,
    )
    l, row, col = grid(2, 6, 24)
    j, c12 = col // 12, col % 12
    off = (row % 2) * 2 + c12 % 2
    to_rows = permutation(
        2 * GROUP,
        2 * QUADS,
        l * 144 + row * 24 + col,
        (j * 4 + off) * QUAD + l * 18 + (row // 2) * 6 + c12 // 2,
    )
    total_rows = 12 * lats
    position = (np.arange(total_rows, dtype=np.float32) + np.float32(0.5)) / np.float32(
        total_rows
    ) - np.float32(0.5)
    weights = np.cos(np.float32(np.pi) * position).astype(np.float32)
    scale = float(np.sqrt(24.0 * lons * np.sum(weights.astype(np.float64) ** 2)))
    high = weights.astype(ml_dtypes.bfloat16)
    low = (weights - high.astype(np.float32)).astype(ml_dtypes.bfloat16)
    parts = np.stack([high, low]).astype(np.float32)
    sums = np.zeros((lats, 2, 3, 16, GROUP), np.float32)
    l, quad, r, c = [v.ravel() for v in grid(2, 4, 3, 6)]
    token = np.arange(GROUP)
    for lat in range(lats):
        for half in range(2):
            level = LEVELS[half][l]
            for part in range(2):
                for a in range(2):
                    row = (lat * 12 + 3 + 6 * a + 3 * (quad // 2) + r) % total_rows
                    sums[lat, half, a, part * 4 + level, token] = parts[part, row]
                for ro in range(2):
                    row = (2 * (lat * 6 + 3 + 3 * (quad // 2) + r) + ro) % total_rows
                    sums[lat, half, 2, part * 8 + ro * 4 + level, token] = parts[part, row]
    return (
        to_quads,
        to_window,
        np.ascontiguousarray(to_window.T),
        to_patches,
        to_coarse,
        coarse_window,
        sums.astype(ml_dtypes.bfloat16),
        to_rows,
        scale,
    )


def dot(a, b):
    return jnp.dot(a, b, preferred_element_type=F32)


def dot_nt(a, b):
    return lax.dot_general(a, b, (((1,), (1,)), ((), ())), preferred_element_type=F32)


def stacked(x):
    half = x.shape[1] // 2
    return jnp.concatenate([x[:, :half], x[:, half:]], 0)


def unstacked(x):
    half = x.shape[0] // 2
    return jnp.concatenate([x[:half], x[half:]], 1)


def quad_rows(quads):
    rows = quads.shape[0] * quads.shape[1] * quads.shape[2]
    return quads.astype(F32).reshape(rows, quads.shape[3]).astype(BF16)


def layer_norm(x, gain):
    mean = jnp.mean(x, -1, keepdims=True)
    centred = x - mean
    var = jnp.mean(centred * centred, -1, keepdims=True)
    return centred * lax.rsqrt(var + EPS) * gain


def kernel(
    lats,
    lons,
    scale,
    latent_h,
    triple1_h,
    out1_h,
    merge_h,
    triple2_h,
    out2_h,
    split_h,
    quads_h,
    window_h,
    unwindow_h,
    patches_h,
    to_coarse_h,
    coarse_window_h,
    sums_h,
    rows_h,
    gain1,
    gainm,
    gain2,
    decoded_h,
    means,
    latent,
    triple1,
    out1,
    mergew,
    triple2,
    out2,
    splitw,
    quads_p,
    window_p,
    unwindow_p,
    patches_p,
    to_coarse_p,
    coarse_window_p,
    sums,
    rows_p,
    xq,
    fq,
    normed,
    qs,
    ks,
    vs,
    att,
    bias,
    grouped,
    groupn,
    coarse,
    up,
    ur,
    ub,
    fg,
    fsum,
    usums,
    decoded_v,
    part2,
    part1,
    load_sem,
    out_sem,
    send_sem,
    recv_sem,
    ar_send,
    ar_recv,
):
    lat = lax.axis_index("lat")
    lon = lax.axis_index("lon")

    def at(dlat, dlon):
        return {
            "lat": lax.rem(lat + dlat + lats, lats),
            "lon": lax.rem(lon + dlon + lons, lons),
        }

    barrier = pltpu.get_barrier_semaphore()
    peers = [at(k, 0) for k in range(1, lats)] + [at(0, k) for k in range(1, lons)]
    peers += [at(1, 1), at(-1, -1)]
    for peer in peers:
        pl.semaphore_signal(barrier, inc=1, device_id=peer, device_id_type=MESH)

    loads = [
        pltpu.make_async_copy(s, d, load_sem.at[i])
        for i, (s, d) in enumerate(
            [
                (latent_h, latent),
                (quads_h, quads_p),
                (window_h, window_p),
                (triple1_h, triple1),
                (unwindow_h, unwindow_p),
                (out1_h, out1),
                (sums_h.at[lat], sums),
                (patches_h, patches_p),
                (merge_h, mergew),
                (triple2_h, triple2),
                (out2_h, out2),
                (split_h, splitw),
                (to_coarse_h, to_coarse_p),
                (coarse_window_h, coarse_window_p),
                (rows_h, rows_p),
            ]
        )
    ]
    (l_latent, l_quads, l_window, l_triple1, l_unwindow, l_out1, l_sums) = loads[:7]
    (l_patches, l_merge, l_triple2, l_out2, l_split) = loads[7:12]
    (l_coarse, l_window2, l_rows) = loads[12:]
    for load in loads[:7]:
        load.start()

    tq = lax.broadcasted_iota(jnp.int32, (GROUP, GROUP), 0)
    tk = lax.broadcasted_iota(jnp.int32, (GROUP, GROUP), 1)
    lev_q, lev_k = tq >= 72, tk >= 72
    half_q = jnp.where(lev_q, tq - 72, tq) >= 36
    half_k = jnp.where(lev_k, tk - 72, tk) >= 36
    other_lev = jnp.where(lev_q == lev_k, 0.0, MASKED).astype(F32)
    other_row = jnp.where(half_q == half_k, 0.0, MASKED).astype(F32)
    bias[0] = jnp.zeros((GROUP, GROUP), F32)
    bias[1] = other_lev
    bias[2] = other_row
    bias[3] = jnp.minimum(other_lev, other_row)
    fsum[...] = jnp.zeros_like(fsum)
    usums[...] = jnp.zeros_like(usums)

    def copy(number, half, src, dst, target):
        number = number + 12 * half
        return pltpu.make_async_remote_copy(
            src_ref=src,
            dst_ref=dst,
            send_sem=send_sem.at[number],
            recv_sem=recv_sem.at[number],
            device_id=target,
            device_id_type=MESH,
        )

    three, edge = pl.ds(1, 3), pl.ds(2, 3)

    def x_lat(h):
        return copy(0, h, xq.at[h, 0, three], xq.at[h, 4, three], at(-1, 0))

    def x_lon(h):
        return copy(1, h, xq.at[h, three, 0], xq.at[h, three, 4], at(0, -1))

    def x_dia(h):
        return copy(2, h, xq.at[h, 0, 0], xq.at[h, 4, 4], at(-1, -1))

    def f_lat(h):
        return copy(3, h, fq.at[h, 1, edge], fq.at[h, 5, edge], at(-1, 0))

    def f_lon(h):
        return copy(4, h, fq.at[h, edge, 1], fq.at[h, edge, 5], at(0, -1))

    def f_dia(h):
        return copy(5, h, fq.at[h, 1, 1], fq.at[h, 5, 5], at(-1, -1))

    def b_lat(h):
        return copy(6, h, fq.at[h, 4, three], fq.at[h, 0, three], at(1, 0))

    def b_lon(h):
        return copy(7, h, fq.at[h, three, 4], fq.at[h, three, 0], at(0, 1))

    def b_dia(h):
        return copy(8, h, fq.at[h, 4, 4], fq.at[h, 0, 0], at(1, 1))

    def u_lat(h):
        return copy(9, h, up.at[h, 1, 0], ur.at[h, 0, 1], at(1, 0))

    def u_lon(h):
        return copy(10, h, up.at[h, 0, 1], ur.at[h, 1, 0], at(0, 1))

    def u_dia(h):
        return copy(11, h, up.at[h, 1, 1], ur.at[h, 0, 0], at(1, 1))

    l_latent.wait()
    l_quads.wait()

    def form_quads(h):
        def form(qr, carry):
            rows = jnp.concatenate([latent[int(l), qr].astype(F32) for l in LEVELS[h]], 0)
            quads = dot(quads_p[...], stacked(rows.astype(BF16)))
            xq[h, qr, pl.ds(0, 4)] = quads.reshape(4, SENT, D1 // 2).astype(BF16)
            return carry

        lax.fori_loop(0, 4, form, 0, unroll=True)

    form_quads(0)
    for load in loads[7:]:
        load.start()
    pl.semaphore_wait(barrier, len(peers))
    x_lon(0).start()
    x_lat(0).start()
    x_dia(0).start()
    form_quads(1)

    l_window.wait()
    l_triple1.wait()
    l_unwindow.wait()
    l_out1.wait()
    l_sums.wait()

    lane = lax.broadcasted_iota(jnp.int32, (1, 256), 1)
    head_masks = [((lane >= HD * h) & (lane < HD * (h + 1))).astype(BF16) for h in range(4)]

    def section(x, gain, triple, out_w, width, kinds):
        count = len(kinds)
        size = count * GROUP
        normed[:size, :width] = layer_norm(x, gain).astype(BF16)
        groups = width // 256

        for which, dest in enumerate((qs, ks, vs)):

            def project(i, carry, which=which, dest=dest):
                src = pl.ds(pl.multiple_of(which * width + i * 256, 256), 256)
                dst = pl.ds(pl.multiple_of(i * 256, 256), 256)
                value = dot(normed[:size, :width], triple[:, src]).astype(BF16)
                if which == 0:
                    value = value * jnp.asarray(HD**-0.5, BF16)
                dest[:size, dst] = value
                return carry

            lax.fori_loop(0, groups, project, 0, unroll=True)

        for slot in range(count):
            for hg in range(groups):
                rows = slice(slot * GROUP, (slot + 1) * GROUP)
                lanes = slice(hg * 256, (hg + 1) * 256)
                q, k, v = qs[rows, lanes], ks[rows, lanes], vs[rows, lanes]
                away = bias[kinds[slot]]
                scores = dot_nt(jnp.concatenate([q * mask for mask in head_masks], 0), k)
                weights = []
                for h in range(4):
                    s = scores[h * GROUP : (h + 1) * GROUP] + away
                    peak = jnp.max(s, -1, keepdims=True)
                    weights.append(jnp.exp(s - peak).astype(BF16))
                weights = jnp.concatenate(weights, 0)
                values = dot(weights, v) / jnp.sum(weights.astype(F32), -1, keepdims=True)
                result = values[:GROUP]
                for h in range(1, 4):
                    own = values[h * GROUP : (h + 1) * GROUP]
                    result = jnp.where(lane >= HD * h, own, result)
                att[rows, lanes] = result.astype(BF16)
        return x + dot(att[:size, :width], out_w[...])

    def fine_step(w, carry):
        pick = lambda yes: jnp.where(yes, 1, 0)
        slots = [
            (pick(w == 2), pick(w == 3), pick(w >= 1)),
            (pick(w != 1), pick(w >= 1), pick(w == 3)),
        ]

        @pl.when(w == 1)
        def _():
            x_lon(0).wait_send()
            x_lat(0).wait_send()
            x_dia(0).wait_send()
            x_lon(1).start()
            x_lat(1).start()
            x_dia(1).start()
            x_lon(0).wait_recv()
            x_lat(0).wait_recv()

        @pl.when(w == 2)
        def _():
            x_lon(1).wait_recv()
            x_lat(1).wait_recv()

        @pl.when(w == 3)
        def _():
            x_dia(0).wait_recv()
            x_dia(1).wait_recv()

        x, kinds = [], []
        for h, a, b in slots:
            quads = xq[h, pl.ds(1 + 2 * a, 2), pl.ds(1 + 2 * b, 2)]
            x.append(unstacked(dot(window_p[...], quad_rows(quads))))
            kinds.append(h + jnp.where((a == 1) & (lat == lats - 1), 2, 0))
        fine = section(jnp.concatenate(x, 0), gain1[...], triple1, out1, D1, kinds).astype(BF16)
        for slot, (h, a, b) in enumerate(slots):
            own = fine[slot * GROUP : (slot + 1) * GROUP]
            quads = dot(unwindow_p[...], stacked(own)).reshape(2, 2, SENT, D1 // 2)
            fq[h, pl.ds(1 + 2 * a, 2), pl.ds(1 + 2 * b, 2)] = quads.astype(BF16)
            fsum[...] += dot(sums[h, a], own)

        @pl.when(w == 0)
        def _():
            f_dia(0).start()
            f_dia(1).start()

        @pl.when(w == 1)
        def _():
            f_lon(0).start()
            f_lat(0).start()

        @pl.when(w == 2)
        def _():
            f_lon(1).start()
            f_lat(1).start()

        return carry

    lax.fori_loop(0, 4, fine_step, 0)
    for h in range(2):
        b_lon(h).start()
        b_lat(h).start()
        b_dia(h).start()

    l_patches.wait()
    l_window2.wait()
    l_merge.wait()
    l_triple2.wait()
    l_out2.wait()

    def patches(h, first_r, first_c):
        x = fq[h, pl.ds(first_r, 2), pl.ds(first_c, 2)]
        return unstacked(dot(patches_p[...], quad_rows(x)))

    def coarse_half(h, carry):
        f_dia(h).wait_recv()
        f_lat(h).wait_recv()
        f_lon(h).wait_recv()
        for cq in range(4):
            x = patches(h, 2 + 2 * (cq // 2), 2 + 2 * (cq % 2))
            for off in range(4):
                rows = slice(cq * QUAD, (cq + 1) * QUAD)
                grouped[rows, off * D1 : (off + 1) * D1] = x[off * QUAD : (off + 1) * QUAD]
        for i in range(2):
            rows = slice(i * 80, (i + 1) * 80)
            groupn[rows, :] = layer_norm(grouped[rows, :], gainm[...]).astype(BF16)
        for i in range(4):
            lanes = slice(i * 256, (i + 1) * 256)
            coarse[:, lanes] = dot(groupn[...], mergew[:, lanes]).astype(BF16)
        x = dot(coarse_window_p[...], coarse[...])
        kind = h + jnp.where(lat == lats - 1, 2, 0)
        upper = section(x, gain2[...], triple2, out2, D2, [kind]).astype(BF16)
        quads = dot(unwindow_p[...], stacked(upper))
        up[h] = quads.reshape(2, 2, SENT, D2 // 2).astype(BF16)

        @pl.when(h == 0)
        def _():
            u_lon(0).start()
            u_lat(0).start()
            u_dia(0).start()

        ur[h, 1, 1] = up[h, 0, 0]
        usums[...] += dot(sums[h, 2], upper)
        return carry

    lax.fori_loop(0, 2, coarse_half, 0)

    usum = usums[:8] + usums[8:]
    high = usum.astype(BF16).astype(F32)
    usum = jnp.concatenate([high, usum - high], 0).astype(BF16)
    l_split.wait()
    partial = fsum[0:4] + fsum[4:8]
    for ro in range(2):
        for co in range(2):
            off = 2 * ro + co
            t = dot(usum, splitw[:, off * D1 : (off + 1) * D1])
            t = t[:8] + t[8:]
            partial += t[4 * ro : 4 * ro + 4]
    part1[lon] = partial

    def ar_copy(buf, me, number, target):
        return pltpu.make_async_remote_copy(
            src_ref=buf.at[me],
            dst_ref=buf.at[me],
            send_sem=ar_send.at[number],
            recv_sem=ar_recv.at[number],
            device_id=target,
            device_id_type=MESH,
        )

    ar2 = [ar_copy(part2, lat, k, at(k, 0)) for k in range(1, lats)]
    ar1 = [ar_copy(part1, lon, lats + k, at(0, k)) for k in range(1, lons)]
    for c in ar1:
        c.start()
    u_lon(1).start()
    u_lat(1).start()
    u_dia(1).start()

    def skip(h):
        b_lat(h).wait_recv()
        b_lon(h).wait_recv()
        b_dia(h).wait_recv()
        for cq in range(4):
            x = patches(h, 2 * (cq // 2), 2 * (cq % 2))
            for off in range(4):
                rows = slice(cq * QUAD, (cq + 1) * QUAD)
                fg[h, off, rows, :] = x[off * QUAD : (off + 1) * QUAD]

    def out_copy(level, i):
        return pltpu.make_async_copy(
            decoded_v.at[level, i], decoded_h.at[level, i], out_sem.at[2 * level + i]
        )

    def split(h):
        u_lat(h).wait_recv()
        u_lon(h).wait_recv()
        u_dia(h).wait_recv()
        ub[...] = unstacked(dot(to_coarse_p[...], quad_rows(ur[h]))).astype(BF16)
        for i in range(8):
            dst = slice((i % 2) * 256, (i % 2) * 256 + 256)
            fg[h, i // 2, :, dst] += dot(ub[...], splitw[:, i * 256 : (i + 1) * 256])
        for i in range(2):
            pieces = []
            for j in range(2):
                rows = slice((2 * i + j) * QUAD, (2 * i + j + 1) * QUAD)
                pieces += [fg[h, off, rows, :] for off in range(4)]
            x = dot(rows_p[...], jnp.concatenate(pieces, 0).astype(BF16)).astype(BF16)
            for l in range(2):
                level = int(LEVELS[h][l])
                decoded_v[level, i] = x[l * 144 : (l + 1) * 144]
                out_copy(level, i).start()

    skip(0)
    skip(1)
    l_coarse.wait()
    l_rows.wait()
    split(0)
    for c in ar1:
        c.wait_recv()
    total = part1[0]
    for k in range(1, lons):
        total += part1[k]
    part2[lat] = total
    for c in ar2:
        c.start()
    split(1)

    for c in ar2:
        c.wait_recv()
    total = part2[0]
    for k in range(1, lats):
        total += part2[k]
    means[...] = total * (1.0 / scale)
    for c in (x_lat, x_lon, x_dia):
        c(1).wait_send()
    for c in (f_lat, f_lon, f_dia, b_lat, b_lon, b_dia, u_lat, u_lon, u_dia):
        c(0).wait_send()
        c(1).wait_send()
    for level in range(4):
        for i in range(2):
            out_copy(level, i).wait()
    for c in ar2 + ar1:
        c.wait_send()


def solution(mesh):
    lats, lons = mesh.shape["lat"], mesh.shape["lon"]
    *consts, scale = tables(lats, lons)

    def shards(
        latent,
        gain_first,
        triple_first,
        output_first,
        gain_merge,
        merge_weight,
        gain_second,
        triple_second,
        output_second,
        split_weight,
    ):
        hbm = pl.BlockSpec(memory_space=pl.ANY)
        vmem = pl.BlockSpec(memory_space=pltpu.VMEM)
        bf = lambda *shape: pltpu.VMEM(shape, BF16)
        f4 = lambda *shape: pltpu.VMEM(shape, F32)
        decoded, means = pl.pallas_call(
            functools.partial(kernel, lats, lons, scale),
            name="windows",
            out_shape=(
                jax.ShapeDtypeStruct((4, 2, 144, D1), BF16),
                jax.ShapeDtypeStruct((4, D1), F32),
            ),
            in_specs=[hbm] * 15 + [vmem] * 3,
            out_specs=(hbm, vmem),
            scratch_shapes=[
                bf(4, 4, 72, D1),
                bf(D1, 3 * D1),
                bf(D1, D1),
                bf(4 * D1, D2),
                bf(D2, 3 * D2),
                bf(D2, D2),
                bf(D2, 4 * D1),
                bf(4 * SENT, 2 * GROUP),
                bf(2 * GROUP, 4 * SENT),
                bf(4 * SENT, 2 * GROUP),
                bf(2 * QUADS, 4 * SENT),
                bf(2 * QUADS, 4 * SENT),
                bf(GROUP, QUADS),
                bf(2, 3, 16, GROUP),
                bf(2 * GROUP, 2 * QUADS),
                bf(2, 5, 5, SENT, D1 // 2),
                bf(2, 6, 6, SENT, D1 // 2),
                bf(2 * GROUP, D2),
                bf(2 * GROUP, D2),
                bf(2 * GROUP, D2),
                bf(2 * GROUP, D2),
                bf(2 * GROUP, D2),
                f4(4, GROUP, GROUP),
                f4(QUADS, 4 * D1),
                bf(QUADS, 4 * D1),
                bf(QUADS, D2),
                bf(2, 2, 2, SENT, D2 // 2),
                bf(2, 2, 2, SENT, D2 // 2),
                bf(QUADS, D2),
                f4(2, 4, QUADS, D1),
                f4(16, D1),
                f4(16, D2),
                bf(4, 2, 144, D1),
                f4(lats, 4, D1),
                f4(lons, 4, D1),
                pltpu.SemaphoreType.DMA((15,)),
                pltpu.SemaphoreType.DMA((8,)),
                pltpu.SemaphoreType.DMA((24,)),
                pltpu.SemaphoreType.DMA((24,)),
                pltpu.SemaphoreType.DMA((lats + lons,)),
                pltpu.SemaphoreType.DMA((lats + lons,)),
            ],
            compiler_params=pltpu.CompilerParams(
                collective_id=0, has_side_effects=True, vmem_limit_bytes=60 * 1024 * 1024
            ),
        )(
            latent.reshape(4, 4, 72, D1),
            triple_first,
            output_first,
            merge_weight,
            triple_second,
            output_second,
            split_weight,
            *[jnp.asarray(c) for c in consts],
            gain_first.reshape(1, -1),
            gain_merge.reshape(1, -1),
            gain_second.reshape(1, -1),
        )
        return decoded.reshape(4, 12, 24, D1), means

    in_specs = (P(None, "lat", "lon", None),) + (P(),) * 9
    out_specs = (P(None, "lat", "lon", None), P())
    return jax.shard_map(
        shards, mesh=mesh, in_specs=in_specs, out_specs=out_specs, check_vma=False
    )
```

```python
import functools

import jax
import jax.numpy as jnp
import ml_dtypes
import numpy as np
from jax import lax
from jax.experimental import pallas as pl
from jax.experimental.pallas import tpu as pltpu
from jax.sharding import PartitionSpec as P

HD = 64
D1 = 512
D2 = 1024
EPS = 1e-05
MASKED = -1e30
CELLS = 36
SENT = 72
QUAD = 40
QUADS = 160
GROUP = 144
LEVELS = np.array([[1, 2], [3, 0]])
MESH = pl.DeviceIdType.MESH
F32 = jnp.float32
BF16 = jnp.bfloat16


def permutation(rows, columns, place, source):
    matrix = np.zeros((rows, columns), np.float32)
    matrix[place.ravel(), source.ravel()] = 1.0
    return matrix.astype(ml_dtypes.bfloat16)


def grid(*extents):
    return np.meshgrid(*map(np.arange, extents), indexing="ij")


@functools.lru_cache(None)
def tables(lats, lons):
    q, f, l, r, c = grid(4, 2, 2, 3, 6)
    token = l * 18 + r * 6 + c
    quads = q * SENT + f * CELLS + token
    to_quads = permutation(
        4 * SENT, 2 * GROUP, quads, f * GROUP + l * 72 + r * 24 + q * 6 + c
    )
    window = l * 72 + q * 18 + r * 6 + c
    to_window = permutation(2 * GROUP, 4 * SENT, f * GROUP + window, quads)
    to_coarse = permutation(2 * QUADS, 4 * SENT, f * QUADS + q * QUAD + token, quads)
    coarse_window = permutation(GROUP, QUADS, window[:, 0], (q * QUAD + token)[:, 0])
    f, ro, co, l, cr, cc = grid(2, 2, 2, 2, 3, 6)
    row, col = 2 * cr + ro, 2 * cc + co
    quad = (row // 3) * 2 + col // 6
    to_patches = permutation(
        2 * QUADS,
        4 * SENT,
        f * QUADS + (2 * ro + co) * QUAD + l * 18 + cr * 6 + cc,
        quad * SENT + f * CELLS + l * 18 + (row % 3) * 6 + col % 6,
    )
    l, row, col = grid(2, 6, 24)
    j, c12 = col // 12, col % 12
    off = (row % 2) * 2 + c12 % 2
    to_rows = permutation(
        2 * GROUP,
        2 * QUADS,
        l * 144 + row * 24 + col,
        (j * 4 + off) * QUAD + l * 18 + (row // 2) * 6 + c12 // 2,
    )
    total_rows = 12 * lats
    position = (np.arange(total_rows, dtype=np.float32) + np.float32(0.5)) / np.float32(
        total_rows
    ) - np.float32(0.5)
    weights = np.cos(np.float32(np.pi) * position).astype(np.float32)
    scale = float(np.sqrt(24.0 * lons * np.sum(weights.astype(np.float64) ** 2)))
    high = weights.astype(ml_dtypes.bfloat16)
    low = (weights - high.astype(np.float32)).astype(ml_dtypes.bfloat16)
    parts = np.stack([high, low]).astype(np.float32)
    sums = np.zeros((lats, 2, 3, 16, GROUP), np.float32)
    l, quad, r, c = [v.ravel() for v in grid(2, 4, 3, 6)]
    token = np.arange(GROUP)
    for lat in range(lats):
        for half in range(2):
            level = LEVELS[half][l]
            for part in range(2):
                for a in range(2):
                    row = (lat * 12 + 3 + 6 * a + 3 * (quad // 2) + r) % total_rows
                    sums[lat, half, a, part * 4 + level, token] = parts[part, row]
                for ro in range(2):
                    row = (2 * (lat * 6 + 3 + 3 * (quad // 2) + r) + ro) % total_rows
                    sums[lat, half, 2, part * 8 + ro * 4 + level, token] = parts[part, row]
    return (
        to_quads,
        to_window,
        np.ascontiguousarray(to_window.T),
        to_patches,
        to_coarse,
        coarse_window,
        sums.astype(ml_dtypes.bfloat16),
        to_rows,
        scale,
    )


def dot(a, b):
    return jnp.dot(a, b, preferred_element_type=F32)


def dot_nt(a, b):
    return lax.dot_general(a, b, (((1,), (1,)), ((), ())), preferred_element_type=F32)


def stacked(x):
    half = x.shape[1] // 2
    return jnp.concatenate([x[:, :half], x[:, half:]], 0)


def unstacked(x):
    half = x.shape[0] // 2
    return jnp.concatenate([x[:half], x[half:]], 1)


def quad_rows(quads):
    rows = quads.shape[0] * quads.shape[1] * quads.shape[2]
    return quads.astype(F32).reshape(rows, quads.shape[3]).astype(BF16)


def layer_norm(x, gain):
    mean = jnp.mean(x, -1, keepdims=True)
    centred = x - mean
    var = jnp.mean(centred * centred, -1, keepdims=True)
    return centred * lax.rsqrt(var + EPS) * gain


def kernel(
    lats,
    lons,
    scale,
    latent_h,
    triple1_h,
    out1_h,
    merge_h,
    triple2_h,
    out2_h,
    split_h,
    quads_h,
    window_h,
    unwindow_h,
    patches_h,
    to_coarse_h,
    coarse_window_h,
    sums_h,
    rows_h,
    gain1,
    gainm,
    gain2,
    decoded_h,
    means,
    latent,
    triple1,
    out1,
    mergew,
    triple2,
    out2,
    splitw,
    quads_p,
    window_p,
    unwindow_p,
    patches_p,
    to_coarse_p,
    coarse_window_p,
    sums,
    rows_p,
    xq,
    fq,
    normed,
    qs,
    ks,
    vs,
    att,
    bias,
    grouped,
    groupn,
    coarse,
    up,
    ur,
    ub,
    fg,
    fsum,
    usums,
    decoded_v,
    part2,
    part1,
    load_sem,
    out_sem,
    send_sem,
    recv_sem,
    ar_send,
    ar_recv,
):
    lat = lax.axis_index("lat")
    lon = lax.axis_index("lon")

    def at(dlat, dlon):
        return {
            "lat": lax.rem(lat + dlat + lats, lats),
            "lon": lax.rem(lon + dlon + lons, lons),
        }

    barrier = pltpu.get_barrier_semaphore()
    peers = [at(k, 0) for k in range(1, lats)] + [at(0, k) for k in range(1, lons)]
    peers += [at(1, 1), at(-1, -1)]
    for peer in peers:
        pl.semaphore_signal(barrier, inc=1, device_id=peer, device_id_type=MESH)

    loads = [
        pltpu.make_async_copy(s, d, load_sem.at[i])
        for i, (s, d) in enumerate(
            [
                (latent_h, latent),
                (quads_h, quads_p),
                (window_h, window_p),
                (triple1_h, triple1),
                (unwindow_h, unwindow_p),
                (out1_h, out1),
                (sums_h.at[lat], sums),
                (patches_h, patches_p),
                (merge_h, mergew),
                (triple2_h, triple2),
                (out2_h, out2),
                (split_h, splitw),
                (to_coarse_h, to_coarse_p),
                (coarse_window_h, coarse_window_p),
                (rows_h, rows_p),
            ]
        )
    ]
    (l_latent, l_quads, l_window, l_triple1, l_unwindow, l_out1, l_sums) = loads[:7]
    (l_patches, l_merge, l_triple2, l_out2, l_split) = loads[7:12]
    (l_coarse, l_window2, l_rows) = loads[12:]
    for load in loads[:7]:
        load.start()

    tq = lax.broadcasted_iota(jnp.int32, (GROUP, GROUP), 0)
    tk = lax.broadcasted_iota(jnp.int32, (GROUP, GROUP), 1)
    lev_q, lev_k = tq >= 72, tk >= 72
    half_q = jnp.where(lev_q, tq - 72, tq) >= 36
    half_k = jnp.where(lev_k, tk - 72, tk) >= 36
    other_lev = jnp.where(lev_q == lev_k, 0.0, MASKED).astype(F32)
    other_row = jnp.where(half_q == half_k, 0.0, MASKED).astype(F32)
    bias[0] = jnp.zeros((GROUP, GROUP), F32)
    bias[1] = other_lev
    bias[2] = other_row
    bias[3] = jnp.minimum(other_lev, other_row)
    fsum[...] = jnp.zeros_like(fsum)
    usums[...] = jnp.zeros_like(usums)

    def copy(number, half, src, dst, target):
        number = number + 12 * half
        return pltpu.make_async_remote_copy(
            src_ref=src,
            dst_ref=dst,
            send_sem=send_sem.at[number],
            recv_sem=recv_sem.at[number],
            device_id=target,
            device_id_type=MESH,
        )

    three, edge = pl.ds(1, 3), pl.ds(2, 3)

    def x_lat(h):
        return copy(0, h, xq.at[h, 0, three], xq.at[h, 4, three], at(-1, 0))

    def x_lon(h):
        return copy(1, h, xq.at[h, three, 0], xq.at[h, three, 4], at(0, -1))

    def x_dia(h):
        return copy(2, h, xq.at[h, 0, 0], xq.at[h, 4, 4], at(-1, -1))

    def f_lat(h):
        return copy(3, h, fq.at[h, 1, edge], fq.at[h, 5, edge], at(-1, 0))

    def f_lon(h):
        return copy(4, h, fq.at[h, edge, 1], fq.at[h, edge, 5], at(0, -1))

    def f_dia(h):
        return copy(5, h, fq.at[h, 1, 1], fq.at[h, 5, 5], at(-1, -1))

    def b_lat(h):
        return copy(6, h, fq.at[h, 4, three], fq.at[h, 0, three], at(1, 0))

    def b_lon(h):
        return copy(7, h, fq.at[h, three, 4], fq.at[h, three, 0], at(0, 1))

    def b_dia(h):
        return copy(8, h, fq.at[h, 4, 4], fq.at[h, 0, 0], at(1, 1))

    def u_lat(h):
        return copy(9, h, up.at[h, 1, 0], ur.at[h, 0, 1], at(1, 0))

    def u_lon(h):
        return copy(10, h, up.at[h, 0, 1], ur.at[h, 1, 0], at(0, 1))

    def u_dia(h):
        return copy(11, h, up.at[h, 1, 1], ur.at[h, 0, 0], at(1, 1))

    l_latent.wait()
    l_quads.wait()

    def form_quads(h):
        def form(qr, carry):
            rows = jnp.concatenate([latent[int(l), qr].astype(F32) for l in LEVELS[h]], 0)
            quads = dot(quads_p[...], stacked(rows.astype(BF16)))
            xq[h, qr, pl.ds(0, 4)] = quads.reshape(4, SENT, D1 // 2).astype(BF16)
            return carry

        lax.fori_loop(0, 4, form, 0, unroll=True)

    form_quads(0)
    for load in loads[7:]:
        load.start()
    pl.semaphore_wait(barrier, len(peers))
    x_lon(0).start()
    x_lat(0).start()
    x_dia(0).start()
    form_quads(1)

    l_window.wait()
    l_triple1.wait()
    l_unwindow.wait()
    l_out1.wait()
    l_sums.wait()

    lane = lax.broadcasted_iota(jnp.int32, (1, 256), 1)
    head_masks = [((lane >= HD * h) & (lane < HD * (h + 1))).astype(BF16) for h in range(4)]

    def section(x, gain, triple, out_w, width, kinds):
        count = len(kinds)
        size = count * GROUP
        normed[:size, :width] = layer_norm(x, gain).astype(BF16)
        groups = width // 256

        for which, dest in enumerate((qs, ks, vs)):

            def project(i, carry, which=which, dest=dest):
                src = pl.ds(pl.multiple_of(which * width + i * 256, 256), 256)
                dst = pl.ds(pl.multiple_of(i * 256, 256), 256)
                value = dot(normed[:size, :width], triple[:, src]).astype(BF16)
                if which == 0:
                    value = value * jnp.asarray(HD**-0.5, BF16)
                dest[:size, dst] = value
                return carry

            lax.fori_loop(0, groups, project, 0, unroll=True)

        for slot in range(count):
            for hg in range(groups):
                rows = slice(slot * GROUP, (slot + 1) * GROUP)
                lanes = slice(hg * 256, (hg + 1) * 256)
                q, k, v = qs[rows, lanes], ks[rows, lanes], vs[rows, lanes]
                away = bias[kinds[slot]]
                scores = dot_nt(jnp.concatenate([q * mask for mask in head_masks], 0), k)
                weights = []
                for h in range(4):
                    s = scores[h * GROUP : (h + 1) * GROUP] + away
                    peak = jnp.max(s, -1, keepdims=True)
                    weights.append(jnp.exp(s - peak).astype(BF16))
                weights = jnp.concatenate(weights, 0)
                values = dot(weights, v) / jnp.sum(weights.astype(F32), -1, keepdims=True)
                result = values[:GROUP]
                for h in range(1, 4):
                    own = values[h * GROUP : (h + 1) * GROUP]
                    result = jnp.where(lane >= HD * h, own, result)
                att[rows, lanes] = result.astype(BF16)
        return x + dot(att[:size, :width], out_w[...])

    def fine_step(w, carry):
        pick = lambda yes: jnp.where(yes, 1, 0)
        slots = [
            (pick(w == 2), pick(w == 3), pick(w >= 1)),
            (pick(w != 1), pick(w >= 1), pick(w == 3)),
        ]

        @pl.when(w == 1)
        def _():
            x_lon(0).wait_send()
            x_lat(0).wait_send()
            x_dia(0).wait_send()
            x_lon(1).start()
            x_lat(1).start()
            x_dia(1).start()
            x_lon(0).wait_recv()
            x_lat(0).wait_recv()

        @pl.when(w == 2)
        def _():
            x_lon(1).wait_recv()
            x_lat(1).wait_recv()

        @pl.when(w == 3)
        def _():
            x_dia(0).wait_recv()
            x_dia(1).wait_recv()

        x, kinds = [], []
        for h, a, b in slots:
            quads = xq[h, pl.ds(1 + 2 * a, 2), pl.ds(1 + 2 * b, 2)]
            x.append(unstacked(dot(window_p[...], quad_rows(quads))))
            kinds.append(h + jnp.where((a == 1) & (lat == lats - 1), 2, 0))
        fine = section(jnp.concatenate(x, 0), gain1[...], triple1, out1, D1, kinds).astype(BF16)
        for slot, (h, a, b) in enumerate(slots):
            own = fine[slot * GROUP : (slot + 1) * GROUP]
            quads = dot(unwindow_p[...], stacked(own)).reshape(2, 2, SENT, D1 // 2)
            fq[h, pl.ds(1 + 2 * a, 2), pl.ds(1 + 2 * b, 2)] = quads.astype(BF16)
            fsum[...] += dot(sums[h, a], own)

        @pl.when(w == 0)
        def _():
            f_dia(0).start()
            f_dia(1).start()

        @pl.when(w == 1)
        def _():
            f_lon(0).start()
            f_lat(0).start()

        @pl.when(w == 2)
        def _():
            f_lon(1).start()
            f_lat(1).start()

        return carry

    lax.fori_loop(0, 4, fine_step, 0)
    for h in range(2):
        b_lon(h).start()
        b_lat(h).start()
        b_dia(h).start()

    l_patches.wait()
    l_window2.wait()
    l_merge.wait()
    l_triple2.wait()
    l_out2.wait()

    def patches(h, first_r, first_c):
        x = fq[h, pl.ds(first_r, 2), pl.ds(first_c, 2)]
        return unstacked(dot(patches_p[...], quad_rows(x)))

    def coarse_half(h, carry):
        f_dia(h).wait_recv()
        f_lat(h).wait_recv()
        f_lon(h).wait_recv()
        for cq in range(4):
            x = patches(h, 2 + 2 * (cq // 2), 2 + 2 * (cq % 2))
            for off in range(4):
                rows = slice(cq * QUAD, (cq + 1) * QUAD)
                grouped[rows, off * D1 : (off + 1) * D1] = x[off * QUAD : (off + 1) * QUAD]
        for i in range(2):
            rows = slice(i * 80, (i + 1) * 80)
            groupn[rows, :] = layer_norm(grouped[rows, :], gainm[...]).astype(BF16)
        for i in range(4):
            lanes = slice(i * 256, (i + 1) * 256)
            coarse[:, lanes] = dot(groupn[...], mergew[:, lanes]).astype(BF16)
        x = dot(coarse_window_p[...], coarse[...])
        kind = h + jnp.where(lat == lats - 1, 2, 0)
        upper = section(x, gain2[...], triple2, out2, D2, [kind]).astype(BF16)
        quads = dot(unwindow_p[...], stacked(upper))
        up[h] = quads.reshape(2, 2, SENT, D2 // 2).astype(BF16)

        @pl.when(h == 0)
        def _():
            u_lon(0).start()
            u_lat(0).start()
            u_dia(0).start()

        ur[h, 1, 1] = up[h, 0, 0]
        usums[...] += dot(sums[h, 2], upper)
        return carry

    lax.fori_loop(0, 2, coarse_half, 0)

    usum = usums[:8] + usums[8:]
    high = usum.astype(BF16).astype(F32)
    usum = jnp.concatenate([high, usum - high], 0).astype(BF16)
    l_split.wait()
    partial = fsum[0:4] + fsum[4:8]
    for ro in range(2):
        for co in range(2):
            off = 2 * ro + co
            t = dot(usum, splitw[:, off * D1 : (off + 1) * D1])
            t = t[:8] + t[8:]
            partial += t[4 * ro : 4 * ro + 4]
    part1[lon] = partial

    def ar_copy(buf, me, number, target):
        return pltpu.make_async_remote_copy(
            src_ref=buf.at[me],
            dst_ref=buf.at[me],
            send_sem=ar_send.at[number],
            recv_sem=ar_recv.at[number],
            device_id=target,
            device_id_type=MESH,
        )

    ar2 = [ar_copy(part2, lat, k, at(k, 0)) for k in range(1, lats)]
    ar1 = [ar_copy(part1, lon, lats + k, at(0, k)) for k in range(1, lons)]
    for c in ar1:
        c.start()
    u_lon(1).start()
    u_lat(1).start()
    u_dia(1).start()

    def skip(h):
        b_lat(h).wait_recv()
        b_lon(h).wait_recv()
        b_dia(h).wait_recv()
        for cq in range(4):
            x = patches(h, 2 * (cq // 2), 2 * (cq % 2))
            for off in range(4):
                rows = slice(cq * QUAD, (cq + 1) * QUAD)
                fg[h, off, rows, :] = x[off * QUAD : (off + 1) * QUAD]

    def out_copy(level, i):
        return pltpu.make_async_copy(
            decoded_v.at[level, i], decoded_h.at[level, i], out_sem.at[2 * level + i]
        )

    def split(h):
        u_lat(h).wait_recv()
        u_lon(h).wait_recv()
        u_dia(h).wait_recv()
        ub[...] = unstacked(dot(to_coarse_p[...], quad_rows(ur[h]))).astype(BF16)
        for i in range(8):
            dst = slice((i % 2) * 256, (i % 2) * 256 + 256)
            fg[h, i // 2, :, dst] += dot(ub[...], splitw[:, i * 256 : (i + 1) * 256])
        for i in range(2):
            pieces = []
            for j in range(2):
                rows = slice((2 * i + j) * QUAD, (2 * i + j + 1) * QUAD)
                pieces += [fg[h, off, rows, :] for off in range(4)]
            x = dot(rows_p[...], jnp.concatenate(pieces, 0).astype(BF16)).astype(BF16)
            for l in range(2):
                level = int(LEVELS[h][l])
                decoded_v[level, i] = x[l * 144 : (l + 1) * 144]
                out_copy(level, i).start()

    skip(0)
    skip(1)
    l_coarse.wait()
    l_rows.wait()
    for c in ar1:
        c.wait_recv()
    total = part1[0]
    for k in range(1, lons):
        total += part1[k]
    part2[lat] = total
    for c in ar2:
        c.start()
    split(0)
    split(1)

    for c in ar2:
        c.wait_recv()
    total = part2[0]
    for k in range(1, lats):
        total += part2[k]
    means[...] = total * (1.0 / scale)
    for c in (x_lat, x_lon, x_dia):
        c(1).wait_send()
    for c in (f_lat, f_lon, f_dia, b_lat, b_lon, b_dia, u_lat, u_lon, u_dia):
        c(0).wait_send()
        c(1).wait_send()
    for level in range(4):
        for i in range(2):
            out_copy(level, i).wait()
    for c in ar2 + ar1:
        c.wait_send()


def solution(mesh):
    lats, lons = mesh.shape["lat"], mesh.shape["lon"]
    *consts, scale = tables(lats, lons)

    def shards(
        latent,
        gain_first,
        triple_first,
        output_first,
        gain_merge,
        merge_weight,
        gain_second,
        triple_second,
        output_second,
        split_weight,
    ):
        hbm = pl.BlockSpec(memory_space=pl.ANY)
        vmem = pl.BlockSpec(memory_space=pltpu.VMEM)
        bf = lambda *shape: pltpu.VMEM(shape, BF16)
        f4 = lambda *shape: pltpu.VMEM(shape, F32)
        decoded, means = pl.pallas_call(
            functools.partial(kernel, lats, lons, scale),
            name="windows",
            out_shape=(
                jax.ShapeDtypeStruct((4, 2, 144, D1), BF16),
                jax.ShapeDtypeStruct((4, D1), F32),
            ),
            in_specs=[hbm] * 15 + [vmem] * 3,
            out_specs=(hbm, vmem),
            scratch_shapes=[
                bf(4, 4, 72, D1),
                bf(D1, 3 * D1),
                bf(D1, D1),
                bf(4 * D1, D2),
                bf(D2, 3 * D2),
                bf(D2, D2),
                bf(D2, 4 * D1),
                bf(4 * SENT, 2 * GROUP),
                bf(2 * GROUP, 4 * SENT),
                bf(4 * SENT, 2 * GROUP),
                bf(2 * QUADS, 4 * SENT),
                bf(2 * QUADS, 4 * SENT),
                bf(GROUP, QUADS),
                bf(2, 3, 16, GROUP),
                bf(2 * GROUP, 2 * QUADS),
                bf(2, 5, 5, SENT, D1 // 2),
                bf(2, 6, 6, SENT, D1 // 2),
                bf(2 * GROUP, D2),
                bf(2 * GROUP, D2),
                bf(2 * GROUP, D2),
                bf(2 * GROUP, D2),
                bf(2 * GROUP, D2),
                f4(4, GROUP, GROUP),
                f4(QUADS, 4 * D1),
                bf(QUADS, 4 * D1),
                bf(QUADS, D2),
                bf(2, 2, 2, SENT, D2 // 2),
                bf(2, 2, 2, SENT, D2 // 2),
                bf(QUADS, D2),
                f4(2, 4, QUADS, D1),
                f4(16, D1),
                f4(16, D2),
                bf(4, 2, 144, D1),
                f4(lats, 4, D1),
                f4(lons, 4, D1),
                pltpu.SemaphoreType.DMA((15,)),
                pltpu.SemaphoreType.DMA((8,)),
                pltpu.SemaphoreType.DMA((24,)),
                pltpu.SemaphoreType.DMA((24,)),
                pltpu.SemaphoreType.DMA((lats + lons,)),
                pltpu.SemaphoreType.DMA((lats + lons,)),
            ],
            compiler_params=pltpu.CompilerParams(
                collective_id=0, has_side_effects=True, vmem_limit_bytes=60 * 1024 * 1024
            ),
        )(
            latent.reshape(4, 4, 72, D1),
            triple_first,
            output_first,
            merge_weight,
            triple_second,
            output_second,
            split_weight,
            *[jnp.asarray(c) for c in consts],
            gain_first.reshape(1, -1),
            gain_merge.reshape(1, -1),
            gain_second.reshape(1, -1),
        )
        return decoded.reshape(4, 12, 24, D1), means

    in_specs = (P(None, "lat", "lon", None),) + (P(),) * 9
    out_specs = (P(None, "lat", "lon", None), P())
    return jax.shard_map(
        shards, mesh=mesh, in_specs=in_specs, out_specs=out_specs, check_vma=False
    )
```

```python
import functools

import jax
import jax.numpy as jnp
import ml_dtypes
import numpy as np
from jax import lax
from jax.experimental import pallas as pl
from jax.experimental.pallas import tpu as pltpu
from jax.sharding import PartitionSpec as P

HD = 64
D1 = 512
D2 = 1024
EPS = 1e-05
MASKED = -1e30
CELLS = 36
SENT = 72
QUAD = 40
QUADS = 160
GROUP = 144
LEVELS = np.array([[1, 2], [3, 0]])
MESH = pl.DeviceIdType.MESH
F32 = jnp.float32
BF16 = jnp.bfloat16


def permutation(rows, columns, place, source):
    matrix = np.zeros((rows, columns), np.float32)
    matrix[place.ravel(), source.ravel()] = 1.0
    return matrix.astype(ml_dtypes.bfloat16)


def grid(*extents):
    return np.meshgrid(*map(np.arange, extents), indexing="ij")


@functools.lru_cache(None)
def tables(lats, lons):
    q, f, l, r, c = grid(4, 2, 2, 3, 6)
    token = l * 18 + r * 6 + c
    quads = q * SENT + f * CELLS + token
    to_quads = permutation(
        4 * SENT, 2 * GROUP, quads, f * GROUP + l * 72 + r * 24 + q * 6 + c
    )
    window = l * 72 + q * 18 + r * 6 + c
    to_window = permutation(2 * GROUP, 4 * SENT, f * GROUP + window, quads)
    to_coarse = permutation(2 * QUADS, 4 * SENT, f * QUADS + q * QUAD + token, quads)
    coarse_window = permutation(GROUP, QUADS, window[:, 0], (q * QUAD + token)[:, 0])
    f, ro, co, l, cr, cc = grid(2, 2, 2, 2, 3, 6)
    row, col = 2 * cr + ro, 2 * cc + co
    quad = (row // 3) * 2 + col // 6
    to_patches = permutation(
        2 * QUADS,
        4 * SENT,
        f * QUADS + (2 * ro + co) * QUAD + l * 18 + cr * 6 + cc,
        quad * SENT + f * CELLS + l * 18 + (row % 3) * 6 + col % 6,
    )
    l, row, col = grid(2, 6, 24)
    j, c12 = col // 12, col % 12
    off = (row % 2) * 2 + c12 % 2
    to_rows = permutation(
        2 * GROUP,
        2 * QUADS,
        l * 144 + row * 24 + col,
        (j * 4 + off) * QUAD + l * 18 + (row // 2) * 6 + c12 // 2,
    )
    total_rows = 12 * lats
    position = (np.arange(total_rows, dtype=np.float32) + np.float32(0.5)) / np.float32(
        total_rows
    ) - np.float32(0.5)
    weights = np.cos(np.float32(np.pi) * position).astype(np.float32)
    scale = float(np.sqrt(24.0 * lons * np.sum(weights.astype(np.float64) ** 2)))
    high = weights.astype(ml_dtypes.bfloat16)
    low = (weights - high.astype(np.float32)).astype(ml_dtypes.bfloat16)
    parts = np.stack([high, low]).astype(np.float32)
    sums = np.zeros((lats, 2, 3, 16, GROUP), np.float32)
    l, quad, r, c = [v.ravel() for v in grid(2, 4, 3, 6)]
    token = np.arange(GROUP)
    for lat in range(lats):
        for half in range(2):
            level = LEVELS[half][l]
            for part in range(2):
                for a in range(2):
                    row = (lat * 12 + 3 + 6 * a + 3 * (quad // 2) + r) % total_rows
                    sums[lat, half, a, part * 4 + level, token] = parts[part, row]
                for ro in range(2):
                    row = (2 * (lat * 6 + 3 + 3 * (quad // 2) + r) + ro) % total_rows
                    sums[lat, half, 2, part * 8 + ro * 4 + level, token] = parts[part, row]
    return (
        to_quads,
        to_window,
        np.ascontiguousarray(to_window.T),
        to_patches,
        to_coarse,
        coarse_window,
        sums.astype(ml_dtypes.bfloat16),
        to_rows,
        scale,
    )


def dot(a, b):
    return jnp.dot(a, b, preferred_element_type=F32)


def dot_nt(a, b):
    return lax.dot_general(a, b, (((1,), (1,)), ((), ())), preferred_element_type=F32)


def stacked(x):
    half = x.shape[1] // 2
    return jnp.concatenate([x[:, :half], x[:, half:]], 0)


def unstacked(x):
    half = x.shape[0] // 2
    return jnp.concatenate([x[:half], x[half:]], 1)


def quad_rows(quads):
    rows = quads.shape[0] * quads.shape[1] * quads.shape[2]
    return quads.astype(F32).reshape(rows, quads.shape[3]).astype(BF16)


def layer_norm(x, gain):
    mean = jnp.mean(x, -1, keepdims=True)
    centred = x - mean
    var = jnp.mean(centred * centred, -1, keepdims=True)
    return centred * lax.rsqrt(var + EPS) * gain


def kernel(
    lats,
    lons,
    scale,
    latent_h,
    triple1_h,
    out1_h,
    merge_h,
    triple2_h,
    out2_h,
    split_h,
    quads_h,
    window_h,
    unwindow_h,
    patches_h,
    to_coarse_h,
    coarse_window_h,
    sums_h,
    rows_h,
    gain1,
    gainm,
    gain2,
    decoded_h,
    means,
    latent,
    triple1,
    out1,
    mergew,
    triple2,
    out2,
    splitw,
    quads_p,
    window_p,
    unwindow_p,
    patches_p,
    to_coarse_p,
    coarse_window_p,
    sums,
    rows_p,
    xq,
    fq,
    normed,
    qs,
    ks,
    vs,
    att,
    bias,
    grouped,
    groupn,
    coarse,
    up,
    ur,
    ub,
    fg,
    fsum,
    usums,
    decoded_v,
    part2,
    part1,
    load_sem,
    out_sem,
    send_sem,
    recv_sem,
    ar_send,
    ar_recv,
):
    lat = lax.axis_index("lat")
    lon = lax.axis_index("lon")

    def at(dlat, dlon):
        return {
            "lat": lax.rem(lat + dlat + lats, lats),
            "lon": lax.rem(lon + dlon + lons, lons),
        }

    barrier = pltpu.get_barrier_semaphore()
    peers = [at(k, 0) for k in range(1, lats)] + [at(0, k) for k in range(1, lons)]
    peers += [at(1, 1), at(-1, -1)]
    for peer in peers:
        pl.semaphore_signal(barrier, inc=1, device_id=peer, device_id_type=MESH)

    loads = [
        pltpu.make_async_copy(s, d, load_sem.at[i])
        for i, (s, d) in enumerate(
            [
                (latent_h, latent),
                (quads_h, quads_p),
                (window_h, window_p),
                (triple1_h, triple1),
                (unwindow_h, unwindow_p),
                (out1_h, out1),
                (sums_h.at[lat], sums),
                (patches_h, patches_p),
                (merge_h, mergew),
                (triple2_h, triple2),
                (out2_h, out2),
                (split_h, splitw),
                (to_coarse_h, to_coarse_p),
                (coarse_window_h, coarse_window_p),
                (rows_h, rows_p),
            ]
        )
    ]
    (l_latent, l_quads, l_window, l_triple1, l_unwindow, l_out1, l_sums) = loads[:7]
    (l_patches, l_merge, l_triple2, l_out2, l_split) = loads[7:12]
    (l_coarse, l_window2, l_rows) = loads[12:]
    for load in loads[:7]:
        load.start()

    tq = lax.broadcasted_iota(jnp.int32, (GROUP, GROUP), 0)
    tk = lax.broadcasted_iota(jnp.int32, (GROUP, GROUP), 1)
    lev_q, lev_k = tq >= 72, tk >= 72
    half_q = jnp.where(lev_q, tq - 72, tq) >= 36
    half_k = jnp.where(lev_k, tk - 72, tk) >= 36
    other_lev = jnp.where(lev_q == lev_k, 0.0, MASKED).astype(F32)
    other_row = jnp.where(half_q == half_k, 0.0, MASKED).astype(F32)
    bias[0] = jnp.zeros((GROUP, GROUP), F32)
    bias[1] = other_lev
    bias[2] = other_row
    bias[3] = jnp.minimum(other_lev, other_row)
    fsum[...] = jnp.zeros_like(fsum)
    usums[...] = jnp.zeros_like(usums)

    def copy(number, half, src, dst, target):
        number = number + 12 * half
        return pltpu.make_async_remote_copy(
            src_ref=src,
            dst_ref=dst,
            send_sem=send_sem.at[number],
            recv_sem=recv_sem.at[number],
            device_id=target,
            device_id_type=MESH,
        )

    three, edge = pl.ds(1, 3), pl.ds(2, 3)

    def x_lat(h):
        return copy(0, h, xq.at[h, 0, three], xq.at[h, 4, three], at(-1, 0))

    def x_lon(h):
        return copy(1, h, xq.at[h, three, 0], xq.at[h, three, 4], at(0, -1))

    def x_dia(h):
        return copy(2, h, xq.at[h, 0, 0], xq.at[h, 4, 4], at(-1, -1))

    def f_lat(h):
        return copy(3, h, fq.at[h, 1, edge], fq.at[h, 5, edge], at(-1, 0))

    def f_lon(h):
        return copy(4, h, fq.at[h, edge, 1], fq.at[h, edge, 5], at(0, -1))

    def f_dia(h):
        return copy(5, h, fq.at[h, 1, 1], fq.at[h, 5, 5], at(-1, -1))

    def b_lat(h):
        return copy(6, h, fq.at[h, 4, three], fq.at[h, 0, three], at(1, 0))

    def b_lon(h):
        return copy(7, h, fq.at[h, three, 4], fq.at[h, three, 0], at(0, 1))

    def b_dia(h):
        return copy(8, h, fq.at[h, 4, 4], fq.at[h, 0, 0], at(1, 1))

    def u_lat(h):
        return copy(9, h, up.at[h, 1, 0], ur.at[h, 0, 1], at(1, 0))

    def u_lon(h):
        return copy(10, h, up.at[h, 0, 1], ur.at[h, 1, 0], at(0, 1))

    def u_dia(h):
        return copy(11, h, up.at[h, 1, 1], ur.at[h, 0, 0], at(1, 1))

    l_latent.wait()
    l_quads.wait()

    def form_quads(h):
        def form(qr, carry):
            rows = jnp.concatenate([latent[int(l), qr].astype(F32) for l in LEVELS[h]], 0)
            quads = dot(quads_p[...], stacked(rows.astype(BF16)))
            xq[h, qr, pl.ds(0, 4)] = quads.reshape(4, SENT, D1 // 2).astype(BF16)
            return carry

        lax.fori_loop(0, 4, form, 0, unroll=True)

    form_quads(0)
    for load in loads[7:]:
        load.start()
    pl.semaphore_wait(barrier, len(peers))
    x_lon(0).start()
    x_lat(0).start()
    x_dia(0).start()
    form_quads(1)

    l_window.wait()
    l_triple1.wait()
    l_unwindow.wait()
    l_out1.wait()
    l_sums.wait()

    lane = lax.broadcasted_iota(jnp.int32, (1, 256), 1)
    head_masks = [((lane >= HD * h) & (lane < HD * (h + 1))).astype(BF16) for h in range(4)]

    def section(x, gain, triple, out_w, width, kinds):
        count = len(kinds)
        size = count * GROUP
        normed[:size, :width] = layer_norm(x, gain).astype(BF16)
        groups = width // 256

        for which, dest in enumerate((qs, ks, vs)):

            def project(i, carry, which=which, dest=dest):
                src = pl.ds(pl.multiple_of(which * width + i * 256, 256), 256)
                dst = pl.ds(pl.multiple_of(i * 256, 256), 256)
                value = dot(normed[:size, :width], triple[:, src]).astype(BF16)
                if which == 0:
                    value = value * jnp.asarray(HD**-0.5, BF16)
                dest[:size, dst] = value
                return carry

            lax.fori_loop(0, groups, project, 0, unroll=True)

        for slot in range(count):
            for hg in range(groups):
                rows = slice(slot * GROUP, (slot + 1) * GROUP)
                lanes = slice(hg * 256, (hg + 1) * 256)
                q, k, v = qs[rows, lanes], ks[rows, lanes], vs[rows, lanes]
                away = bias[kinds[slot]]
                scores = dot_nt(jnp.concatenate([q * mask for mask in head_masks], 0), k)
                weights = []
                for h in range(4):
                    s = scores[h * GROUP : (h + 1) * GROUP] + away
                    peak = jnp.max(s, -1, keepdims=True)
                    weights.append(jnp.exp(s - peak).astype(BF16))
                weights = jnp.concatenate(weights, 0)
                values = dot(weights, v) / jnp.sum(weights.astype(F32), -1, keepdims=True)
                result = values[:GROUP]
                for h in range(1, 4):
                    own = values[h * GROUP : (h + 1) * GROUP]
                    result = jnp.where(lane >= HD * h, own, result)
                att[rows, lanes] = result.astype(BF16)
        return x + dot(att[:size, :width], out_w[...])

    def fine_step(w, carry):
        pick = lambda yes: jnp.where(yes, 1, 0)
        slots = [
            (pick(w == 2), pick(w == 3), pick(w >= 1)),
            (pick(w != 1), pick(w >= 1), pick(w == 3)),
        ]

        @pl.when(w == 1)
        def _():
            x_lon(0).wait_send()
            x_lat(0).wait_send()
            x_dia(0).wait_send()
            x_lon(1).start()
            x_lat(1).start()
            x_dia(1).start()
            x_lon(0).wait_recv()
            x_lat(0).wait_recv()

        @pl.when(w == 2)
        def _():
            x_lon(1).wait_recv()
            x_lat(1).wait_recv()

        @pl.when(w == 3)
        def _():
            x_dia(0).wait_recv()
            x_dia(1).wait_recv()

        x, kinds = [], []
        for h, a, b in slots:
            quads = xq[h, pl.ds(1 + 2 * a, 2), pl.ds(1 + 2 * b, 2)]
            x.append(unstacked(dot(window_p[...], quad_rows(quads))))
            kinds.append(h + jnp.where((a == 1) & (lat == lats - 1), 2, 0))
        fine = section(jnp.concatenate(x, 0), gain1[...], triple1, out1, D1, kinds).astype(BF16)
        for slot, (h, a, b) in enumerate(slots):
            own = fine[slot * GROUP : (slot + 1) * GROUP]
            quads = dot(unwindow_p[...], stacked(own)).reshape(2, 2, SENT, D1 // 2)
            fq[h, pl.ds(1 + 2 * a, 2), pl.ds(1 + 2 * b, 2)] = quads.astype(BF16)
            fsum[...] += dot(sums[h, a], own)

        @pl.when(w == 0)
        def _():
            f_dia(0).start()
            f_dia(1).start()

        @pl.when(w == 1)
        def _():
            f_lon(0).start()
            f_lat(0).start()

        @pl.when(w == 2)
        def _():
            f_lon(1).start()
            f_lat(1).start()

        return carry

    lax.fori_loop(0, 4, fine_step, 0)
    for h in range(2):
        b_lon(h).start()
        b_lat(h).start()
        b_dia(h).start()

    l_patches.wait()
    l_window2.wait()
    l_merge.wait()
    l_triple2.wait()
    l_out2.wait()

    def patches(h, first_r, first_c):
        x = fq[h, pl.ds(first_r, 2), pl.ds(first_c, 2)]
        return unstacked(dot(patches_p[...], quad_rows(x)))

    def ar_copy(buf, me, number, target):
        return pltpu.make_async_remote_copy(
            src_ref=buf.at[me],
            dst_ref=buf.at[me],
            send_sem=ar_send.at[number],
            recv_sem=ar_recv.at[number],
            device_id=target,
            device_id_type=MESH,
        )

    ar2 = [ar_copy(part2, lat, k, at(k, 0)) for k in range(1, lats)]
    ar1 = [ar_copy(part1, lon, lats + k, at(0, k)) for k in range(1, lons)]
    def coarse_half(h, carry):
        f_dia(h).wait_recv()
        f_lat(h).wait_recv()
        f_lon(h).wait_recv()
        for cq in range(4):
            x = patches(h, 2 + 2 * (cq // 2), 2 + 2 * (cq % 2))
            for off in range(4):
                rows = slice(cq * QUAD, (cq + 1) * QUAD)
                grouped[rows, off * D1 : (off + 1) * D1] = x[off * QUAD : (off + 1) * QUAD]
        for i in range(2):
            rows = slice(i * 80, (i + 1) * 80)
            groupn[rows, :] = layer_norm(grouped[rows, :], gainm[...]).astype(BF16)
        for i in range(4):
            lanes = slice(i * 256, (i + 1) * 256)
            coarse[:, lanes] = dot(groupn[...], mergew[:, lanes]).astype(BF16)
        x = dot(coarse_window_p[...], coarse[...])
        kind = h + jnp.where(lat == lats - 1, 2, 0)
        upper = section(x, gain2[...], triple2, out2, D2, [kind]).astype(BF16)
        usums[...] += dot(sums[h, 2], upper)

        @pl.when(h == 1)
        def _():
            usum = usums[:8] + usums[8:]
            high = usum.astype(BF16).astype(F32)
            usum = jnp.concatenate([high, usum - high], 0).astype(BF16)
            l_split.wait()
            partial = fsum[0:4] + fsum[4:8]
            for ro in range(2):
                for co in range(2):
                    off = 2 * ro + co
                    t = dot(usum, splitw[:, off * D1 : (off + 1) * D1])
                    t = t[:8] + t[8:]
                    partial += t[4 * ro : 4 * ro + 4]
            part1[lon] = partial
            for c in ar1:
                c.start()

        quads = dot(unwindow_p[...], stacked(upper))
        up[h] = quads.reshape(2, 2, SENT, D2 // 2).astype(BF16)
        u_lon(h).start()
        u_lat(h).start()
        u_dia(h).start()
        ur[h, 1, 1] = up[h, 0, 0]
        return carry

    lax.fori_loop(0, 2, coarse_half, 0)

    def skip(h):
        b_lat(h).wait_recv()
        b_lon(h).wait_recv()
        b_dia(h).wait_recv()
        for cq in range(4):
            x = patches(h, 2 * (cq // 2), 2 * (cq % 2))
            for off in range(4):
                rows = slice(cq * QUAD, (cq + 1) * QUAD)
                fg[h, off, rows, :] = x[off * QUAD : (off + 1) * QUAD]

    def out_copy(level, i):
        return pltpu.make_async_copy(
            decoded_v.at[level, i], decoded_h.at[level, i], out_sem.at[2 * level + i]
        )

    def split(h):
        u_lat(h).wait_recv()
        u_lon(h).wait_recv()
        u_dia(h).wait_recv()
        ub[...] = unstacked(dot(to_coarse_p[...], quad_rows(ur[h]))).astype(BF16)
        for i in range(8):
            dst = slice((i % 2) * 256, (i % 2) * 256 + 256)
            fg[h, i // 2, :, dst] += dot(ub[...], splitw[:, i * 256 : (i + 1) * 256])
        for i in range(2):
            pieces = []
            for j in range(2):
                rows = slice((2 * i + j) * QUAD, (2 * i + j + 1) * QUAD)
                pieces += [fg[h, off, rows, :] for off in range(4)]
            x = dot(rows_p[...], jnp.concatenate(pieces, 0).astype(BF16)).astype(BF16)
            for l in range(2):
                level = int(LEVELS[h][l])
                decoded_v[level, i] = x[l * 144 : (l + 1) * 144]
                out_copy(level, i).start()

    skip(0)
    skip(1)
    l_coarse.wait()
    l_rows.wait()
    for c in ar1:
        c.wait_recv()
    total = part1[0]
    for k in range(1, lons):
        total += part1[k]
    part2[lat] = total
    for c in ar2:
        c.start()
    split(0)
    split(1)

    for c in ar2:
        c.wait_recv()
    total = part2[0]
    for k in range(1, lats):
        total += part2[k]
    means[...] = total * (1.0 / scale)
    for c in (x_lat, x_lon, x_dia):
        c(1).wait_send()
    for c in (f_lat, f_lon, f_dia, b_lat, b_lon, b_dia, u_lat, u_lon, u_dia):
        c(0).wait_send()
        c(1).wait_send()
    for level in range(4):
        for i in range(2):
            out_copy(level, i).wait()
    for c in ar2 + ar1:
        c.wait_send()


def solution(mesh):
    lats, lons = mesh.shape["lat"], mesh.shape["lon"]
    *consts, scale = tables(lats, lons)

    def shards(
        latent,
        gain_first,
        triple_first,
        output_first,
        gain_merge,
        merge_weight,
        gain_second,
        triple_second,
        output_second,
        split_weight,
    ):
        hbm = pl.BlockSpec(memory_space=pl.ANY)
        vmem = pl.BlockSpec(memory_space=pltpu.VMEM)
        bf = lambda *shape: pltpu.VMEM(shape, BF16)
        f4 = lambda *shape: pltpu.VMEM(shape, F32)
        decoded, means = pl.pallas_call(
            functools.partial(kernel, lats, lons, scale),
            name="windows",
            out_shape=(
                jax.ShapeDtypeStruct((4, 2, 144, D1), BF16),
                jax.ShapeDtypeStruct((4, D1), F32),
            ),
            in_specs=[hbm] * 15 + [vmem] * 3,
            out_specs=(hbm, vmem),
            scratch_shapes=[
                bf(4, 4, 72, D1),
                bf(D1, 3 * D1),
                bf(D1, D1),
                bf(4 * D1, D2),
                bf(D2, 3 * D2),
                bf(D2, D2),
                bf(D2, 4 * D1),
                bf(4 * SENT, 2 * GROUP),
                bf(2 * GROUP, 4 * SENT),
                bf(4 * SENT, 2 * GROUP),
                bf(2 * QUADS, 4 * SENT),
                bf(2 * QUADS, 4 * SENT),
                bf(GROUP, QUADS),
                bf(2, 3, 16, GROUP),
                bf(2 * GROUP, 2 * QUADS),
                bf(2, 5, 5, SENT, D1 // 2),
                bf(2, 6, 6, SENT, D1 // 2),
                bf(2 * GROUP, D2),
                bf(2 * GROUP, D2),
                bf(2 * GROUP, D2),
                bf(2 * GROUP, D2),
                bf(2 * GROUP, D2),
                f4(4, GROUP, GROUP),
                f4(QUADS, 4 * D1),
                bf(QUADS, 4 * D1),
                bf(QUADS, D2),
                bf(2, 2, 2, SENT, D2 // 2),
                bf(2, 2, 2, SENT, D2 // 2),
                bf(QUADS, D2),
                f4(2, 4, QUADS, D1),
                f4(16, D1),
                f4(16, D2),
                bf(4, 2, 144, D1),
                f4(lats, 4, D1),
                f4(lons, 4, D1),
                pltpu.SemaphoreType.DMA((15,)),
                pltpu.SemaphoreType.DMA((8,)),
                pltpu.SemaphoreType.DMA((24,)),
                pltpu.SemaphoreType.DMA((24,)),
                pltpu.SemaphoreType.DMA((lats + lons,)),
                pltpu.SemaphoreType.DMA((lats + lons,)),
            ],
            compiler_params=pltpu.CompilerParams(
                collective_id=0, has_side_effects=True, vmem_limit_bytes=60 * 1024 * 1024
            ),
        )(
            latent.reshape(4, 4, 72, D1),
            triple_first,
            output_first,
            merge_weight,
            triple_second,
            output_second,
            split_weight,
            *[jnp.asarray(c) for c in consts],
            gain_first.reshape(1, -1),
            gain_merge.reshape(1, -1),
            gain_second.reshape(1, -1),
        )
        return decoded.reshape(4, 12, 24, D1), means

    in_specs = (P(None, "lat", "lon", None),) + (P(),) * 9
    out_specs = (P(None, "lat", "lon", None), P())
    return jax.shard_map(
        shards, mesh=mesh, in_specs=in_specs, out_specs=out_specs, check_vma=False
    )
```
